32 devices in a mesh: grp: 8 (over y, x, core), row: 4 (over z).
Axes of the slice: x: 2, y: 2, z: 4, core: 2. Of those that a mesh axis runs over, the one named last changes fastest.
Arguments:
- inputs: bfloat16 [4096, 768], P(('grp', 'row')), may hold values from -6 to 6
- cotangent: float32 [4096, 768], P(('grp', 'row')), may hold values from -6 to 6
- pass_counts: int32 [8], P('grp'), may hold values from 0 to 2
- doc_starts: int32 [8, 4], P('grp'), may hold values from 0 to 511, as said below
- token_counts: int32 [8], P('grp'), may hold values from 1 to 512
- ln1_gain: float32 [2, 768], replicated, may hold values from 0.5 to 1.5
- ln1_bias: float32 [2, 768], replicated, may hold values from -1.25 to 1.25
- qkv_weight: bfloat16 [2, 768, 2304], replicated, may hold values from -0.21875 to 0.21875
- query_bias: float32 [2, 768], replicated, may hold values from -1.25 to 1.25
- value_bias: float32 [2, 768], replicated, may hold values from -1.25 to 1.25
- out_weight: bfloat16 [2, 768, 768], replicated, may hold values from -0.625 to 0.625
- out_bias: float32 [2, 768], replicated, may hold values from -1.25 to 1.25
- ln2_gain: float32 [2, 768], replicated, may hold values from 0.5 to 1.5
- ln2_bias: float32 [2, 768], replicated, may hold values from -1.25 to 1.25
- up_weight: bfloat16 [2, 768, 3072], replicated, may hold values from -0.21875 to 0.21875
- up_bias: float32 [2, 3072], replicated, may hold values from -1.25 to 1.25
- down_weight: bfloat16 [2, 3072, 768], replicated, may hold values from -0.109375 to 0.109375
- down_bias: float32 [2, 768], replicated, may hold values from -1.25 to 1.25
Outputs:
- hidden_out: float32 [4096, 768], P(('grp', 'row'))
- grad_inputs: float32 [4096, 768], P(('grp', 'row'))
- grad_ln1_gain: float32 [2, 768], P(None, ('grp', 'row'))
- grad_ln1_bias: float32 [2, 768], P(None, ('grp', 'row'))
- grad_qkv_weight: float32 [2, 768, 2304], P(None, ('grp', 'row'))
- grad_query_bias: float32 [2, 768], P(None, ('grp', 'row'))
- grad_value_bias: float32 [2, 768], P(None, ('grp', 'row'))
- grad_out_weight: float32 [2, 768, 768], P(None, ('grp', 'row'))
- grad_out_bias: float32 [2, 768], P(None, ('grp', 'row'))
- grad_ln2_gain: float32 [2, 768], P(None, ('grp', 'row'))
- grad_ln2_bias: float32 [2, 768], P(None, ('grp', 'row'))
- grad_up_weight: float32 [2, 768, 3072], P(None, ('grp', 'row'))
- grad_up_bias: float32 [2, 3072], P(None, ('grp', 'row'))
- grad_down_weight: float32 [2, 3072, 768], P(None, ('grp', 'row'))
- grad_down_bias: float32 [2, 768], P(None, ('grp', 'row'))
The draws below stay inside these ranges and needn't reach their ends.
Inputs may be any that keep to these rules, and one draw needn't show every extreme that they name: `doc_starts`: a group's 4 document starts rise strictly and the first is 0.
All inputs are finite; a program needn't handle non-finite values.
Results may differ from the reference program's by a relative error of at most 0.02.
Values may be sent and summed in bfloat16 or wider, within the bound.
A program may use at most 320 MiB of HBM per device.

```python
import jax
import jax.numpy as jnp
from jax import lax

HEADS = 12
HEAD = 64
D = 768
FF = 3072
TOK_DEV = 128
LAYERS = 2
MAXP = 2
GROUPS = 8
LEN = 512
TOKENS = 4096


def draw_doc_starts(key, part):
    key = jax.random.fold_in(key, 11)
    key_one, key_two, key_three = jax.random.split(key, 3)
    first = jax.random.randint(key_one, (GROUPS,), 1, TOK_DEV // 2)
    second = jax.random.randint(key_two, (GROUPS,), LEN - TOK_DEV // 2, LEN - TOK_DEV // 4)
    third = LEN - 1 - jax.random.randint(key_three, (GROUPS,), 0, TOK_DEV // 4)
    third = third.at[0].set(LEN - 1)
    zero = jnp.zeros((GROUPS,), jnp.int32)
    return jnp.stack([zero, first, second, third], axis=1).astype(jnp.int32)


def draw_token_counts(key, part):
    key = jax.random.fold_in(key, 5)
    extra = jax.random.randint(key, (GROUPS,), 0, LEN // 4)
    rising = LEN // 2 * lax.iota(jnp.int32, GROUPS) // (GROUPS - 1)
    return (LEN // 4 + rising + extra).astype(jnp.int32)


def with_ends(entries, rng, smallest, high):
    dims = entries.shape
    place = [jax.random.randint(jax.random.fold_in(rng, axis), (), 0, dims[axis]) for axis in range(len(dims))]
    entries = entries.at[tuple(place)].set(smallest)
    longest = dims.index(max(dims))
    place[longest] = (place[longest] + 1) % dims[longest]
    return entries.at[tuple(place)].set(high)


def spiked(drawn, key, source, target, parts, factor):
    owner, partner = [(jnp.arange(drawn.shape[dim]) // (drawn.shape[dim] // parts)).reshape([-1 if axis == dim else 1 for axis in range(drawn.ndim)]) for dim in (source, target)]
    chosen = jax.random.permutation(key, parts)[partner]
    strong = (owner == chosen) | (owner == (partner + parts // 2) % parts)
    return jnp.where(strong, factor * drawn, drawn)


def steps_of(key, dims, pieces, smallest, top_value):
    factor_of, own = 1.0, jax.random.fold_in(key, 6)
    for axis_at, shards_of in pieces:
        heights = jnp.exp(jax.random.uniform(jax.random.fold_in(own, axis_at), (shards_of,), jnp.float32, smallest / len(pieces), top_value / len(pieces)))
        factor_of = factor_of * jnp.repeat(heights, dims[axis_at] // shards_of).reshape([-1 if axis == axis_at else 1 for axis in range(len(dims))])
    return factor_of


def noise(own_key, shape, width, bound, cuts=(), kind=jnp.bfloat16):
    drawn = jax.random.normal(own_key, shape, jnp.float32) * width
    if len(cuts) > 0:
        drawn = steps_of(own_key, shape, cuts, -0.22, 0.18) * drawn
    return jnp.clip(drawn, min=-bound, max=bound).astype(kind)


def bell_draw_with(stream_key, dims, width, most, shards, heavy, held_as=jnp.bfloat16):
    values = width * jax.random.normal(stream_key, dims, jnp.float32)
    if shards:
        values = values * steps_of(stream_key, dims, shards, -0.22, 0.18)
    return jnp.clip(spiked(values, jax.random.fold_in(stream_key, 3), *heavy), -most, most).astype(held_as)


def setup_inputs(seed: int = 0) -> dict:
    arg_keys = jax.random.split(jax.random.key(seed), 19)
    inputs = noise(arg_keys[0], (TOKENS, D), 1.0, 6.0, ((0, 32),))
    cotangent = bell_draw_with(arg_keys[1], (TOKENS, D), 1.0, 6.0, ((0, 32),), (0, 1, 32, 2.75), jnp.float32)
    pass_counts = with_ends(jax.random.randint(arg_keys[2], (GROUPS,), 0, MAXP + 1), jax.random.fold_in(arg_keys[2], 1), 0, MAXP).astype(jnp.int32)
    doc_starts = draw_doc_starts(jax.random.fold_in(arg_keys[18], 71), 0)
    token_counts = draw_token_counts(jax.random.fold_in(arg_keys[18], 71), 0)
    ln1_gain = jnp.clip(1.0 + 0.1 * jax.random.normal(arg_keys[5], (LAYERS, D), jnp.float32), 0.5, 1.5)
    ln1_bias = noise(arg_keys[6], (LAYERS, D), 0.2, 1.25, (), jnp.float32)
    qkv_weight = noise(arg_keys[7], (LAYERS, D, 3 * D), D ** -0.5, 0.21875)
    query_bias = noise(arg_keys[8], (LAYERS, D), 0.2, 1.25, (), jnp.float32)
    value_bias = noise(arg_keys[9], (LAYERS, D), 0.2, 1.25, (), jnp.float32)
    out_weight = noise(arg_keys[10], (LAYERS, D, D), (D // 8) ** -0.5, 0.625)
    out_bias = noise(arg_keys[11], (LAYERS, D), 0.2, 1.25, (), jnp.float32)
    ln2_gain = jnp.clip(1.0 + 0.1 * jax.random.normal(arg_keys[12], (LAYERS, D), jnp.float32), 0.5, 1.5)
    ln2_bias = noise(arg_keys[13], (LAYERS, D), 0.2, 1.25, (), jnp.float32)
    up_weight = noise(arg_keys[14], (LAYERS, D, FF), D ** -0.5, 0.21875)
    up_bias = noise(arg_keys[15], (LAYERS, FF), 0.2, 1.25, (), jnp.float32)
    down_weight = noise(arg_keys[16], (LAYERS, FF, D), FF ** -0.5, 0.109375)
    down_bias = noise(arg_keys[17], (LAYERS, D), 0.2, 1.25, (), jnp.float32)
    return dict(inputs=inputs, cotangent=cotangent, pass_counts=pass_counts, doc_starts=doc_starts, token_counts=token_counts, ln1_gain=ln1_gain, ln1_bias=ln1_bias, qkv_weight=qkv_weight, query_bias=query_bias, value_bias=value_bias, out_weight=out_weight, out_bias=out_bias, ln2_gain=ln2_gain, ln2_bias=ln2_bias, up_weight=up_weight, up_bias=up_bias, down_weight=down_weight, down_bias=down_bias)


@jax.custom_vjp
def low(v):
    return lax.optimization_barrier(v.astype(jnp.bfloat16)).astype(jnp.float32)

@jax.custom_vjp
def low_back(v):
    return v

def low_keep(v):
    return (low(v), None)

def low_pass(kept, grad):
    return (grad,)

def back_keep(v):
    return (v, None)

def back_low(kept, grad):
    return (low(grad),)
low.defvjp(low_keep, low_pass)
low_back.defvjp(back_keep, back_low)
eps = 1e-05
negative = -1000000000.0
highest = lax.Precision.HIGHEST

def layer_norm(value, gain, shift):
    mean = lax.optimization_barrier(jnp.mean(value, axis=-1, keepdims=True))
    centred = value - mean
    spread = lax.optimization_barrier(jnp.mean(centred * centred, axis=-1, keepdims=True))
    return centred * lax.rsqrt(spread + eps) * gain + shift

def layer_apply(weights, hidden, allowed):
    gain_one, bias_one, qkv_w, q_bias, v_bias, out_w, out_b, gain_two, bias_two, up_w, up_b, down_w, down_b = weights
    length = hidden.shape[0]
    normed = low(layer_norm(hidden, gain_one, bias_one))
    full_bias = jnp.concatenate([q_bias, jnp.zeros_like(q_bias), v_bias])
    projected = low(low_back(jnp.dot(normed, qkv_w, precision=highest) + full_bias))
    query3 = projected[:, :D].reshape(length, HEADS, HEAD)
    keys3 = projected[:, D:2 * D].reshape(length, HEADS, HEAD)
    values3 = projected[:, 2 * D:].reshape(length, HEADS, HEAD)
    raw = low_back(jnp.einsum('qhd,khd->hqk', query3, keys3, precision=highest))
    scaled = jnp.where(allowed[None], raw * 0.125, negative)
    top = lax.optimization_barrier(jnp.max(scaled, axis=-1, keepdims=True))
    expo = jnp.exp(scaled - top)
    probs = expo / lax.optimization_barrier(jnp.sum(expo, axis=-1, keepdims=True))
    mixed = jnp.einsum('hqk,khd->qhd', low(probs), values3, precision=highest).reshape(length, D)
    attended = low(low_back(mixed))
    middle = hidden + low_back(jnp.dot(attended, out_w, precision=highest) + out_b)
    normed_two = low(layer_norm(middle, gain_two, bias_two))
    before = low_back(jnp.dot(normed_two, up_w, precision=highest) + up_b)
    activated = low(jax.nn.gelu(before, approximate=True))
    return middle + low_back(jnp.dot(activated, down_w, precision=highest) + down_b)

def stack_apply(weights, hidden, allowed):
    for layer in range(LAYERS):
        hidden = layer_apply(tuple((item[layer] for item in weights)), hidden, allowed)
    return hidden

def group_forward(weights, hidden, count, allowed):
    for section in range(MAXP):
        moved = stack_apply(weights, hidden, allowed)
        hidden = jnp.where(section < count, moved, hidden)
    return stack_apply(weights, hidden, allowed)

def reference(inputs, cotangent, pass_counts, doc_starts, token_counts, ln1_gain, ln1_bias, qkv_weight, query_bias, value_bias, out_weight, out_bias, ln2_gain, ln2_bias, up_weight, up_bias, down_weight, down_bias):
    params = tuple((item.astype(jnp.float32) for item in (ln1_gain, ln1_bias, qkv_weight, query_bias, value_bias, out_weight, out_bias, ln2_gain, ln2_bias, up_weight, up_bias, down_weight, down_bias)))
    counts_float = token_counts.astype(jnp.float32)
    total = jnp.sum(counts_float)
    hidden_in = inputs.astype(jnp.float32).reshape(GROUPS, LEN, D)
    grads_in = cotangent.astype(jnp.float32).reshape(GROUPS, LEN, D)
    positions = lax.iota(jnp.int32, LEN)

    def one_group(carry, item):
        hidden, grad_out, count, starts, weight = item
        document = lax.optimization_barrier(jnp.sum((positions[:, None] >= starts[None, :]).astype(jnp.int32), axis=1))
        allowed = (document[:, None] == document[None, :]) & (positions[None, :] <= positions[:, None])

        def forward(weights, start_hidden):
            return group_forward(weights, start_hidden, count, allowed)
        result, pull = jax.vjp(forward, params, hidden)
        grad_weights, grad_hidden = pull(grad_out)
        carry = tuple((acc + weight * part_grad for acc, part_grad in zip(carry, grad_weights)))
        return (carry, (result, weight * grad_hidden))
    zeros = tuple((jnp.zeros_like(item) for item in params))
    sums, (results, grad_hidden) = lax.scan(one_group, zeros, (hidden_in, grads_in, pass_counts, doc_starts, counts_float))
    grads = tuple((item / total for item in sums))
    hidden_out = results.reshape(TOKENS, D)
    grad_inputs = (grad_hidden / total).reshape(TOKENS, D)
    return (hidden_out, grad_inputs, grads[0], grads[1], grads[2], grads[3], grads[4], grads[5], grads[6], grads[7], grads[8], grads[9], grads[10], grads[11], grads[12])
```

```python
import functools

import jax
import jax.numpy as jnp
import numpy as np
from jax import lax
from jax.experimental import pallas as pl
from jax.experimental.pallas import tpu as pltpu
from jax.sharding import PartitionSpec as P

HEADS = 12
HEAD = 64
D = 768
FF = 3072
LAYERS = 2
MAXP = 2
STEPS = LAYERS * (MAXP + 1)

EPS = 1e-05
NEG = -1000000000.0
LOG2E = 1.4426950408889634
MESH = pl.DeviceIdType.MESH
F32 = jnp.float32
BF16 = jnp.bfloat16


def nn(a, b):
    return jnp.dot(a, b, preferred_element_type=F32)


def nt(a, b):
    return lax.dot_general(a, b, (((1,), (1,)), ((), ())), preferred_element_type=F32)


def tn(a, b):
    return lax.dot_general(a, b, (((0,), (0,)), ((), ())), preferred_element_type=F32)


def normalised(x):
    mean = jnp.mean(x, axis=-1, keepdims=True)
    centred = x - mean
    spread = jnp.mean(centred * centred, axis=-1, keepdims=True)
    inv = lax.rsqrt(spread + EPS)
    return centred * inv, inv


def norm_back(grad, gain, hat, inv):
    g = grad * gain
    mean_g = jnp.mean(g, axis=-1, keepdims=True)
    mean_gh = jnp.mean(g * hat, axis=-1, keepdims=True)
    return inv * (g - mean_g - hat * mean_gh)


def column_sum(x):
    return jnp.sum(x, axis=0, keepdims=True)


class Plan:
    def __init__(self, ngrp, nrow, tok):
        self.ngrp, self.nrow, self.tok = ngrp, nrow, tok
        self.ncol = ngrp // 2
        self.bits = max(self.ncol.bit_length() - 1, 0)
        self.ndev = ngrp * nrow
        self.ch = D // self.ndev
        self.chp = -(-self.ch // 8) * 8
        self.cf = FF // self.ndev
        self.rows = self.ncol * 2 * self.chp
        self.nsel = 2 * self.rows
        self.wide = FF // ngrp
        self.per = D // (2 * self.wide)
        self.frows = self.ncol * 2 * self.cf
        cols = list(range(self.bits))[::-1]
        self.order_up = cols[1:] + [-1] + cols[:1]
        self.order_qkv = [-1] + cols
        self.order_down = cols + [-1]

    def selector(self, order):
        table = np.zeros((2, self.nsel, D), np.float32)
        for half in range(2):
            for c in range(2):
                for piece in range(self.ncol * 2):
                    col, pair = 0, 0
                    for place, dim in enumerate(order):
                        bit = (piece >> (len(order) - 1 - place)) & 1
                        if dim < 0:
                            pair = bit
                        else:
                            col |= bit << dim
                    first = ((col * 2 + c) * 4 + 2 * half + pair) * self.ch
                    row = c * self.rows + piece * self.chp
                    for i in range(self.ch):
                        table[half, row + i, first + i] = 1
        return table

    def selector_ff(self):
        n = D // 2
        table = np.zeros((2, n, D), np.float32)
        for half in range(2):
            row = 0
            for c in range(2):
                for j in range(self.per):
                    first = (j * 2 + c) * self.wide + half * 2 * self.cf
                    for i in range(2 * self.cf):
                        table[half, row, first + i] = 1
                        row += 1
        return table


def where_am_i():
    g = lax.axis_index("grp")
    z = lax.axis_index("row")
    c = lax.rem(g, 2)
    col = lax.div(g, 2)
    outer = jnp.logical_or(z == 0, z == 3)
    parity = jnp.where(outer, 0, 1)
    return g, z, c, col, outer, parity


def main_kernel(
    plan,
    x_own, cot_own, par_ref, ln1g, ln1b, qb, vb, ob, ln2g, ln2b, ub, db, sel_h,
    wq_h, wo_h, wu_h, wd_h,
    hid_o, gin_o, vec_o, tot_o, asel_h, osel_h, usel_h, gsel_h, dp_h, dy_h, df_h, dr_h,
    sx_h, sq_h, skv_h, slse_h, sm_h, sgp_h,
    wq, wo, wu, wd, sel, xin, cot, par_in, tsend, trecv,
    bias1, bias2, X, Q, KV, LSE, M, GP, O, GF, XN, asel, osel, usel, gsel,
    R, U, DKV, RDKV, DP, DR, DY, VAC, ret_s, ret_r,
    w_sem, sel_sem, in_send, in_recv, cot_send, cot_recv, par_sem, t_sem, kv_send, kv_recv,
    st_sem, ld_sem, sel_out, dkv_send, dkv_recv, bst_sem, ret_send, ret_recv, out_sem,
):
    tok = plan.tok
    T = 2 * tok
    g, z, c, col, outer, parity = where_am_i()
    half = lax.div(z, 2)
    peer = (col * 2 + 1 - c, z)
    off_lo = pl.multiple_of(c * tok, tok)
    off_hi = pl.multiple_of((3 - c) * tok, tok)
    poff_lo = pl.multiple_of((1 - c) * tok, tok)
    poff_hi = pl.multiple_of((2 + c) * tok, tok)

    weight_copies = []
    for l in range(LAYERS):
        for i, (src, dst) in enumerate(((wq_h, wq), (wo_h, wo), (wu_h, wu), (wd_h, wd))):
            weight_copies.append(pltpu.make_async_copy(src.at[l], dst.at[l], w_sem.at[l, i]))
    weight_copies[0].start()
    sel_copies = [
        pltpu.make_async_copy(sel_h.at[i, half], sel.at[i], sel_sem.at[i]) for i in range(3)
    ]
    for cp in sel_copies:
        cp.start()

    barrier = pltpu.get_barrier_semaphore()
    count = 0
    for dc in range(2):
        for dz in range(plan.nrow):
            if dc == 0 and dz == 0:
                continue
            target = (col * 2 + lax.rem(c + dc, 2), lax.rem(z + dz, plan.nrow))
            pl.semaphore_signal(barrier, inc=1, device_id=target, device_id_type=MESH)
            count += 1
    others = [(col ^ (1 << b)) * 2 + c for b in range(plan.bits)]
    for other in others:
        pl.semaphore_signal(barrier, inc=1, device_id=(other, z), device_id_type=MESH)
        count += 1
    pl.semaphore_wait(barrier, count)

    block_core = jnp.where(outer, 0, 1)
    slot_in = lax.div(z, 2)
    send_list = []
    for i in range(2):
        zt = jnp.where(c == 0, 3 * i, 1 + i)
        is_self = jnp.logical_and(c == block_core, zt == z)
        send_list.append((i, zt, is_self))

    def deliver(src, dst, send, recv):
        for i, zt, is_self in send_list:

            @pl.when(is_self)
            def _():
                pltpu.make_async_copy(src, dst.at[slot_in], recv.at[slot_in]).start()

            @pl.when(jnp.logical_not(is_self))
            def _():
                pltpu.make_async_remote_copy(
                    src_ref=src, dst_ref=dst.at[slot_in], send_sem=send.at[i], recv_sem=recv.at[slot_in],
                    device_id=(col * 2 + block_core, zt), device_id_type=MESH,
                ).start()

    def deliver_sent(src, dst, send, recv):
        for i, zt, is_self in send_list:

            @pl.when(jnp.logical_not(is_self))
            def _():
                pltpu.make_async_remote_copy(
                    src_ref=src, dst_ref=dst.at[slot_in], send_sem=send.at[i], recv_sem=recv.at[slot_in],
                    device_id=(col * 2 + block_core, zt), device_id_type=MESH,
                ).wait_send()

    def deliver_wait(src, dst, recv):
        for i in range(2):
            pltpu.make_async_copy(src, dst.at[i], recv.at[i]).wait()

    deliver(x_own, xin, in_send, in_recv)

    par_copy = pltpu.make_async_remote_copy(
        src_ref=par_ref, dst_ref=par_in, send_sem=par_sem.at[0], recv_sem=par_sem.at[1],
        device_id=peer, device_id_type=MESH,
    )
    par_copy.start()
    for cp in weight_copies[1:]:
        cp.start()
    par_copy.wait()
    served = jnp.where(parity == c, par_ref[...], par_in[...])
    tcount = par_ref[1:2, :] + par_in[1:2, :]
    total = jnp.broadcast_to(tcount, (8, 128))
    for b in range(plan.bits):
        tsend[b] = total
        cp = pltpu.make_async_remote_copy(
            src_ref=tsend.at[b], dst_ref=trecv.at[b], send_sem=t_sem.at[0, b], recv_sem=t_sem.at[1, b],
            device_id=(others[b], z), device_id_type=MESH,
        )
        cp.start()
        cp.wait()
        total = total + trecv[b]
    factor = served[1:2, :] / total[0:1, :]
    tot_o[...] = jnp.broadcast_to(factor, (8, 128))
    passes = served[0:1, 0:1]

    lane = lax.broadcasted_iota(jnp.int32, (1, T), 1)
    qpos = jnp.where(lane < tok, c * tok + lane, (3 - c) * tok + lane - tok).astype(F32)
    begin = jnp.zeros((1, T), F32)
    for k in range(4):
        s_k = served[2 + k : 3 + k, 0:1]
        begin = jnp.maximum(begin, jnp.where(qpos >= s_k, s_k, 0.0))
    kpos = lax.broadcasted_iota(jnp.int32, (T, T), 0).astype(F32)
    bias1[...] = jnp.where((kpos <= qpos) & (kpos >= begin), 0.0, NEG)
    kpos2 = kpos[:, tok:] + float(T)
    bias2[...] = jnp.where((kpos2 <= qpos[:, tok:]) & (kpos2 >= begin[:, tok:]), 0.0, NEG)

    VAC[...] = jnp.zeros_like(VAC)
    for cp in sel_copies:
        cp.wait()

    deliver_wait(x_own, xin, in_recv)
    deliver_sent(x_own, xin, in_send, in_recv)
    XN[0:tok] = xin[0].astype(F32)
    XN[tok:T] = xin[1].astype(F32)
    deliver(cot_own, cot, cot_send, cot_recv)

    low = lax.broadcasted_iota(jnp.int32, (1, 128), 1) < HEAD

    def stash_copies(s, slot, sem, back):
        pairs = ((X, sx_h), (Q, sq_h), (LSE, slse_h), (M, sm_h), (GP, sgp_h))
        out = []
        for i, (v, h) in enumerate(pairs):
            if back:
                out.append(pltpu.make_async_copy(h.at[s], v.at[slot], sem.at[slot, i]))
            else:
                out.append(pltpu.make_async_copy(v.at[slot], h.at[s], sem.at[slot, i]))
        return out

    def kv_stash(s, slot):
        return pltpu.make_async_copy(KV.at[slot], skv_h.at[s], st_sem.at[slot, 5])

    def kv_load(s, slot):
        return pltpu.make_async_copy(skv_h.at[s], KV.at[slot], ld_sem.at[slot, 5])

    def sel_copies_out(l, sect):
        at = pl.ds(pl.multiple_of(sect * T, T), T)
        return [
            pltpu.make_async_copy(asel, asel_h.at[l, :, at], sel_out.at[0]),
            pltpu.make_async_copy(osel, osel_h.at[l, :, at], sel_out.at[1]),
            pltpu.make_async_copy(usel, usel_h.at[l, :, at], sel_out.at[2]),
            pltpu.make_async_copy(gsel, gsel_h.at[l, :, at], sel_out.at[3]),
        ]

    def kv_copies(slot):
        out = []
        for i, off in enumerate((off_lo, off_hi)):
            ref = KV.at[slot, pl.ds(off, tok), :]
            out.append(
                pltpu.make_async_remote_copy(
                    src_ref=ref, dst_ref=ref, send_sem=kv_send.at[slot, i], recv_sem=kv_recv.at[slot, i],
                    device_id=peer, device_id_type=MESH,
                )
            )
        return out

    def kv_arrivals(slot):
        out = []
        for i, off in enumerate((poff_lo, poff_hi)):
            ref = KV.at[slot, pl.ds(off, tok), :]
            out.append(
                pltpu.make_async_remote_copy(
                    src_ref=ref, dst_ref=ref, send_sem=kv_send.at[slot, i], recv_sem=kv_recv.at[slot, i],
                    device_id=peer, device_id_type=MESH,
                )
            )
        return out

    def forward(s, carry):
        l = lax.rem(s, LAYERS)
        sect = lax.div(s, LAYERS)
        slot = lax.rem(s, 2)

        @pl.when(s >= 2)
        def _():
            for cp in stash_copies(s - 2, slot, st_sem, False):
                cp.wait()

        x = XN[...]
        X[slot] = x
        hat, _ = normalised(x)
        a = (hat * ln1g[pl.ds(l, 1), :] + ln1b[pl.ds(l, 1), :]).astype(BF16)

        @pl.when(s < 2)
        def _():
            pltpu.make_async_copy(wq_h.at[l], wq.at[l], w_sem.at[l, 0]).wait()

        kk = nn(a, wq[l, :, D : 2 * D]).astype(BF16)
        vv = (nn(a, wq[l, :, 2 * D : 3 * D]) + vb[pl.ds(l, 1), :]).astype(BF16)
        KV[slot, pl.ds(off_lo, tok), 0:D] = kk[:tok]
        KV[slot, pl.ds(off_lo, tok), D : 2 * D] = vv[:tok]
        KV[slot, pl.ds(off_hi, tok), 0:D] = kk[tok:]
        KV[slot, pl.ds(off_hi, tok), D : 2 * D] = vv[tok:]
        sends = kv_copies(slot)
        for cp in sends:
            cp.start()
        q = (nn(a, wq[l, :, 0:D]) + qb[pl.ds(l, 1), :]).astype(BF16)
        Q[slot] = q * jnp.asarray(0.125, BF16)

        @pl.when(s >= 1)
        def _():
            for cp in sel_copies_out(0, 0):
                cp.wait()

        asel[...] = nt(sel[0], a).astype(BF16)
        for cp in kv_arrivals(slot):
            cp.wait_recv()
        for cp in sends:
            cp.wait_send()

        @pl.when(s < STEPS - 2)
        def _():
            kv_stash(s, slot).start()

        def pair(p, carry):
            at = pl.ds(pl.multiple_of(p * 128, 128), 128)
            atv = pl.ds(pl.multiple_of(D + p * 128, 128), 128)
            kp = KV[slot, :, at]
            vp = KV[slot, :, atv]
            qp = Q[slot, :, at]
            outs = []
            for e in range(2):
                qe = jnp.where(low if e == 0 else jnp.logical_not(low), qp, jnp.zeros_like(qp))
                s1 = nt(kp[:T], qe) * LOG2E + bias1[...]
                s2 = nt(kp[T:], qe[tok:]) * LOG2E + bias2[...]
                m1 = jnp.max(s1, axis=0, keepdims=True)
                m2 = jnp.max(s2, axis=0, keepdims=True)
                m = jnp.concatenate([m1[:, :tok], jnp.maximum(m1[:, tok:], m2)], axis=1)
                e1 = jnp.exp2(s1 - m)
                e2 = jnp.exp2(s2 - m[:, tok:])
                l1 = jnp.sum(e1, axis=0, keepdims=True)
                l2 = jnp.sum(e2, axis=0, keepdims=True)
                ll = jnp.concatenate([l1[:, :tok], l1[:, tok:] + l2], axis=1)
                rl = 1.0 / ll
                p1 = (e1 * rl).astype(BF16)
                p2 = (e2 * rl[:, tok:]).astype(BF16)
                LSE[slot, p, e : e + 1, :] = m + jnp.log2(ll)
                o1 = tn(p1, vp[:T])
                o2 = tn(p2, vp[T:])
                outs.append(jnp.concatenate([o1[:tok], o1[tok:] + o2], axis=0))
            O[:, at] = jnp.where(low, outs[0], outs[1]).astype(BF16)
            return carry

        lax.fori_loop(0, HEADS // 2, pair, 0)

        @pl.when(s < 2)
        def _():
            pltpu.make_async_copy(wo_h.at[l], wo.at[l], w_sem.at[l, 1]).wait()

        o = O[...]
        osel[...] = nt(sel[0], o).astype(BF16)
        m = x + (nn(o, wo[l]) + ob[pl.ds(l, 1), :])
        M[slot] = m
        hat2, _ = normalised(m)
        a2 = (hat2 * ln2g[pl.ds(l, 1), :] + ln2b[pl.ds(l, 1), :]).astype(BF16)
        usel[...] = nt(sel[1], a2).astype(BF16)

        @pl.when(s < 2)
        def _():
            pltpu.make_async_copy(wu_h.at[l], wu.at[l], w_sem.at[l, 2]).wait()

        for j in range(FF // D):
            js = slice(j * D, (j + 1) * D)
            f = nn(a2, wu[l, :, js]) + ub[pl.ds(l, 1), js]
            f2 = f * f
            u = f * (0.7978845608028654 + 0.035677408136300125 * f2)
            t = jnp.tanh(u)
            h = 0.5 + 0.5 * t
            ga = f * h
            gp = h + ga * (1.0 - h) * (1.5957691216057308 + 0.21406444881780074 * f2)
            gb = ga.astype(BF16)
            GF[:, js] = gb
            GP[slot, :, js] = gp.astype(BF16)
            gs = nt(sel[2], gb).astype(BF16)
            n = plan.per * 2 * plan.cf
            for cc in range(2):
                gsel[cc * plan.frows + j * n : cc * plan.frows + (j + 1) * n] = gs[cc * n : (cc + 1) * n]

        @pl.when(s < 2)
        def _():
            pltpu.make_async_copy(wd_h.at[l], wd.at[l], w_sem.at[l, 3]).wait()

        y = m + (nn(GF[...], wd[l]) + db[pl.ds(l, 1), :])
        last = jnp.logical_and(l == 1, sect < MAXP)
        bar = jnp.where(last, sect, -1).astype(F32)
        XN[...] = jnp.where(passes > bar, y, X[0])

        @pl.when(s < STEPS - 2)
        def _():
            for cp in stash_copies(s, slot, st_sem, False):
                cp.start()
            kv_stash(s, slot).wait()

        for cp in sel_copies_out(l, sect):
            cp.start()
        return carry

    lax.fori_loop(0, STEPS, forward, 0)

    block = jnp.where(z < 2, c, 3 - c)
    owner = (col * 2 + parity, block)
    mine = jnp.logical_and(parity == c, block == z)

    def give_back(i):
        @pl.when(z < 2)
        def _():
            ret_s[i] = XN[0:tok] if i == 0 else R[0:tok]

        @pl.when(z >= 2)
        def _():
            ret_s[i] = XN[tok:T] if i == 0 else R[tok:T]

        @pl.when(mine)
        def _():
            pltpu.make_async_copy(ret_s.at[i], ret_r.at[i], ret_recv.at[i]).start()

        @pl.when(jnp.logical_not(mine))
        def _():
            pltpu.make_async_remote_copy(
                src_ref=ret_s.at[i], dst_ref=ret_r.at[i], send_sem=ret_send.at[i], recv_sem=ret_recv.at[i],
                device_id=owner, device_id_type=MESH,
            ).start()

    def take_back(i, out):
        pltpu.make_async_copy(ret_s.at[i], ret_r.at[i], ret_recv.at[i]).wait()

        @pl.when(jnp.logical_not(mine))
        def _():
            pltpu.make_async_remote_copy(
                src_ref=ret_s.at[i], dst_ref=ret_r.at[i], send_sem=ret_send.at[i], recv_sem=ret_recv.at[i],
                device_id=owner, device_id_type=MESH,
            ).wait_send()

        out[...] = ret_r[i]

    give_back(0)
    deliver_wait(cot_own, cot, cot_recv)
    deliver_sent(cot_own, cot, cot_send, cot_recv)
    U[0:tok] = cot[0]
    U[tok:T] = cot[1]
    for cp in sel_copies_out(0, 0):
        cp.wait()

    def back_copies(l, sect):
        at = pl.ds(pl.multiple_of(sect * T, T), T)
        return [
            pltpu.make_async_copy(DP, dp_h.at[l, at, :], bst_sem.at[0]),
            pltpu.make_async_copy(DY, dy_h.at[l, at, :], bst_sem.at[1]),
            pltpu.make_async_copy(GF, df_h.at[l, at, :], bst_sem.at[2]),
            pltpu.make_async_copy(DR, dr_h.at[l, at, :], bst_sem.at[3]),
        ]

    def dkv_copies(par):
        out = []
        for i, off in enumerate((poff_lo, poff_hi)):
            out.append(
                pltpu.make_async_remote_copy(
                    src_ref=DKV.at[pl.ds(off, tok), :], dst_ref=RDKV.at[par, i],
                    send_sem=dkv_send.at[par, i], recv_sem=dkv_recv.at[par, i],
                    device_id=peer, device_id_type=MESH,
                )
            )
        return out

    def backward(i, carry):
        s = STEPS - 1 - i
        l = lax.rem(s, LAYERS)
        sect = lax.div(s, LAYERS)
        slot = lax.rem(s, 2)

        @pl.when(i >= 1)
        def _():
            for cp in back_copies(0, 0):
                cp.wait()

        @pl.when(i >= 2)
        def _():
            for cp in stash_copies(s, slot, ld_sem, True):
                cp.wait()
            kv_load(s, slot).wait()

        active = jnp.where(
            passes > jnp.where(sect == MAXP, -1, sect).astype(F32), jnp.ones((1, 1), F32), jnp.zeros((1, 1), F32)
        )

        @pl.when(l == 1)
        def _():
            R[...] = U[...] * active

        r = R[...]
        dr = r.astype(BF16)
        DR[...] = dr
        VAC[l, 7:8] += column_sum(dr.astype(F32))
        for j in range(FF // D):
            js = slice(j * D, (j + 1) * D)
            dg = nt(dr, wd[l, js, :])
            df = (dg * GP[slot, :, js].astype(F32)).astype(BF16)
            GF[:, js] = df
            VAC[l, 8 + j : 9 + j] += column_sum(df.astype(F32))
        da2 = nt(GF[...], wu[l])
        hat2, inv2 = normalised(M[slot])
        VAC[l, 5:6] += column_sum(da2 * hat2)
        VAC[l, 6:7] += column_sum(da2)
        dm = r + norm_back(da2, ln2g[pl.ds(l, 1), :], hat2, inv2)
        R[...] = dm
        dy = dm.astype(BF16)
        DY[...] = dy
        VAC[l, 4:5] += column_sum(dy.astype(F32))
        O[...] = nt(dy, wo[l]).astype(BF16)

        def pair(p, carry):
            at = pl.ds(pl.multiple_of(p * 128, 128), 128)
            atv = pl.ds(pl.multiple_of(D + p * 128, 128), 128)
            kp = KV[slot, :, at]
            vp = KV[slot, :, atv]
            qp = Q[slot, :, at]
            dop = O[:, at]
            zero = jnp.zeros_like(qp)
            pb1, pb2, t1, t2, qs, dos, dq = [], [], [], [], [], [], []
            for e in range(2):
                keep = low if e == 0 else jnp.logical_not(low)
                qe = jnp.where(keep, qp, zero)
                doe = jnp.where(keep, dop, zero)
                lse = LSE[slot, p, e : e + 1, :]
                s1 = nt(kp[:T], qe) * LOG2E + bias1[...]
                s2 = nt(kp[T:], qe[tok:]) * LOG2E + bias2[...]
                p1 = jnp.exp2(s1 - lse)
                p2 = jnp.exp2(s2 - lse[:, tok:])
                d1 = nt(vp[:T], doe)
                d2 = nt(vp[T:], doe[tok:])
                i1 = jnp.sum(p1 * d1, axis=0, keepdims=True)
                i2 = jnp.sum(p2 * d2, axis=0, keepdims=True)
                inner = jnp.concatenate([i1[:, :tok], i1[:, tok:] + i2], axis=1)
                x1 = (p1 * (d1 - inner)).astype(BF16)
                x2 = (p2 * (d2 - inner[:, tok:])).astype(BF16)
                pb1.append(p1.astype(BF16))
                pb2.append(p2.astype(BF16))
                t1.append(x1)
                t2.append(x2)
                qs.append(qe)
                dos.append(doe)
                q1 = tn(x1, kp[:T])
                q2 = tn(x2, kp[T:])
                dq.append(jnp.concatenate([q1[:tok], q1[tok:] + q2], axis=0))
            DP[:, at] = (jnp.where(low, dq[0], dq[1]) * 0.125).astype(BF16)
            dos_all = jnp.concatenate(dos, axis=0)
            qs_all = jnp.concatenate(qs, axis=0)
            dos_hi = jnp.concatenate([dos[0][tok:], dos[1][tok:]], axis=0)
            qs_hi = jnp.concatenate([qs[0][tok:], qs[1][tok:]], axis=0)
            DKV[0:T, atv] = nn(jnp.concatenate(pb1, axis=1), dos_all).astype(BF16)
            DKV[T : 2 * T, atv] = nn(jnp.concatenate(pb2, axis=1), dos_hi).astype(BF16)
            DKV[0:T, at] = nn(jnp.concatenate(t1, axis=1), qs_all).astype(BF16)
            DKV[T : 2 * T, at] = nn(jnp.concatenate(t2, axis=1), qs_hi).astype(BF16)
            return carry

        lax.fori_loop(0, HEADS // 2, pair, 0)
        sends = dkv_copies(slot)
        for cp in sends:
            cp.start()

        x = X[slot]
        hat, inv = normalised(x)

        @pl.when(s >= 2)
        def _():
            for cp in stash_copies(s - 2, slot, ld_sem, True):
                cp.start()
            kv_load(s - 2, slot).start()

        dqb = DP[:, 0:D]
        VAC[l, 2:3] += column_sum(dqb.astype(F32))
        da = nt(dqb, wq[l, :, 0:D])
        for cp in sends:
            cp.wait_recv()
        for j in range(2):
            off = off_lo if j == 0 else off_hi
            dkv = (DKV[pl.ds(off, tok), :].astype(F32) + RDKV[slot, j].astype(F32)).astype(BF16)
            DP[j * tok : (j + 1) * tok, D : 3 * D] = dkv
        for cp in sends:
            cp.wait_send()
        dkv = DP[:, D : 3 * D]
        VAC[l, 3:4] += column_sum(dkv[:, D:].astype(F32))
        da = da + nt(dkv, wq[l, :, D : 3 * D])
        VAC[l, 0:1] += column_sum(da * hat)
        VAC[l, 1:2] += column_sum(da)
        R[...] = R[...] + norm_back(da, ln1g[pl.ds(l, 1), :], hat, inv)

        @pl.when(l == 0)
        def _():
            U[...] = R[...] + (1.0 - active) * U[...]

        for cp in back_copies(l, sect):
            cp.start()
        return carry

    lax.fori_loop(0, STEPS, backward, 0)
    take_back(0, hid_o)
    R[...] = U[...] * factor[0:1, 0:1]
    give_back(1)
    vec_o[...] = VAC[...] * factor[0:1, 0:1]
    for cp in back_copies(0, 0):
        cp.wait()
    take_back(1, gin_o)


def run_main(plan, x, cot, par, vecs, sel, weights):
    tok = plan.tok
    T = 2 * tok
    L = 4 * tok
    vmem = pl.BlockSpec(memory_space=pltpu.VMEM)
    hbm = pl.BlockSpec(memory_space=pl.ANY)
    S = jax.ShapeDtypeStruct
    K = (MAXP + 1) * T
    outs = [
        (S((tok, D), F32), vmem),
        (S((tok, D), F32), vmem),
        (S((LAYERS, 16, D), F32), vmem),
        (S((8, 128), F32), vmem),
        (S((LAYERS, plan.nsel, K), BF16), hbm),
        (S((LAYERS, plan.nsel, K), BF16), hbm),
        (S((LAYERS, plan.nsel, K), BF16), hbm),
        (S((LAYERS, 2 * plan.frows, K), BF16), hbm),
        (S((LAYERS, K, 3 * D), BF16), hbm),
        (S((LAYERS, K, D), BF16), hbm),
        (S((LAYERS, K, FF), BF16), hbm),
        (S((LAYERS, K, D), BF16), hbm),
        (S((STEPS, T, D), F32), hbm),
        (S((STEPS, T, D), BF16), hbm),
        (S((STEPS, L, 2 * D), BF16), hbm),
        (S((STEPS, 8, 8, T), F32), hbm),
        (S((STEPS, T, D), F32), hbm),
        (S((STEPS, T, FF), BF16), hbm),
    ]
    V = pltpu.VMEM
    DMA = pltpu.SemaphoreType.DMA
    nb = max(plan.bits, 1)
    scratch = [
        V((LAYERS, D, 3 * D), BF16), V((LAYERS, D, D), BF16), V((LAYERS, D, FF), BF16), V((LAYERS, FF, D), BF16),
        V((3, sel.shape[2], D), BF16), V((2, tok, D), BF16), V((2, tok, D), F32), V((8, 128), F32),
        V((nb, 8, 128), F32), V((nb, 8, 128), F32),
        V((T, T), F32), V((T, tok), F32),
        V((2, T, D), F32), V((2, T, D), BF16), V((2, L, 2 * D), BF16), V((2, 8, 8, T), F32), V((2, T, D), F32),
        V((2, T, FF), BF16), V((T, D), BF16), V((T, FF), BF16), V((T, D), F32),
        V((plan.nsel, T), BF16), V((plan.nsel, T), BF16), V((plan.nsel, T), BF16), V((2 * plan.frows, T), BF16),
        V((T, D), F32), V((T, D), F32), V((L, 2 * D), BF16), V((2, 2, tok, 2 * D), BF16), V((T, 3 * D), BF16),
        V((T, D), BF16), V((T, D), BF16), V((LAYERS, 16, D), F32), V((2, tok, D), F32), V((2, tok, D), F32),
        DMA((LAYERS, 4)), DMA((3,)), DMA((2,)), DMA((2,)), DMA((2,)), DMA((2,)), DMA((2,)), DMA((2, nb)),
        DMA((2, 2)), DMA((2, 2)), DMA((2, 6)), DMA((2, 6)), DMA((4,)), DMA((2, 2)), DMA((2, 2)), DMA((4,)),
        DMA((2,)), DMA((2,)), DMA((2,)),
    ]
    call = pl.pallas_call(
        functools.partial(main_kernel, plan),
        out_shape=[o[0] for o in outs],
        out_specs=[o[1] for o in outs],
        in_specs=[vmem, vmem, vmem] + [vmem] * 9 + [hbm] * 5,
        scratch_shapes=scratch,
        compiler_params=pltpu.CompilerParams(
            collective_id=0, has_side_effects=True, vmem_limit_bytes=60 * 2**20
        ),
        name="layers",
    )
    return call(x, cot, par, *vecs, sel, *weights)


def fold(x):
    n = x.shape[1] // 2
    return jnp.concatenate([x[:, :n], x[:, n:]], axis=0)


def unfold(x):
    n = x.shape[0] // 2
    return jnp.concatenate([x[:n], x[n:]], axis=1)


class Item:
    def __init__(self, name, rows, cols, order):
        self.name, self.rows, self.cols, self.order = name, rows, cols, order


def items_of(plan):
    return [
        Item("down", plan.frows, D, plan.order_down),
        Item("up", plan.rows, FF, plan.order_up),
        Item("out", plan.rows, D, plan.order_qkv),
        Item("qkv", plan.rows, 3 * D, plan.order_qkv),
    ]


def sum_kernel(plan, vec_ref, tot_ref, asel_h, osel_h, usel_h, gsel_h, dp_h, dy_h, df_h, dr_h, *refs):
    items = items_of(plan)
    n = len(items)
    outs, vec_o, refs = refs[:n], refs[n], refs[n + 1 :]
    lhs, rhs, refs = refs[:n], refs[n : 2 * n], refs[2 * n :]
    W, C, refs = refs[:n], refs[n : 2 * n], refs[2 * n :]
    stages = plan.bits + 1
    RB = []
    for k in range(stages - 1):
        RB.append(refs[:n])
        refs = refs[n:]
    FS, FR, FB, refs = refs[:n], refs[n : 2 * n], refs[2 * n : 3 * n], refs[3 * n :]
    vs, vr, l_sem, chip_sem, stage_sem, vec_sem = refs
    g, z, c, col, outer, parity = where_am_i()
    peer = (col * 2 + 1 - c, z)
    sources = ((gsel_h, dr_h), (usel_h, df_h), (osel_h, dy_h), (asel_h, dp_h))

    def loads(l, i):
        a, b = sources[i]
        return (
            pltpu.make_async_copy(a.at[l], lhs[i], l_sem.at[i, 0]),
            pltpu.make_async_copy(b.at[l], rhs[i], l_sem.at[i, 1]),
        )

    for i in range(n):
        for cp in loads(LAYERS - 1, i):
            cp.start()

    def partner(dim):
        if dim < 0:
            return (g, z + 1 - 2 * lax.rem(z, 2))
        return ((col ^ (1 << dim)) * 2 + c, z)

    def bit_of(dim):
        if dim < 0:
            return lax.rem(z, 2)
        return lax.rem(lax.div(col, 1 << dim), 2)

    dims = [-1] + list(range(plan.bits))
    barrier = pltpu.get_barrier_semaphore()
    pl.semaphore_signal(barrier, inc=1, device_id=peer, device_id_type=MESH)
    for dim in dims:
        pl.semaphore_signal(barrier, inc=1, device_id=partner(dim), device_id_type=MESH)
    pl.semaphore_wait(barrier, 1 + len(dims))

    vec_targets = [peer] + [partner(dim) for dim in dims]
    vs[0] = vec_ref[...]

    def vec_copy(k):
        return pltpu.make_async_remote_copy(
            src_ref=vs.at[k], dst_ref=vr.at[k], send_sem=vec_sem.at[0, k], recv_sem=vec_sem.at[1, k],
            device_id=vec_targets[k], device_id_type=MESH,
        )

    vec_copy(0).start()

    def vec_step(k):
        vec_copy(k).wait()
        if k + 1 < len(vec_targets):
            vs[k + 1] = vs[k] + vr[k]
            vec_copy(k + 1).start()
        else:
            vec_o[...] = vs[k] + vr[k]

    factor = tot_ref[0:1, 0:1]

    def chip_copy(l, i):
        rows = items[i].rows
        at = pl.ds(pl.multiple_of((1 - c) * rows, 16), rows)
        return pltpu.make_async_remote_copy(
            src_ref=W[i].at[l, at, :], dst_ref=C[i].at[l], send_sem=chip_sem.at[0, l, i],
            recv_sem=chip_sem.at[1, l, i], device_id=peer, device_id_type=MESH,
        )

    def base_of(i, k):
        item = items[i]
        base, rows = c * item.rows, item.rows
        for j in range(k):
            rows //= 2
            base = base + bit_of(item.order[j]) * rows
        return base, rows

    def stage_copy(l, i, k):
        item = items[i]
        if k == stages - 1:
            src, dst = FS[i].at[l], FR[i].at[l]
        else:
            base, rows = base_of(i, k)
            rows //= 2
            first = base + (1 - bit_of(item.order[k])) * rows
            src, dst = W[i].at[l, pl.ds(pl.multiple_of(first, 16), rows), :], RB[k][i].at[l]
        return pltpu.make_async_remote_copy(
            src_ref=src, dst_ref=dst, send_sem=stage_sem.at[0, l, i, k], recv_sem=stage_sem.at[1, l, i, k],
            device_id=partner(item.order[k]), device_id_type=MESH,
        )

    def compute(l, i):
        for cp in loads(l, i):
            cp.wait()
        item = items[i]
        left = lhs[i][...]
        step = D
        for j in range(item.cols // step):
            js = slice(j * step, (j + 1) * step)
            W[i][l, :, js] = (nn(left, rhs[i][:, js]) * factor).astype(BF16)
        if l > 0:
            for cp in loads(l - 1, i):
                cp.start()
        chip_copy(l, i).start()

    def after_chip(l, i):
        chip_copy(l, i).wait()
        rows = items[i].rows
        at = pl.ds(pl.multiple_of(c * rows, 16), rows)
        W[i][l, at, :] = (W[i][l, at, :].astype(F32) + C[i][l].astype(F32)).astype(BF16)
        stage_copy(l, i, 0).start()

    def after_stage(l, i, k):
        item = items[i]
        stage_copy(l, i, k).wait()
        if k == stages - 1:
            rows = FB[i].shape[1] // 2
            first = pl.multiple_of(bit_of(item.order[k]) * rows, 8)
            mine = FB[i][l, pl.ds(first, rows), :] + unfold(FR[i][l].astype(F32))
            outs[i][l] = mine[: outs[i].shape[1]]
            return
        base, rows = base_of(i, k + 1)
        at = pl.ds(pl.multiple_of(base, 16), rows)
        both = W[i][l, at, :].astype(F32) + RB[k][i][l].astype(F32)
        if k + 1 == stages - 1:
            FB[i][l] = both
            rows //= 2
            first = pl.multiple_of((1 - bit_of(item.order[k + 1])) * rows, 8)
            FS[i][l] = fold(FB[i][l, pl.ds(first, rows), :]).astype(BF16)
        else:
            W[i][l, at, :] = both.astype(BF16)
        stage_copy(l, i, k + 1).start()

    work = [(l, i) for l in range(LAYERS - 1, -1, -1) for i in range(n)]
    for t, (l, i) in enumerate(work):
        compute(l, i)
        if t > 0:
            after_chip(*work[t - 1])
        if t > 0 and t - 1 < len(vec_targets):
            vec_step(t - 1)
    after_chip(*work[-1])
    for k in range(len(work) - 1, len(vec_targets)):
        vec_step(k)
    for k in range(stages):
        for l, i in work:
            after_stage(l, i, k)


def run_sum(plan, vec, tot, stashes):
    vmem = pl.BlockSpec(memory_space=pltpu.VMEM)
    hbm = pl.BlockSpec(memory_space=pl.ANY)
    S = jax.ShapeDtypeStruct
    V = pltpu.VMEM
    DMA = pltpu.SemaphoreType.DMA
    items = items_of(plan)
    stages = plan.bits + 1
    own = {"down": plan.cf, "up": plan.ch, "out": plan.ch, "qkv": plan.ch}
    outs = [S((LAYERS, own[i.name], i.cols), F32) for i in items] + [S(vec.shape, F32)]
    K = stashes[0].shape[2]
    scratch = [V((2 * i.rows, K), BF16) for i in items]
    scratch += [V((K, i.cols), BF16) for i in items]
    scratch += [V((LAYERS, 2 * i.rows, i.cols), BF16) for i in items]
    scratch += [V((LAYERS, i.rows, i.cols), BF16) for i in items]
    for k in range(stages - 1):
        scratch += [V((LAYERS, i.rows >> (k + 1), i.cols), BF16) for i in items]
    last = [i.rows >> stages for i in items]
    scratch += [V((LAYERS, 2 * r, i.cols // 2), BF16) for r, i in zip(last, items)]
    scratch += [V((LAYERS, 2 * r, i.cols // 2), BF16) for r, i in zip(last, items)]
    scratch += [V((LAYERS, 2 * r, i.cols), F32) for r, i in zip(last, items)]
    nv = 2 + plan.bits
    scratch += [
        V((nv,) + vec.shape, F32), V((nv,) + vec.shape, F32), DMA((len(items), 2)),
        DMA((2, LAYERS, len(items))), DMA((2, LAYERS, len(items), stages)), DMA((2, nv)),
    ]
    call = pl.pallas_call(
        functools.partial(sum_kernel, plan),
        out_shape=outs,
        out_specs=[vmem] * len(outs),
        in_specs=[vmem, vmem] + [hbm] * 8,
        scratch_shapes=scratch,
        compiler_params=pltpu.CompilerParams(
            collective_id=1, has_side_effects=True, vmem_limit_bytes=60 * 2**20
        ),
        name="sums",
    )
    return call(vec, tot, *stashes)


def body(
    plan,
    inputs, cotangent, pass_counts, doc_starts, token_counts,
    ln1_gain, ln1_bias, qkv_weight, query_bias, value_bias, out_weight, out_bias,
    ln2_gain, ln2_bias, up_weight, up_bias, down_weight, down_bias,
):
    numbers = jnp.concatenate([pass_counts, token_counts, doc_starts[0], jnp.zeros((2,), jnp.int32)])
    par = jnp.broadcast_to(numbers.astype(F32)[:, None], (8, 128))
    ff = plan.selector_ff()
    wide = np.zeros((3, 2, max(plan.nsel, ff.shape[1]), D), np.float32)
    wide[0, :, : plan.nsel] = plan.selector(plan.order_qkv)
    wide[1, :, : plan.nsel] = plan.selector(plan.order_up)
    wide[2, :, : ff.shape[1]] = ff
    sel = jnp.asarray(wide.astype(jnp.bfloat16))
    vecs = (ln1_gain, ln1_bias, query_bias, value_bias, out_bias, ln2_gain, ln2_bias, up_bias, down_bias)
    weights = (qkv_weight, out_weight, up_weight, down_weight)
    hidden, grad_in, vec, tot, *rest = run_main(plan, inputs, cotangent, par, vecs, sel, weights)
    g_down, g_up, g_out, g_qkv, vec = run_sum(plan, vec, tot, rest[:8])
    me = lax.axis_index("grp") * plan.nrow + lax.axis_index("row")

    def own(row):
        return lax.dynamic_slice(vec[:, row, :], (0, me * plan.ch), (LAYERS, plan.ch))

    up_vec = vec[:, 8:12, :].reshape(LAYERS, FF)
    g_ub = lax.dynamic_slice(up_vec, (0, me * plan.cf), (LAYERS, plan.cf))
    return (
        hidden, grad_in, own(0), own(1), g_qkv, own(2), own(3), g_out, own(4), own(5), own(6),
        g_up, g_ub, g_down, own(7),
    )


def solution(mesh):
    ngrp, nrow = mesh.shape["grp"], mesh.shape["row"]
    whole = P(("grp", "row"), None)
    vector = P(None, ("grp", "row"))
    matrix = P(None, ("grp", "row"), None)

    def run(*args):
        return body(Plan(ngrp, nrow, args[0].shape[0]), *args)

    return jax.shard_map(
        run,
        mesh=mesh,
        in_specs=(whole, whole, P("grp"), P("grp", None), P("grp")) + (P(),) * 13,
        out_specs=(
            whole, whole, vector, vector, matrix, vector, vector, matrix, vector, vector, vector,
            matrix, vector, matrix, vector,
        ),
        check_vma=False,
    )
```

```python
import functools

import jax
import jax.numpy as jnp
import numpy as np
from jax import lax
from jax.experimental import pallas as pl
from jax.experimental.pallas import tpu as pltpu
from jax.sharding import PartitionSpec as P

HEADS = 12
HEAD = 64
D = 768
FF = 3072
LAYERS = 2
MAXP = 2
STEPS = LAYERS * (MAXP + 1)

EPS = 1e-05
NEG = -1000000000.0
LOG2E = 1.4426950408889634
MESH = pl.DeviceIdType.MESH
VMEM_LIMIT = 63 * 2**20
F32 = jnp.float32
BF16 = jnp.bfloat16


def nn(a, b):
    return jnp.dot(a, b, preferred_element_type=F32)


def nt(a, b):
    return lax.dot_general(a, b, (((1,), (1,)), ((), ())), preferred_element_type=F32)


def tn(a, b):
    return lax.dot_general(a, b, (((0,), (0,)), ((), ())), preferred_element_type=F32)


def normalised(x):
    mean = jnp.mean(x, axis=-1, keepdims=True)
    centred = x - mean
    spread = jnp.mean(centred * centred, axis=-1, keepdims=True)
    inv = lax.rsqrt(spread + EPS)
    return centred * inv, inv


def norm_back(grad, gain, hat, inv):
    g = grad * gain
    mean_g = jnp.mean(g, axis=-1, keepdims=True)
    mean_gh = jnp.mean(g * hat, axis=-1, keepdims=True)
    return inv * (g - mean_g - hat * mean_gh)


def column_sum(x):
    return jnp.sum(x, axis=0, keepdims=True)


def of_head(h):
    p = h // 2
    at, atv = slice(p * 128, (p + 1) * 128), slice(D + p * 128, D + (p + 1) * 128)
    low = lax.broadcasted_iota(jnp.int32, (1, 128), 1) < HEAD
    return at, atv, low if h % 2 == 0 else jnp.logical_not(low)


def attention_forward(KV, Q, LSE, bias, O):
    def scores(h):
        at, _, keep = of_head(h)
        qp = Q[:, at]
        return nt(KV[:, at], jnp.where(keep, qp, jnp.zeros_like(qp)))

    def mixed(h, raw):
        _, atv, _ = of_head(h)
        logits = raw * LOG2E + bias[...]
        top = jnp.max(logits, axis=0, keepdims=True)
        expo = jnp.exp2(logits - top)
        denom = jnp.sum(expo, axis=0, keepdims=True)
        LSE[h // 2, h % 2 : h % 2 + 1, :] = top + jnp.log2(denom)
        return tn((expo * (1.0 / denom)).astype(BF16), KV[:, atv])

    ahead = scores(0)
    even = None
    for h in range(HEADS):
        raw = ahead
        if h + 1 < HEADS:
            ahead = scores(h + 1)
        out = mixed(h, raw)
        if h % 2 == 0:
            even = out
        else:
            at, _, high = of_head(h)
            O[:, at] = jnp.where(high, out, even).astype(BF16)


def attention_backward(KV, Q, LSE, bias, DO, DP, DKV, between):
    low_row = lax.broadcasted_iota(jnp.int32, (128, 1), 0) < HEAD

    def parts(h):
        at, atv, keep = of_head(h)
        qp, dop = Q[:, at], DO[:, at]
        zero = jnp.zeros_like(qp)
        return KV[:, at], KV[:, atv], jnp.where(keep, qp, zero), jnp.where(keep, dop, zero)

    def products(h):
        kp, vp, qe, doe = parts(h)
        return nt(kp, qe), nt(vp, doe)

    def grads(h, raw, dpr):
        lse = LSE[h // 2, h % 2 : h % 2 + 1, :]
        pr = jnp.exp2(raw * LOG2E + bias[...] - lse)
        inner = jnp.sum(pr * dpr, axis=0, keepdims=True)
        return pr.astype(BF16), (pr * (dpr - inner)).astype(BF16)

    def finish(h0, one, two):
        at, atv, _ = of_head(h0)
        kp, _, q0, do0 = parts(h0)
        _, _, q1, do1 = parts(h0 + 1)
        dqt = jnp.where(low_row, tn(kp, one[1]), tn(kp, two[1])) * 0.125
        DP[:, at] = dqt.T.astype(BF16)
        DKV[:, atv] = nn(
            jnp.concatenate([one[0], two[0]], axis=1), jnp.concatenate([do0, do1], axis=0)
        ).astype(BF16)
        DKV[:, at] = nn(
            jnp.concatenate([one[1], two[1]], axis=1), jnp.concatenate([q0, q1], axis=0)
        ).astype(BF16)

    ahead = products(0)
    even = None
    for h in range(HEADS):
        now = ahead
        if h + 1 < HEADS:
            ahead = products(h + 1)
        pair = grads(h, *now)
        if h % 2 == 0:
            even = pair
        else:
            finish(h - 1, even, pair)
        if h in between:
            between[h]()


class Plan:
    def __init__(self, ngrp, nrow, tok):
        self.ngrp, self.nrow, self.tok = ngrp, nrow, tok
        self.ncol = ngrp // 2
        self.bits = max(self.ncol.bit_length() - 1, 0)
        self.ndev = ngrp * nrow
        self.ch = D // self.ndev
        self.chp = -(-self.ch // 8) * 8
        self.cf = FF // self.ndev
        self.rows = self.ncol * 2 * self.chp
        self.nsel = 2 * self.rows
        self.wide = FF // ngrp
        self.per = D // (2 * self.wide)
        self.frows = self.ncol * 2 * self.cf
        cols = list(range(self.bits))[::-1]
        self.order_up = cols[1:] + [-1] + cols[:1]
        self.order_qkv = [-1] + cols
        self.order_down = cols + [-1]

    def selector(self, order):
        table = np.zeros((2, self.nsel, D), np.float32)
        for half in range(2):
            for c in range(2):
                for piece in range(self.ncol * 2):
                    col, pair = 0, 0
                    for place, dim in enumerate(order):
                        bit = (piece >> (len(order) - 1 - place)) & 1
                        if dim < 0:
                            pair = bit
                        else:
                            col |= bit << dim
                    first = ((col * 2 + c) * 4 + 2 * half + pair) * self.ch
                    row = c * self.rows + piece * self.chp
                    for i in range(self.ch):
                        table[half, row + i, first + i] = 1
        return table

    def selector_ff(self):
        table = np.zeros((2, self.nsel, D), np.float32)
        for half in range(2):
            for c in range(2):
                row = c * self.rows
                for j in range(self.per):
                    first = (j * 2 + c) * self.wide + half * 2 * self.cf
                    for i in range(2 * self.cf):
                        table[half, row, first + i] = 1
                        row += 1
        return table


def where_am_i():
    g = lax.axis_index("grp")
    z = lax.axis_index("row")
    c = lax.rem(g, 2)
    col = lax.div(g, 2)
    outer = jnp.logical_or(z == 0, z == 3)
    parity = jnp.where(outer, 0, 1)
    return g, z, c, col, outer, parity


def fill_bias(bias, starts, c, tok):
    T = 2 * tok
    lane = lax.broadcasted_iota(jnp.int32, (1, T), 1)
    qpos = jnp.where(lane < tok, c * tok + lane, (3 - c) * tok + lane - tok).astype(F32)
    begin = jnp.zeros((1, T), F32)
    for start in starts:
        begin = jnp.maximum(begin, jnp.where(qpos >= start, start, 0.0))
    kpos = lax.broadcasted_iota(jnp.int32, (2 * T, T), 0).astype(F32)
    bias[...] = jnp.where((kpos <= qpos) & (kpos >= begin), 0.0, NEG)


def main_kernel(
    plan,
    x_own, cot_own, pass_ref, doc_ref, tok_ref, ln1g, ln1b, qb, vb, ob, ln2g, ln2b, ub, db, sel_h,
    wq_h, wo_h, wu_h, wd_h,
    hid_o, up_o, vec_o, tot_o, asel_h, osel_h, usel_h, gsel_h, dp_h, dy_h, df_h, dr_h,
    sx_h, sq_h, skv_h, slse_h, sm_h, sgp_h,
    wq, wo, wu, wd, sel, xin, cot, par_ref, par_in, tsend, trecv,
    bias, X, Q, KV, LSE, M, GP, O, GF, XN, asel, osel, usel, gsel,
    R, U, DKV, RDKV, DP, DR, DY, VAC, ret_s, ret_r,
    w_sem, sel_sem, in_send, in_recv, cot_send, cot_recv, par_sem, t_sem, kv_send, kv_recv,
    st_sem, ld_sem, sel_out, dkv_send, dkv_recv, bst_sem, ret_send, ret_recv,
):
    tok = plan.tok
    T = 2 * tok
    g, z, c, col, outer, parity = where_am_i()
    half = lax.div(z, 2)
    peer = (col * 2 + 1 - c, z)
    off_lo = pl.multiple_of(c * tok, tok)
    off_hi = pl.multiple_of((3 - c) * tok, tok)
    poff_lo = pl.multiple_of((1 - c) * tok, tok)
    poff_hi = pl.multiple_of((2 + c) * tok, tok)

    weight_copies = []
    for l in range(LAYERS):
        for i, (src, dst) in enumerate(((wq_h, wq), (wo_h, wo), (wu_h, wu), (wd_h, wd))):
            weight_copies.append(pltpu.make_async_copy(src.at[l], dst.at[l], w_sem.at[l, i]))
    weight_copies[0].start()
    n_rows = sel.shape[1] // 2
    sel_copies = []
    for i in range(3):
        for j, core in enumerate((c, 1 - c)):
            src = sel_h.at[i, half, pl.ds(pl.multiple_of(core * n_rows, 16), n_rows), :]
            dst = sel.at[i, pl.ds(j * n_rows, n_rows), :]
            sel_copies.append(pltpu.make_async_copy(src, dst, sel_sem.at[i, j]))
    for cp in sel_copies:
        cp.start()

    numbers = [pass_ref[0], tok_ref[0]] + [doc_ref[0, k] for k in range(4)] + [0, 0]
    for k, number in enumerate(numbers):
        par_ref[k : k + 1, :] = jnp.full((1, 128), number, jnp.int32).astype(F32)

    barrier = pltpu.get_barrier_semaphore()
    count = 0
    for dc in range(2):
        for dz in range(plan.nrow):
            if dc == 0 and dz == 0:
                continue
            target = (col * 2 + lax.rem(c + dc, 2), lax.rem(z + dz, plan.nrow))
            pl.semaphore_signal(barrier, inc=1, device_id=target, device_id_type=MESH)
            count += 1
    others = [(col ^ (1 << b)) * 2 + c for b in range(plan.bits)]
    for other in others:
        pl.semaphore_signal(barrier, inc=1, device_id=(other, z), device_id_type=MESH)
        count += 1
    pl.semaphore_wait(barrier, count)

    block_core = jnp.where(outer, 0, 1)
    slot_in = lax.div(z, 2)
    send_list = []
    for i in range(2):
        zt = jnp.where(c == 0, 3 * i, 1 + i)
        is_self = jnp.logical_and(c == block_core, zt == z)
        send_list.append((i, zt, is_self))

    def deliver(src, dst, send, recv):
        for i, zt, is_self in send_list:

            @pl.when(is_self)
            def _():
                pltpu.make_async_copy(src, dst.at[slot_in], recv.at[slot_in]).start()

            @pl.when(jnp.logical_not(is_self))
            def _():
                pltpu.make_async_remote_copy(
                    src_ref=src, dst_ref=dst.at[slot_in], send_sem=send.at[i], recv_sem=recv.at[slot_in],
                    device_id=(col * 2 + block_core, zt), device_id_type=MESH,
                ).start()

    def deliver_sent(src, dst, send, recv):
        for i, zt, is_self in send_list:

            @pl.when(jnp.logical_not(is_self))
            def _():
                pltpu.make_async_remote_copy(
                    src_ref=src, dst_ref=dst.at[slot_in], send_sem=send.at[i], recv_sem=recv.at[slot_in],
                    device_id=(col * 2 + block_core, zt), device_id_type=MESH,
                ).wait_send()

    def deliver_wait(src, dst, recv):
        for i in range(2):
            pltpu.make_async_copy(src, dst.at[i], recv.at[i]).wait()

    deliver(x_own, xin, in_send, in_recv)

    par_copy = pltpu.make_async_remote_copy(
        src_ref=par_ref, dst_ref=par_in, send_sem=par_sem.at[0], recv_sem=par_sem.at[1],
        device_id=peer, device_id_type=MESH,
    )
    par_copy.start()
    for cp in weight_copies[1:]:
        cp.start()
    par_copy.wait()
    served = jnp.where(parity == c, par_ref[...], par_in[...])
    tcount = par_ref[1:2, :] + par_in[1:2, :]
    total = jnp.broadcast_to(tcount, (8, 128))
    for b in range(plan.bits):
        tsend[b] = total
        cp = pltpu.make_async_remote_copy(
            src_ref=tsend.at[b], dst_ref=trecv.at[b], send_sem=t_sem.at[0, b], recv_sem=t_sem.at[1, b],
            device_id=(others[b], z), device_id_type=MESH,
        )
        cp.start()
        cp.wait()
        total = total + trecv[b]
    factor = served[1:2, :] / total[0:1, :]
    tot_o[0:1, :] = factor
    tot_o[1:8, :] = jnp.concatenate([served[0:1, :], served[2:8, :]], axis=0)
    passes = served[0:1, 0:1]

    fill_bias(bias, [served[2 + k : 3 + k, 0:1] for k in range(4)], c, tok)
    VAC[...] = jnp.zeros_like(VAC)
    for cp in sel_copies:
        cp.wait()

    deliver_wait(x_own, xin, in_recv)
    deliver_sent(x_own, xin, in_send, in_recv)
    XN[0:tok] = xin[0].astype(F32)
    XN[tok:T] = xin[1].astype(F32)
    deliver(cot_own, cot, cot_send, cot_recv)

    def stash_copies(s, slot, sem, back):
        pairs = ((X, sx_h), (Q, sq_h), (LSE, slse_h), (M, sm_h), (GP, sgp_h))
        out = []
        for i, (v, h) in enumerate(pairs):
            if back:
                out.append(pltpu.make_async_copy(h.at[s], v.at[slot], sem.at[slot, i]))
            else:
                out.append(pltpu.make_async_copy(v.at[slot], h.at[s], sem.at[slot, i]))
        return out

    def kv_stash(s, slot):
        return pltpu.make_async_copy(KV.at[slot], skv_h.at[s], st_sem.at[slot, 5])

    def kv_load(s, slot):
        return pltpu.make_async_copy(skv_h.at[s], KV.at[slot], ld_sem.at[slot, 5])

    def sel_copies_out(l, sect):
        at = pl.ds(pl.multiple_of(sect * T, T), T)
        return [
            pltpu.make_async_copy(asel, asel_h.at[l, :, at], sel_out.at[0]),
            pltpu.make_async_copy(osel, osel_h.at[l, :, at], sel_out.at[1]),
            pltpu.make_async_copy(usel, usel_h.at[l, :, at], sel_out.at[2]),
            pltpu.make_async_copy(gsel, gsel_h.at[l, :, at], sel_out.at[3]),
        ]

    def kv_copies(slot):
        out = []
        for i, off in enumerate((off_lo, off_hi)):
            ref = KV.at[slot, pl.ds(off, tok), :]
            out.append(
                pltpu.make_async_remote_copy(
                    src_ref=ref, dst_ref=ref, send_sem=kv_send.at[slot, i], recv_sem=kv_recv.at[slot, i],
                    device_id=peer, device_id_type=MESH,
                )
            )
        return out

    def kv_arrivals(slot):
        out = []
        for i, off in enumerate((poff_lo, poff_hi)):
            ref = KV.at[slot, pl.ds(off, tok), :]
            out.append(
                pltpu.make_async_remote_copy(
                    src_ref=ref, dst_ref=ref, send_sem=kv_send.at[slot, i], recv_sem=kv_recv.at[slot, i],
                    device_id=peer, device_id_type=MESH,
                )
            )
        return out

    def forward(s, carry):
        l = lax.rem(s, LAYERS)
        sect = lax.div(s, LAYERS)
        slot = lax.rem(s, 2)

        @pl.when(s >= 2)
        def _():
            for cp in stash_copies(s - 2, slot, st_sem, False):
                cp.wait()

        x = XN[...]
        X[slot] = x
        hat, _ = normalised(x)
        a = (hat * ln1g[pl.ds(l, 1), :] + ln1b[pl.ds(l, 1), :]).astype(BF16)

        @pl.when(s < 2)
        def _():
            pltpu.make_async_copy(wq_h.at[l], wq.at[l], w_sem.at[l, 0]).wait()

        kk = nn(a, wq[l, :, D : 2 * D]).astype(BF16)
        vv = (nn(a, wq[l, :, 2 * D : 3 * D]) + vb[pl.ds(l, 1), :]).astype(BF16)
        KV[slot, pl.ds(off_lo, tok), 0:D] = kk[:tok]
        KV[slot, pl.ds(off_lo, tok), D : 2 * D] = vv[:tok]
        KV[slot, pl.ds(off_hi, tok), 0:D] = kk[tok:]
        KV[slot, pl.ds(off_hi, tok), D : 2 * D] = vv[tok:]
        sends = kv_copies(slot)
        for cp in sends:
            cp.start()
        q = (nn(a, wq[l, :, 0:D]) + qb[pl.ds(l, 1), :]).astype(BF16)
        Q[slot] = q * jnp.asarray(0.125, BF16)

        @pl.when(s >= 1)
        def _():
            for cp in sel_copies_out(0, 0):
                cp.wait()

        asel[...] = nt(sel[0], a).astype(BF16)
        for cp in kv_arrivals(slot):
            cp.wait_recv()
        for cp in sends:
            cp.wait_send()

        @pl.when(s < STEPS - 2)
        def _():
            kv_stash(s, slot).start()

        attention_forward(KV.at[slot], Q.at[slot], LSE.at[slot], bias, O)

        @pl.when(s < 2)
        def _():
            pltpu.make_async_copy(wo_h.at[l], wo.at[l], w_sem.at[l, 1]).wait()

        o = O[...]
        osel[...] = nt(sel[0], o).astype(BF16)
        m = x + (nn(o, wo[l]) + ob[pl.ds(l, 1), :])
        M[slot] = m
        hat2, _ = normalised(m)
        a2 = (hat2 * ln2g[pl.ds(l, 1), :] + ln2b[pl.ds(l, 1), :]).astype(BF16)
        usel[...] = nt(sel[1], a2).astype(BF16)

        @pl.when(s < 2)
        def _():
            pltpu.make_async_copy(wu_h.at[l], wu.at[l], w_sem.at[l, 2]).wait()

        for j in range(FF // D):
            js = slice(j * D, (j + 1) * D)
            f = nn(a2, wu[l, :, js]) + ub[pl.ds(l, 1), js]
            f2 = f * f
            u = f * (0.7978845608028654 + 0.035677408136300125 * f2)
            t = jnp.tanh(u)
            h = 0.5 + 0.5 * t
            ga = f * h
            gp = h + ga * (1.0 - h) * (1.5957691216057308 + 0.21406444881780074 * f2)
            gb = ga.astype(BF16)
            GF[:, js] = gb
            GP[slot, :, js] = gp.astype(BF16)
            gs = nt(sel[2], gb).astype(BF16)
            n = plan.per * 2 * plan.cf
            m2 = sel.shape[1] // 2
            for cc in range(2):
                gsel[cc * plan.frows + j * n : cc * plan.frows + (j + 1) * n] = gs[cc * m2 : cc * m2 + n]

        @pl.when(s < 2)
        def _():
            pltpu.make_async_copy(wd_h.at[l], wd.at[l], w_sem.at[l, 3]).wait()

        y = m + (nn(GF[...], wd[l]) + db[pl.ds(l, 1), :])
        last = jnp.logical_and(l == 1, sect < MAXP)
        bar = jnp.where(last, sect, -1).astype(F32)
        XN[...] = jnp.where(passes > bar, y, X[0])

        @pl.when(s < STEPS - 2)
        def _():
            for cp in stash_copies(s, slot, st_sem, False):
                cp.start()
            kv_stash(s, slot).wait()

        for cp in sel_copies_out(l, sect):
            cp.start()
        return carry

    lax.fori_loop(0, STEPS, forward, 0)

    block = jnp.where(z < 2, c, 3 - c)
    owner = (col * 2 + parity, block)
    mine = jnp.logical_and(parity == c, block == z)

    ret_recv_wait = pltpu.make_async_copy(ret_s, ret_r, ret_recv.at[0])
    ret_remote = pltpu.make_async_remote_copy(
        src_ref=ret_s, dst_ref=ret_r, send_sem=ret_send.at[0], recv_sem=ret_recv.at[0],
        device_id=owner, device_id_type=MESH,
    )

    @pl.when(z < 2)
    def _():
        ret_s[...] = XN[0:tok]

    @pl.when(z >= 2)
    def _():
        ret_s[...] = XN[tok:T]

    @pl.when(mine)
    def _():
        ret_recv_wait.start()

    @pl.when(jnp.logical_not(mine))
    def _():
        ret_remote.start()

    deliver_wait(cot_own, cot, cot_recv)
    deliver_sent(cot_own, cot, cot_send, cot_recv)
    U[0:tok] = cot[0]
    U[tok:T] = cot[1]
    for cp in sel_copies_out(0, 0):
        cp.wait()

    def back_copies(l, sect):
        at = pl.ds(pl.multiple_of(sect * T, T), T)
        return [
            pltpu.make_async_copy(DP, dp_h.at[l, at, :], bst_sem.at[0]),
            pltpu.make_async_copy(DY, dy_h.at[l, at, :], bst_sem.at[1]),
            pltpu.make_async_copy(GF, df_h.at[l, at, :], bst_sem.at[2]),
            pltpu.make_async_copy(DR, dr_h.at[l, at, :], bst_sem.at[3]),
        ]

    def dkv_copies(par):
        out = []
        for i, off in enumerate((poff_lo, poff_hi)):
            out.append(
                pltpu.make_async_remote_copy(
                    src_ref=DKV.at[pl.ds(off, tok), :], dst_ref=RDKV.at[par, i],
                    send_sem=dkv_send.at[par, i], recv_sem=dkv_recv.at[par, i],
                    device_id=peer, device_id_type=MESH,
                )
            )
        return out

    def backward(i, carry):
        s = STEPS - 1 - i
        l = lax.rem(s, LAYERS)
        sect = lax.div(s, LAYERS)
        slot = lax.rem(s, 2)

        @pl.when(i >= 1)
        def _():
            for cp in back_copies(0, 0):
                cp.wait()

        @pl.when(i >= 2)
        def _():
            for cp in stash_copies(s, slot, ld_sem, True):
                cp.wait()
            kv_load(s, slot).wait()

        active = jnp.where(
            passes > jnp.where(sect == MAXP, -1, sect).astype(F32), jnp.ones((1, 1), F32), jnp.zeros((1, 1), F32)
        )

        @pl.when(l == 1)
        def _():
            R[...] = U[...] * active

        r = R[...]
        dr = r.astype(BF16)
        DR[...] = dr
        VAC[l, 7:8] += column_sum(dr.astype(F32))
        for j in range(FF // D):
            js = slice(j * D, (j + 1) * D)
            dg = nt(dr, wd[l, js, :])
            df = (dg * GP[slot, :, js].astype(F32)).astype(BF16)
            GF[:, js] = df
            VAC[l, 8 + j : 9 + j] += column_sum(df.astype(F32))
        da2 = nt(GF[...], wu[l])
        hat2, inv2 = normalised(M[slot])
        VAC[l, 5:6] += column_sum(da2 * hat2)
        VAC[l, 6:7] += column_sum(da2)
        dm = r + norm_back(da2, ln2g[pl.ds(l, 1), :], hat2, inv2)
        R[...] = dm
        dy = dm.astype(BF16)
        DY[...] = dy
        VAC[l, 4:5] += column_sum(dy.astype(F32))
        O[...] = nt(dy, wo[l]).astype(BF16)

        attention_backward(KV.at[slot], Q.at[slot], LSE.at[slot], bias, O, DP, DKV, {})
        sends = dkv_copies(slot)
        for cp in sends:
            cp.start()

        x = X[slot]
        hat, inv = normalised(x)

        @pl.when(s >= 2 + LAYERS)
        def _():
            for cp in stash_copies(s - 2, slot, ld_sem, True):
                cp.start()
            kv_load(s - 2, slot).start()

        dqb = DP[:, 0:D]
        VAC[l, 2:3] += column_sum(dqb.astype(F32))
        da = nt(dqb, wq[l, :, 0:D])
        for cp in sends:
            cp.wait_recv()
        for j in range(2):
            off = off_lo if j == 0 else off_hi
            dkv = (DKV[pl.ds(off, tok), :].astype(F32) + RDKV[slot, j].astype(F32)).astype(BF16)
            DP[j * tok : (j + 1) * tok, D : 3 * D] = dkv
        for cp in sends:
            cp.wait_send()
        dkv = DP[:, D : 3 * D]
        VAC[l, 3:4] += column_sum(dkv[:, D:].astype(F32))
        da = da + nt(dkv, wq[l, :, D : 3 * D])
        VAC[l, 0:1] += column_sum(da * hat)
        VAC[l, 1:2] += column_sum(da)
        R[...] = R[...] + norm_back(da, ln1g[pl.ds(l, 1), :], hat, inv)

        @pl.when(l == 0)
        def _():
            U[...] = R[...] + (1.0 - active) * U[...]

        for cp in back_copies(l, sect):
            cp.start()
        return carry

    lax.fori_loop(0, STEPS - LAYERS, backward, 0)
    ret_recv_wait.wait()

    @pl.when(jnp.logical_not(mine))
    def _():
        ret_remote.wait_send()

    hid_o[...] = ret_r[...]
    up_o[...] = U[...]
    vec_o[...] = VAC[...]
    for cp in back_copies(0, 0):
        cp.wait()


def run_main(plan, x, cot, numbers, vecs, sel, weights):
    tok = plan.tok
    T = 2 * tok
    L = 4 * tok
    vmem = pl.BlockSpec(memory_space=pltpu.VMEM)
    hbm = pl.BlockSpec(memory_space=pl.ANY)
    smem = pl.BlockSpec(memory_space=pltpu.SMEM)
    S = jax.ShapeDtypeStruct
    K = (MAXP + 1) * T
    outs = [
        (S((tok, D), F32), vmem),
        (S((T, D), F32), vmem),
        (S((LAYERS, 16, D), F32), vmem),
        (S((8, 128), F32), vmem),
        (S((LAYERS, plan.nsel, K), BF16), hbm),
        (S((LAYERS, plan.nsel, K), BF16), hbm),
        (S((LAYERS, plan.nsel, K), BF16), hbm),
        (S((LAYERS, 2 * plan.frows, K), BF16), hbm),
        (S((LAYERS, K, 3 * D), BF16), hbm),
        (S((LAYERS, K, D), BF16), hbm),
        (S((LAYERS, K, FF), BF16), hbm),
        (S((LAYERS, K, D), BF16), hbm),
        (S((STEPS, T, D), F32), hbm),
        (S((STEPS, T, D), BF16), hbm),
        (S((STEPS, L, 2 * D), BF16), hbm),
        (S((STEPS, 8, 8, T), F32), hbm),
        (S((STEPS, T, D), F32), hbm),
        (S((STEPS, T, FF), BF16), hbm),
    ]
    V = pltpu.VMEM
    DMA = pltpu.SemaphoreType.DMA
    nb = max(plan.bits, 1)
    scratch = [
        V((LAYERS, D, 3 * D), BF16), V((LAYERS, D, D), BF16), V((LAYERS, D, FF), BF16), V((LAYERS, FF, D), BF16),
        V((3, sel.shape[2], D), BF16), V((2, tok, D), BF16), V((2, tok, D), F32), V((8, 128), F32), V((8, 128), F32),
        V((nb, 8, 128), F32), V((nb, 8, 128), F32),
        V((L, T), F32),
        V((2, T, D), F32), V((2, T, D), BF16), V((2, L, 2 * D), BF16), V((2, 8, 8, T), F32), V((2, T, D), F32),
        V((2, T, FF), BF16), V((T, D), BF16), V((T, FF), BF16), V((T, D), F32),
        V((plan.nsel, T), BF16), V((plan.nsel, T), BF16), V((plan.nsel, T), BF16), V((2 * plan.frows, T), BF16),
        V((T, D), F32), V((T, D), F32), V((L, 2 * D), BF16), V((2, 2, tok, 2 * D), BF16), V((T, 3 * D), BF16),
        V((T, D), BF16), V((T, D), BF16), V((LAYERS, 16, D), F32), V((tok, D), F32), V((tok, D), F32),
        DMA((LAYERS, 4)), DMA((3, 2)), DMA((2,)), DMA((2,)), DMA((2,)), DMA((2,)), DMA((2,)), DMA((2, nb)),
        DMA((2, 2)), DMA((2, 2)), DMA((2, 6)), DMA((2, 6)), DMA((4,)), DMA((2, 2)), DMA((2, 2)), DMA((4,)),
        DMA((1,)), DMA((1,)),
    ]
    call = pl.pallas_call(
        functools.partial(main_kernel, plan),
        out_shape=[o[0] for o in outs],
        out_specs=[o[1] for o in outs],
        in_specs=[vmem] * 2 + [smem] * 3 + [vmem] * 9 + [hbm] * 5,
        scratch_shapes=scratch,
        compiler_params=pltpu.CompilerParams(
            collective_id=0, has_side_effects=True, vmem_limit_bytes=VMEM_LIMIT
        ),
        name="layers",
    )
    return call(x, cot, *numbers, *vecs, sel, *weights)


def fold(x):
    n = x.shape[1] // 2
    return jnp.concatenate([x[:, :n], x[:, n:]], axis=0)


def unfold(x):
    n = x.shape[0] // 2
    return jnp.concatenate([x[:n], x[n:]], axis=1)


class Item:
    def __init__(self, name, rows, cols, order):
        self.name, self.rows, self.cols, self.order = name, rows, cols, order


def items_of(plan):
    return [
        Item("down", plan.frows, D, plan.order_down),
        Item("up", plan.rows, FF, plan.order_up),
        Item("out", plan.rows, D, plan.order_qkv),
        Item("qkv", plan.rows, 3 * D, plan.order_qkv),
    ]


def last_kernel(
    plan,
    up_h, vec_ref, tot_ref, ln1g, ln2g, asel_h, osel_h, usel_h, gsel_h, dp_h, dy_h, df_h, dr_h,
    sx_h, sq_h, skv_h, slse_h, sm_h, sgp_h, wq_h, wo_h, wu_h, wd_h,
    *refs,
):
    items = items_of(plan)
    n = len(items)
    outs, gin_o, vec_o, refs = refs[:n], refs[n], refs[n + 1], refs[n + 2 :]
    lhs, rhs, refs = refs[:n], refs[n : 2 * n], refs[2 * n :]
    OW, CR, refs = refs[:n], refs[n : 2 * n], refs[2 * n :]
    stages = plan.bits + 1
    RB = []
    for k in range(stages - 1):
        RB.append(refs[:n])
        refs = refs[n:]
    FS, FR, refs = refs[:n], refs[n : 2 * n], refs[2 * n :]
    (
        ST, wq, wo, wu, wd, Q, KV, LSE, XM, GP, bias, R, DKV, RDKV, ret_r, vs, vr,
        l_sem, w_sem, s_sem, chip_sem, stage_sem, vec_sem, dkv_sem, ret_sem, up_sem,
    ) = refs
    tok = plan.tok
    T = 2 * tok
    g, z, c, col, outer, parity = where_am_i()
    peer = (col * 2 + 1 - c, z)
    off = [pl.multiple_of(c * tok, tok), pl.multiple_of((3 - c) * tok, tok)]
    poff = [pl.multiple_of((1 - c) * tok, tok), pl.multiple_of((2 + c) * tok, tok)]
    DOWN, UP, OUT, QKV = range(n)
    sources = ((gsel_h, dr_h), (usel_h, df_h), (osel_h, dy_h), (asel_h, dp_h))
    DR, GF, DY, DP = [r.at[0:T] for r in rhs]
    DO = DY
    blocks = FF // D
    rows4 = items[DOWN].rows // blocks
    staged = [ST.at[0:rows4, :], ST, ST.at[:, 3 * D :], ST.at[:, : 3 * D]]

    def operand_loads(l, i):
        a, b = sources[i]
        later = pl.ds(T, rhs[i].shape[0] - T)
        return (
            pltpu.make_async_copy(a.at[l], lhs[i], l_sem.at[i, 0]),
            pltpu.make_async_copy(b.at[l, later, :], rhs[i].at[later, :], l_sem.at[i, 1]),
        )

    weight_refs = {"wd": (wd_h, wd, 0), "wu": (wu_h, wu, 1), "wo": (wo_h, wo, 2), "wq": (wq_h, wq, 3)}
    slot_refs = {
        "GP": (sgp_h, GP, 0), "M": (sm_h, XM, 1), "Q": (sq_h, Q, 2), "KV": (skv_h, KV, 3), "LSE": (slse_h, LSE, 4),
        "X": (sx_h, XM, 5),
    }

    def load(l, *names):
        out = []
        for name in names:
            if name in weight_refs:
                h, v, k = weight_refs[name]
                out.append(pltpu.make_async_copy(h.at[l], v, w_sem.at[k]))
            else:
                h, v, k = slot_refs[name]
                out.append(pltpu.make_async_copy(h.at[l], v, s_sem.at[k]))
        return out

    def start(copies):
        for cp in copies:
            cp.start()

    def wait(copies):
        for cp in copies:
            cp.wait()

    top_layer = LAYERS - 1
    up_load = pltpu.make_async_copy(up_h, R, up_sem.at[0])
    up_load.start()
    start(operand_loads(top_layer, DOWN))
    start(load(top_layer, "wd", "GP"))
    start(operand_loads(top_layer, UP))
    start(load(top_layer, "wu", "M"))
    start(operand_loads(top_layer, OUT))
    start(load(top_layer, "wo", "Q", "KV", "LSE", "wq"))
    start(operand_loads(top_layer, QKV))

    def partner(dim):
        if dim < 0:
            return (g, z + 1 - 2 * lax.rem(z, 2))
        return ((col ^ (1 << dim)) * 2 + c, z)

    def bit_of(dim):
        if dim < 0:
            return lax.rem(z, 2)
        return lax.rem(lax.div(col, 1 << dim), 2)

    dims = [-1] + list(range(plan.bits))
    block = jnp.where(z < 2, c, 3 - c)
    owner = (col * 2 + parity, block)
    mine = jnp.logical_and(parity == c, block == z)
    barrier = pltpu.get_barrier_semaphore()
    count = 0
    for dc in range(2):
        for dz in range(plan.nrow):
            if dc == 0 and dz == 0:
                continue
            target = (col * 2 + lax.rem(c + dc, 2), lax.rem(z + dz, plan.nrow))
            pl.semaphore_signal(barrier, inc=1, device_id=target, device_id_type=MESH)
            count += 1
    for dim in dims[1:]:
        pl.semaphore_signal(barrier, inc=1, device_id=partner(dim), device_id_type=MESH)
        count += 1
    pl.semaphore_wait(barrier, count)

    factor = tot_ref[0:1, 0:1]
    active = jnp.where(tot_ref[1:2, 0:1] > 0.0, jnp.ones((1, 1), F32), jnp.zeros((1, 1), F32))
    fill_bias(bias, [tot_ref[2 + k : 3 + k, 0:1] for k in range(4)], c, tok)

    def chip_copy(l, i):
        return pltpu.make_async_remote_copy(
            src_ref=staged[i], dst_ref=CR[i], send_sem=chip_sem.at[0, i], recv_sem=chip_sem.at[1, i],
            device_id=peer, device_id_type=MESH,
        )

    def base_of(i, k):
        base, rows = 0, items[i].rows
        for j in range(k):
            rows //= 2
            base = base + bit_of(items[i].order[j]) * rows
        return base, rows

    def stage_copy(l, i, k):
        item = items[i]
        if k == stages - 1:
            src, dst = FS[i], FR[i].at[l]
        else:
            base, rows = base_of(i, k)
            rows //= 2
            first = base + (1 - bit_of(item.order[k])) * rows
            src, dst = OW[i].at[l, pl.ds(pl.multiple_of(first, 16), rows), :], RB[k][i].at[l]
        return pltpu.make_async_remote_copy(
            src_ref=src, dst_ref=dst, send_sem=stage_sem.at[0, l, i, k], recv_sem=stage_sem.at[1, l, i, k],
            device_id=partner(item.order[k]), device_id_type=MESH,
        )

    def product(l, i):
        wait(operand_loads(l, i))
        item = items[i]
        step = D if item.rows < D else D // 3
        for j in range(item.cols // step):
            js = slice(j * step, (j + 1) * step)
            r = (nn(lhs[i][...], rhs[i][:, js]) * factor).astype(BF16)
            OW[i][l, :, js] = r[: item.rows]
            if i == DOWN:
                for b in range(blocks):
                    at = slice(b * D + js.start, b * D + js.stop)
                    staged[i][:, at] = r[item.rows + b * rows4 : item.rows + (b + 1) * rows4]
            else:
                staged[i][:, js] = r[item.rows :]
        if l > 0:
            start(operand_loads(l - 1, i))
        chip_copy(l, i).start()

    def after_chip(l, i):
        chip_copy(l, i).wait()
        if i == DOWN:
            for b in range(blocks):
                at = slice(b * rows4, (b + 1) * rows4)
                add = CR[i][:, b * D : (b + 1) * D].astype(F32)
                OW[i][l, at, :] = (OW[i][l, at, :].astype(F32) + add).astype(BF16)
        else:
            OW[i][l] = (OW[i][l].astype(F32) + CR[i][...].astype(F32)).astype(BF16)
        stage_copy(l, i, 0).start()

    def after_stage(l, i, k):
        item = items[i]
        stage_copy(l, i, k).wait()
        if k == stages - 1:
            outs[i][l] += unfold(FR[i][l].astype(F32))[: outs[i].shape[1]]
            return
        base, rows = base_of(i, k + 1)
        at = pl.ds(pl.multiple_of(base, 16), rows)
        both = OW[i][l, at, :].astype(F32) + RB[k][i][l].astype(F32)
        if k + 1 == stages - 1:
            rows //= 2
            first = bit_of(item.order[k + 1]) == 0
            outs[i][l] = jnp.where(first, both[:rows], both[rows:])[: outs[i].shape[1]]
            FS[i][...] = fold(jnp.where(first, both[rows:], both[:rows])).astype(BF16)
        else:
            OW[i][l, at, :] = both.astype(BF16)
        stage_copy(l, i, k + 1).start()

    def dkv_copies():
        return [
            pltpu.make_async_remote_copy(
                src_ref=DKV.at[pl.ds(poff[j], tok), :], dst_ref=RDKV.at[j],
                send_sem=dkv_sem.at[0, j], recv_sem=dkv_sem.at[1, j], device_id=peer, device_id_type=MESH,
            )
            for j in range(2)
        ]

    vec_o[...] = vec_ref[...]

    def backward(l, marks):
        def mark(name):
            for f in marks.get(name, ()):
                f()

        def reload(*names):
            if l > 0:
                start(load(l - 1, *names))

        r = R[...]
        dr = r.astype(BF16)
        DR[...] = dr
        vec_o[l, 7:8] += column_sum(dr.astype(F32))
        product(l, DOWN)
        mark("down")
        wait(load(l, "wd", "GP"))
        for j in range(FF // D):
            js = slice(j * D, (j + 1) * D)
            dg = nt(dr, wd[js, :])
            df = (dg * GP[:, js].astype(F32)).astype(BF16)
            GF[:, js] = df
            vec_o[l, 8 + j : 9 + j] += column_sum(df.astype(F32))
        reload("wd", "GP")
        mark("df")
        product(l, UP)
        mark("up")
        wait(load(l, "wu", "M"))
        da2 = nt(GF[...], wu[...])
        hat2, inv2 = normalised(XM[...])
        vec_o[l, 5:6] += column_sum(da2 * hat2)
        vec_o[l, 6:7] += column_sum(da2)
        dm = r + norm_back(da2, ln2g[l : l + 1, :], hat2, inv2)
        R[...] = dm
        dy = dm.astype(BF16)
        DY[...] = dy
        vec_o[l, 4:5] += column_sum(dy.astype(F32))
        start(load(l, "X"))
        reload("wu")
        mark("dy")
        product(l, OUT)
        wait(load(l, "wo", "Q", "KV", "LSE"))
        DO[...] = nt(dy, wo[...]).astype(BF16)
        reload("wo")
        attention_backward(
            KV, Q, LSE, bias, DO, DP, DKV, {HEADS // 2 - 1: lambda: mark("half")}
        )
        sends = dkv_copies()
        start(sends)
        reload("Q", "KV", "LSE")
        mark("attention")
        wait(load(l, "X", "wq"))
        hat, inv = normalised(XM[...])
        if l == 0:
            up_again.start()
        else:
            reload("M")
        dqb = DP[:, 0:D]
        vec_o[l, 2:3] += column_sum(dqb.astype(F32))
        da = nt(dqb, wq[:, 0:D])
        for cp in sends:
            cp.wait_recv()
        for j in range(2):
            dkv = (DKV[pl.ds(off[j], tok), :].astype(F32) + RDKV[j].astype(F32)).astype(BF16)
            DP[j * tok : (j + 1) * tok, D : 3 * D] = dkv
        for cp in sends:
            cp.wait_send()
        product(l, QKV)
        mark("qkv")
        dkv = DP[:, D : 3 * D]
        vec_o[l, 3:4] += column_sum(dkv[:, D:].astype(F32))
        da = da + nt(dkv, wq[:, D : 3 * D])
        reload("wq")
        vec_o[l, 0:1] += column_sum(da * hat)
        vec_o[l, 1:2] += column_sum(da)
        new = R[...] + norm_back(da, ln1g[l : l + 1, :], hat, inv)
        if l == 0:
            up_again.wait()
            new = (new + (1.0 - active) * XM[...]) * factor
        R[...] = new
        mark("end")

    up_again = pltpu.make_async_copy(up_h, XM, up_sem.at[0])

    def chip(l, i):
        return lambda: after_chip(l, i)

    def stage(l, i, k):
        return lambda: after_stage(l, i, k)

    up_load.wait()
    R[...] = R[...] * active
    late = stages - 1
    backward(1, {
        "df": [chip(1, DOWN)],
        "dy": [chip(1, UP)],
        "half": [chip(1, OUT)],
        "end": [chip(1, QKV), stage(1, OUT, 0)],
    })
    backward(0, {
        "df": [chip(0, DOWN), stage(1, DOWN, 0)],
        "up": [stage(1, UP, 0)],
        "dy": [chip(0, UP), stage(1, OUT, 1)],
        "half": [chip(0, OUT), stage(1, DOWN, 1)],
        "attention": [stage(1, QKV, 0), stage(1, UP, 1)],
    })

    home = R.at[pl.ds(pl.multiple_of(jnp.where(z < 2, 0, tok), tok), tok), :]
    ret_local = pltpu.make_async_copy(home, ret_r, ret_sem.at[1])
    ret_remote = pltpu.make_async_remote_copy(
        src_ref=home, dst_ref=ret_r, send_sem=ret_sem.at[0], recv_sem=ret_sem.at[1],
        device_id=owner, device_id_type=MESH,
    )

    @pl.when(mine)
    def _():
        ret_local.start()

    @pl.when(jnp.logical_not(mine))
    def _():
        ret_remote.start()

    vec_targets = [peer] + [partner(dim) for dim in dims]

    def vec_copy(k):
        return pltpu.make_async_remote_copy(
            src_ref=vs, dst_ref=vr.at[k], send_sem=vec_sem.at[0, k], recv_sem=vec_sem.at[1, k],
            device_id=vec_targets[k], device_id_type=MESH,
        )

    def vec_step(k):
        vec_copy(k).wait()
        if k + 1 < len(vec_targets):
            vs[...] = vs[...] + vr[k]
            vec_copy(k + 1).start()
        else:
            vec_o[...] = vs[...] + vr[k]

    after_chip(0, QKV)
    vs[...] = vec_o[...] * factor
    vec_copy(0).start()
    done = {(1, DOWN): 2, (1, UP): 2, (1, OUT): 2, (1, QKV): 1}
    vec_at = 0
    for k in range(stages):
        for l, i in [(1, DOWN), (1, UP), (1, OUT), (1, QKV), (0, OUT), (0, DOWN), (0, UP), (0, QKV)]:
            step = k + done.get((l, i), 0)
            if step < stages:
                after_stage(l, i, step)
            if vec_at < len(vec_targets) and i == OUT:
                vec_step(vec_at)
                vec_at += 1
    for k in range(vec_at, len(vec_targets)):
        vec_step(k)
    ret_local.wait()

    @pl.when(jnp.logical_not(mine))
    def _():
        ret_remote.wait_send()

    gin_o[...] = ret_r[...]


def run_last(plan, upstream, vec, tot, gains, stashes, weights):
    tok = plan.tok
    T = 2 * tok
    vmem = pl.BlockSpec(memory_space=pltpu.VMEM)
    hbm = pl.BlockSpec(memory_space=pl.ANY)
    S = jax.ShapeDtypeStruct
    V = pltpu.VMEM
    DMA = pltpu.SemaphoreType.DMA
    items = items_of(plan)
    n = len(items)
    stages = plan.bits + 1
    own = {"down": plan.cf, "up": plan.ch, "out": plan.ch, "qkv": plan.ch}
    outs = [S((LAYERS, own[i.name], i.cols), F32) for i in items] + [S((tok, D), F32), S(vec.shape, F32)]
    K = stashes[0].shape[2]
    scratch = [V((2 * i.rows, K), BF16) for i in items]
    scratch += [V((K, i.cols), BF16) for i in items]
    scratch += [V((LAYERS, i.rows, i.cols), BF16) for i in items]
    scratch += [
        V((i.rows * i.cols // FF, FF) if i.name == "down" else (i.rows, i.cols), BF16) for i in items
    ]
    for k in range(stages - 1):
        scratch += [V((LAYERS, i.rows >> (k + 1), i.cols), BF16) for i in items]
    last = [i.rows >> stages for i in items]
    scratch += [V((2 * r, i.cols // 2), BF16) for r, i in zip(last, items)]
    scratch += [V((LAYERS, 2 * r, i.cols // 2), BF16) for r, i in zip(last, items)]
    nv = 2 + plan.bits
    scratch += [
        V((plan.rows, FF), BF16),
        V((D, 3 * D), BF16), V((D, D), BF16), V((D, FF), BF16), V((FF, D), BF16),
        V((T, D), BF16), V((2 * T, 2 * D), BF16), V((8, 8, T), F32), V((T, D), F32), V((T, FF), BF16),
        V((2 * T, T), F32), V((T, D), F32), V((2 * T, 2 * D), BF16), V((2, tok, 2 * D), BF16),
        V((tok, D), F32), V(vec.shape, F32), V((nv,) + vec.shape, F32),
        DMA((n, 2)), DMA((4,)), DMA((6,)), DMA((2, n)), DMA((2, LAYERS, n, stages)), DMA((2, nv)), DMA((2, 2)),
        DMA((2,)), DMA((1,)),
    ]
    call = pl.pallas_call(
        functools.partial(last_kernel, plan),
        out_shape=outs,
        out_specs=[vmem] * len(outs),
        in_specs=[hbm] + [vmem] * 4 + [hbm] * (len(stashes) + 4),
        scratch_shapes=scratch,
        compiler_params=pltpu.CompilerParams(
            collective_id=1, has_side_effects=True, vmem_limit_bytes=VMEM_LIMIT
        ),
        name="last",
    )
    return call(upstream, vec, tot, *gains, *stashes, *weights)


def finish_kernel(plan, vec_ref, *refs):
    big = refs[:6]
    big_o, small_o = refs[6:12], refs[12:21]
    for a, b in zip(big, big_o):
        b[...] = a[...]
    me = lax.axis_index("grp") * plan.nrow + lax.axis_index("row")
    feature = lax.broadcasted_iota(jnp.int32, (D, 128), 0)
    place = lax.broadcasted_iota(jnp.int32, (D, 128), 1)

    def picked(rows, first, n):
        one_hot = jnp.where((feature == first + place) & (place < n), 1.0, 0.0)
        return jnp.dot(rows, one_hot, preferred_element_type=F32, precision=lax.Precision.HIGHEST)

    per = D // plan.cf
    for l in range(LAYERS):
        rows = picked(vec_ref[l], me * plan.ch, plan.ch)
        for i in range(8):
            small_o[i][l : l + 1, :] = rows[i : i + 1, : plan.ch]
        wide = picked(vec_ref[l], lax.rem(me, per) * plan.cf, plan.cf)
        which = lax.broadcasted_iota(jnp.int32, (16, 128), 0) == 8 + lax.div(me, per)
        line = jnp.sum(jnp.where(which, wide, 0.0), axis=0, keepdims=True)
        small_o[8][l : l + 1, :] = line[:, : plan.cf]


def run_finish(plan, vec, big):
    vmem = pl.BlockSpec(memory_space=pltpu.VMEM)
    S = jax.ShapeDtypeStruct
    outs = [S(a.shape, a.dtype) for a in big]
    outs += [S((LAYERS, plan.ch), F32)] * 8 + [S((LAYERS, plan.cf), F32)]
    return pl.pallas_call(
        functools.partial(finish_kernel, plan),
        out_shape=outs,
        in_specs=[vmem] * 7,
        out_specs=[vmem] * 15,
        name="finish",
    )(vec, *big)


def body(
    plan,
    inputs, cotangent, pass_counts, doc_starts, token_counts,
    ln1_gain, ln1_bias, qkv_weight, query_bias, value_bias, out_weight, out_bias,
    ln2_gain, ln2_bias, up_weight, up_bias, down_weight, down_bias,
):
    tables = [plan.selector(plan.order_qkv), plan.selector(plan.order_up), plan.selector_ff()]
    sel = jnp.asarray(np.stack(tables).astype(jnp.bfloat16))
    vecs = (ln1_gain, ln1_bias, query_bias, value_bias, out_bias, ln2_gain, ln2_bias, up_bias, down_bias)
    weights = (qkv_weight, out_weight, up_weight, down_weight)
    hidden, upstream, vec, tot, *rest = run_main(
        plan, inputs, cotangent, (pass_counts, doc_starts, token_counts), vecs, sel, weights
    )
    g_down, g_up, g_out, g_qkv, grad_in, vec = run_last(
        plan, upstream, vec, tot, (ln1_gain, ln2_gain), rest, weights
    )
    big = (hidden, grad_in, g_qkv, g_out, g_up, g_down)
    hidden, grad_in, g_qkv, g_out, g_up, g_down, *v = run_finish(plan, vec, big)
    return (
        hidden, grad_in, v[0], v[1], g_qkv, v[2], v[3], g_out, v[4], v[5], v[6], g_up, v[8], g_down, v[7],
    )


def solution(mesh):
    ngrp, nrow = mesh.shape["grp"], mesh.shape["row"]
    whole = P(("grp", "row"), None)
    vector = P(None, ("grp", "row"))
    matrix = P(None, ("grp", "row"), None)

    def run(*args):
        return body(Plan(ngrp, nrow, args[0].shape[0]), *args)

    return jax.shard_map(
        run,
        mesh=mesh,
        in_specs=(whole, whole, P("grp"), P("grp", None), P("grp")) + (P(),) * 13,
        out_specs=(
            whole, whole, vector, vector, matrix, vector, vector, matrix, vector, vector, vector,
            matrix, vector, matrix, vector,
        ),
        check_vma=False,
    )
```

```python
import functools

import jax
import jax.numpy as jnp
import numpy as np
from jax import lax
from jax.experimental import pallas as pl
from jax.experimental.pallas import tpu as pltpu
from jax.sharding import PartitionSpec as P

HEADS = 12
HEAD = 64
D = 768
FF = 3072
LAYERS = 2
MAXP = 2
STEPS = LAYERS * (MAXP + 1)
SMALL = 12

EPS = 1e-05
NEG = -1000000000.0
LOG2E = 1.4426950408889634
MESH = pl.DeviceIdType.MESH
VMEM_LIMIT = 63 * 2**20
F32 = jnp.float32
BF16 = jnp.bfloat16


def nn(a, b):
    return jnp.dot(a, b, preferred_element_type=F32)


def nt(a, b):
    return lax.dot_general(a, b, (((1,), (1,)), ((), ())), preferred_element_type=F32)


def tn(a, b):
    return lax.dot_general(a, b, (((0,), (0,)), ((), ())), preferred_element_type=F32)


def normalised(x):
    mean = jnp.mean(x, axis=-1, keepdims=True)
    centred = x - mean
    spread = jnp.mean(centred * centred, axis=-1, keepdims=True)
    inv = lax.rsqrt(spread + EPS)
    return centred * inv, inv


def norm_back(grad, gain, hat, inv):
    g = grad * gain
    mean_g = jnp.mean(g, axis=-1, keepdims=True)
    mean_gh = jnp.mean(g * hat, axis=-1, keepdims=True)
    return inv * (g - mean_g - hat * mean_gh)


def column_sum(x):
    return jnp.sum(x, axis=0, keepdims=True)


def of_head(h):
    p = h // 2
    at, atv = slice(p * 128, (p + 1) * 128), slice(D + p * 128, D + (p + 1) * 128)
    low = lax.broadcasted_iota(jnp.int32, (1, 128), 1) < HEAD
    return at, atv, low if h % 2 == 0 else jnp.logical_not(low)


def attention_forward(KV, Q, LSE, bias, O, before_values):
    def scores(h):
        at, _, keep = of_head(h)
        qp = Q[:, at]
        return nt(KV[:, at], jnp.where(keep, qp, jnp.zeros_like(qp)))

    def mixed(h, raw):
        _, atv, _ = of_head(h)
        logits = raw * LOG2E + bias[...]
        top = jnp.max(logits, axis=0, keepdims=True)
        expo = jnp.exp2(logits - top)
        denom = jnp.sum(expo, axis=0, keepdims=True)
        LSE[h // 2, h % 2 : h % 2 + 1, :] = top + jnp.log2(denom)
        return tn((expo * (1.0 / denom)).astype(BF16), KV[:, atv])

    ahead = scores(0)
    before_values()
    even = None
    for h in range(HEADS):
        raw = ahead
        if h + 1 < HEADS:
            ahead = scores(h + 1)
        out = mixed(h, raw)
        if h % 2 == 0:
            even = out
        else:
            at, _, high = of_head(h)
            O[:, at] = jnp.where(high, out, even).astype(BF16)


def attention_backward(KV, Q, LSE, bias, DO, DP, DKV, between):
    low_row = lax.broadcasted_iota(jnp.int32, (128, 1), 0) < HEAD

    def parts(h):
        at, atv, keep = of_head(h)
        qp, dop = Q[:, at], DO[:, at]
        zero = jnp.zeros_like(qp)
        return KV[:, at], KV[:, atv], jnp.where(keep, qp, zero), jnp.where(keep, dop, zero)

    def products(h):
        kp, vp, qe, doe = parts(h)
        return nt(kp, qe), nt(vp, doe)

    def grads(h, raw, dpr):
        lse = LSE[h // 2, h % 2 : h % 2 + 1, :]
        pr = jnp.exp2(raw * LOG2E + bias[...] - lse)
        inner = jnp.sum(pr * dpr, axis=0, keepdims=True)
        return pr.astype(BF16), (pr * (dpr - inner)).astype(BF16)

    def finish(h0, one, two):
        at, atv, _ = of_head(h0)
        kp, _, q0, do0 = parts(h0)
        _, _, q1, do1 = parts(h0 + 1)
        dqt = jnp.where(low_row, tn(kp, one[1]), tn(kp, two[1])) * 0.125
        DP[:, at] = dqt.T.astype(BF16)
        p = h0 // 2
        DKV[:, (2 * p + 1) * 128 : (2 * p + 2) * 128] = nn(
            jnp.concatenate([one[0], two[0]], axis=1), jnp.concatenate([do0, do1], axis=0)
        ).astype(BF16)
        DKV[:, 2 * p * 128 : (2 * p + 1) * 128] = nn(
            jnp.concatenate([one[1], two[1]], axis=1), jnp.concatenate([q0, q1], axis=0)
        ).astype(BF16)

    ahead = products(0)
    even = None
    for h in range(HEADS):
        now = ahead
        if h + 1 < HEADS:
            ahead = products(h + 1)
        pair = grads(h, *now)
        if h % 2 == 0:
            even = pair
        else:
            finish(h - 1, even, pair)
        if h in between:
            between[h]()


def merge_kv(DP, DKV, RDKV, off, half):
    tok = RDKV.shape[1]
    for j in range(2):
        for p in range(half * HEADS // 4, (half + 1) * HEADS // 4):
            at = slice(2 * p * 128, (2 * p + 2) * 128)
            both = (DKV[pl.ds(off[j], tok), at].astype(F32) + RDKV[j, :, at].astype(F32)).astype(BF16)
            DP[j * tok : (j + 1) * tok, D + p * 128 : D + (p + 1) * 128] = both[:, :128]
            DP[j * tok : (j + 1) * tok, 2 * D + p * 128 : 2 * D + (p + 1) * 128] = both[:, 128:]


def row_of(layer, k):
    return slice(layer * SMALL + k, layer * SMALL + k + 1)


class Plan:
    def __init__(self, ngrp, nrow, tok):
        self.ngrp, self.nrow, self.tok = ngrp, nrow, tok
        self.ncol = ngrp // 2
        self.bits = max(self.ncol.bit_length() - 1, 0)
        self.ndev = ngrp * nrow
        self.ch = D // self.ndev
        self.chp = -(-self.ch // 8) * 8
        self.cf = FF // self.ndev
        self.rows = self.ncol * 2 * self.chp
        self.nsel = 2 * self.rows
        self.wide = FF // ngrp
        self.per = D // (2 * self.wide)
        self.frows = self.ncol * 2 * self.cf
        dims = list(range(self.bits))[::-1] + [-1]
        turns = [k * len(dims) // 3 for k in range(3)]
        self.orders = [dims[t:] + dims[:t] for t in turns]

    def piece(self, order, index):
        col, pair = 0, 0
        for place, dim in enumerate(order):
            bit = (index >> (len(order) - 1 - place)) & 1
            if dim < 0:
                pair = bit
            else:
                col |= bit << dim
        return col, pair

    def moved(self, turn):
        first = {self.piece(self.orders[0], k): k for k in range(2 * self.ncol)}
        return [first[self.piece(self.orders[turn], k)] for k in range(2 * self.ncol)]

    def selector(self):
        table = np.zeros((2, self.nsel, D), np.float32)
        for half in range(2):
            for c in range(2):
                for index in range(self.ncol * 2):
                    col, pair = self.piece(self.orders[0], index)
                    first = ((col * 2 + c) * 4 + 2 * half + pair) * self.ch
                    row = c * self.rows + index * self.chp
                    for i in range(self.ch):
                        table[half, row + i, first + i] = 1
        return table

    def selector_ff(self):
        table = np.zeros((2, self.nsel, D), np.float32)
        for half in range(2):
            for c in range(2):
                row = c * self.rows
                for j in range(self.per):
                    first = (j * 2 + c) * self.wide + half * 2 * self.cf
                    for i in range(2 * self.cf):
                        table[half, row, first + i] = 1
                        row += 1
        return table


def where_am_i():
    g = lax.axis_index("grp")
    z = lax.axis_index("row")
    c = lax.rem(g, 2)
    col = lax.div(g, 2)
    outer = jnp.logical_or(z == 0, z == 3)
    parity = jnp.where(outer, 0, 1)
    return g, z, c, col, outer, parity


def fill_bias(bias, starts, c, tok):
    T = 2 * tok
    lane = lax.broadcasted_iota(jnp.int32, (1, T), 1)
    qpos = jnp.where(lane < tok, c * tok + lane, (3 - c) * tok + lane - tok).astype(F32)
    begin = jnp.zeros((1, T), F32)
    for start in starts:
        begin = jnp.maximum(begin, jnp.where(qpos >= start, start, 0.0))
    kpos = lax.broadcasted_iota(jnp.int32, (2 * T, T), 0).astype(F32)
    bias[...] = jnp.where((kpos <= qpos) & (kpos >= begin), 0.0, NEG)


def main_kernel(
    plan,
    x_own, cot_own, pass_ref, doc_ref, tok_ref, ln1g, ln1b, qb, vb, ob, ln2g, ln2b, ub, db, sel_h,
    wq_h, wo_h, wu_h, wd_h,
    hid_o, up_o, vec_o, tot_o, asel_h, osel_h, usel_h, gsel_h, dp_h, dy_h, df_h, dr_h,
    sx_h, sq_h, skv_h, slse_h, sm_h, sgp_h,
    wq, wo, wu, wd, sel, xin, cot, par_ref, par_in, tsend, trecv,
    bias, X, Q, KV, LSE, M, GP, O, GF, XN, asel, osel, usel, gsel,
    R, U, DKV, RDKV, DP, DR, DY, VAC, ret_s, ret_r,
    w_sem, sel_sem, in_send, in_recv, cot_send, cot_recv, par_sem, t_sem, kv_send, kv_recv,
    st_sem, ld_sem, sel_out, dkv_send, dkv_recv, bst_sem, ret_send, ret_recv,
):
    tok = plan.tok
    T = 2 * tok
    g, z, c, col, outer, parity = where_am_i()
    half = lax.div(z, 2)
    peer = (col * 2 + 1 - c, z)
    off_lo = pl.multiple_of(c * tok, tok)
    off_hi = pl.multiple_of((3 - c) * tok, tok)
    poff_lo = pl.multiple_of((1 - c) * tok, tok)
    poff_hi = pl.multiple_of((2 + c) * tok, tok)

    weight_copies = []
    for l in range(LAYERS):
        for i, (src, dst) in enumerate(((wq_h, wq), (wo_h, wo), (wu_h, wu), (wd_h, wd))):
            weight_copies.append(pltpu.make_async_copy(src.at[l], dst.at[l], w_sem.at[l, i]))
    weight_copies[0].start()
    n_rows = sel.shape[1] // 2
    sel_copies = []
    for i in range(2):
        for j, core in enumerate((c, 1 - c)):
            src = sel_h.at[i, half, pl.ds(pl.multiple_of(core * n_rows, 16), n_rows), :]
            dst = sel.at[i, pl.ds(j * n_rows, n_rows), :]
            sel_copies.append(pltpu.make_async_copy(src, dst, sel_sem.at[i, j]))
    for cp in sel_copies:
        cp.start()

    numbers = [pass_ref[0], tok_ref[0]] + [doc_ref[0, k] for k in range(4)] + [0, 0]
    for k, number in enumerate(numbers):
        par_ref[k : k + 1, :] = jnp.full((1, 128), number, jnp.int32).astype(F32)

    barrier = pltpu.get_barrier_semaphore()
    count = 0
    for dc in range(2):
        for dz in range(plan.nrow):
            if dc == 0 and dz == 0:
                continue
            target = (col * 2 + lax.rem(c + dc, 2), lax.rem(z + dz, plan.nrow))
            pl.semaphore_signal(barrier, inc=1, device_id=target, device_id_type=MESH)
            count += 1
    others = [(col ^ (1 << b)) * 2 + c for b in range(plan.bits)]
    for other in others:
        pl.semaphore_signal(barrier, inc=1, device_id=(other, z), device_id_type=MESH)
        count += 1
    pl.semaphore_wait(barrier, count)

    block_core = jnp.where(outer, 0, 1)
    slot_in = lax.div(z, 2)
    send_list = []
    for i in range(2):
        zt = jnp.where(c == 0, 3 * i, 1 + i)
        is_self = jnp.logical_and(c == block_core, zt == z)
        send_list.append((i, zt, is_self))

    def deliver(src, dst, send, recv):
        for i, zt, is_self in send_list:

            @pl.when(is_self)
            def _():
                pltpu.make_async_copy(src, dst.at[slot_in], recv.at[slot_in]).start()

            @pl.when(jnp.logical_not(is_self))
            def _():
                pltpu.make_async_remote_copy(
                    src_ref=src, dst_ref=dst.at[slot_in], send_sem=send.at[i], recv_sem=recv.at[slot_in],
                    device_id=(col * 2 + block_core, zt), device_id_type=MESH,
                ).start()

    def deliver_sent(src, dst, send, recv):
        for i, zt, is_self in send_list:

            @pl.when(jnp.logical_not(is_self))
            def _():
                pltpu.make_async_remote_copy(
                    src_ref=src, dst_ref=dst.at[slot_in], send_sem=send.at[i], recv_sem=recv.at[slot_in],
                    device_id=(col * 2 + block_core, zt), device_id_type=MESH,
                ).wait_send()

    def deliver_wait(src, dst, recv):
        for i in range(2):
            pltpu.make_async_copy(src, dst.at[i], recv.at[i]).wait()

    deliver(x_own, xin, in_send, in_recv)

    par_copy = pltpu.make_async_remote_copy(
        src_ref=par_ref, dst_ref=par_in, send_sem=par_sem.at[0], recv_sem=par_sem.at[1],
        device_id=peer, device_id_type=MESH,
    )
    par_copy.start()
    for cp in weight_copies[1:]:
        cp.start()
    par_copy.wait()
    served = jnp.where(parity == c, par_ref[...], par_in[...])
    tcount = par_ref[1:2, :] + par_in[1:2, :]
    total = jnp.broadcast_to(tcount, (8, 128))
    for b in range(plan.bits):
        tsend[b] = total
        cp = pltpu.make_async_remote_copy(
            src_ref=tsend.at[b], dst_ref=trecv.at[b], send_sem=t_sem.at[0, b], recv_sem=t_sem.at[1, b],
            device_id=(others[b], z), device_id_type=MESH,
        )
        cp.start()
        cp.wait()
        total = total + trecv[b]
    factor = served[1:2, :] / total[0:1, :]
    tot_o[0:1, :] = factor
    tot_o[1:8, :] = jnp.concatenate([served[0:1, :], served[2:8, :]], axis=0)
    passes = served[0:1, 0:1]

    fill_bias(bias, [served[2 + k : 3 + k, 0:1] for k in range(4)], c, tok)
    VAC[...] = jnp.zeros_like(VAC)
    for cp in weight_copies:
        cp.wait()
    for cp in sel_copies:
        cp.wait()

    deliver_wait(x_own, xin, in_recv)
    deliver_sent(x_own, xin, in_send, in_recv)
    XN[0:tok] = xin[0].astype(F32)
    XN[tok:T] = xin[1].astype(F32)
    deliver(cot_own, cot, cot_send, cot_recv)

    def stash_copies(s, slot, sem, back):
        pairs = ((X, sx_h), (Q, sq_h), (LSE, slse_h), (M, sm_h), (GP, sgp_h))
        out = []
        for i, (v, h) in enumerate(pairs):
            if back:
                out.append(pltpu.make_async_copy(h.at[s], v.at[slot], sem.at[slot, i]))
            else:
                out.append(pltpu.make_async_copy(v.at[slot], h.at[s], sem.at[slot, i]))
        return out

    def kv_stash(s, slot):
        return pltpu.make_async_copy(KV.at[slot], skv_h.at[s], st_sem.at[slot, 5])

    def kv_load(s, slot):
        return pltpu.make_async_copy(skv_h.at[s], KV.at[slot], ld_sem.at[slot, 5])

    def sel_copies_out(l, sect):
        at = pl.ds(pl.multiple_of(sect * T, T), T)
        return [
            pltpu.make_async_copy(asel, asel_h.at[l, :, at], sel_out.at[0]),
            pltpu.make_async_copy(osel, osel_h.at[l, :, at], sel_out.at[1]),
            pltpu.make_async_copy(usel, usel_h.at[l, :, at], sel_out.at[2]),
            pltpu.make_async_copy(gsel, gsel_h.at[l, :, at], sel_out.at[3]),
        ]

    def kv_moves(slot, offsets):
        out = []
        for part in range(2):
            out.append([])
            for i, off in enumerate(offsets):
                ref = KV.at[slot, pl.ds(off, tok), part * D : (part + 1) * D]
                out[part].append(
                    pltpu.make_async_remote_copy(
                        src_ref=ref, dst_ref=ref, send_sem=kv_send.at[slot, part, i],
                        recv_sem=kv_recv.at[slot, part, i], device_id=peer, device_id_type=MESH,
                    )
                )
        return out

    def kv_copies(slot):
        return kv_moves(slot, (off_lo, off_hi))

    def kv_arrivals(slot):
        return kv_moves(slot, (poff_lo, poff_hi))

    def forward(sect, l):
        s = sect * LAYERS + l
        slot = l

        @pl.when(sect >= 1)
        def _():
            for cp in stash_copies(s - 2, slot, st_sem, False):
                cp.wait()

        x = XN[...]
        X[slot] = x
        hat, _ = normalised(x)
        a = (hat * ln1g[l : l + 1, :] + ln1b[l : l + 1, :]).astype(BF16)

        def own_rows(values, at):
            KV[slot, pl.ds(off_lo, tok), at] = values[:tok]
            KV[slot, pl.ds(off_hi, tok), at] = values[tok:]

        sends = kv_copies(slot)
        arrivals = kv_arrivals(slot)
        own_rows(nn(a, wq[l, :, D : 2 * D]).astype(BF16), slice(0, D))
        for cp in sends[0]:
            cp.start()
        own_rows((nn(a, wq[l, :, 2 * D : 3 * D]) + vb[l : l + 1, :]).astype(BF16), slice(D, 2 * D))
        for cp in sends[1]:
            cp.start()
        q = (nn(a, wq[l, :, 0:D]) + qb[l : l + 1, :]).astype(BF16)
        Q[slot] = q * jnp.asarray(0.125, BF16)

        def rows_of_before():
            for cp in sel_copies_out(0, 0):
                cp.wait()

        if l == 0:
            pl.when(sect >= 1)(rows_of_before)
        else:
            rows_of_before()
        asel[...] = nt(sel[0], a).astype(BF16)
        for cp in arrivals[0]:
            cp.wait_recv()

        def values_here():
            for cp in arrivals[1]:
                cp.wait_recv()
            for cp in sends[0] + sends[1]:
                cp.wait_send()

            @pl.when(sect < MAXP)
            def _():
                kv_stash(s, slot).start()

        attention_forward(KV.at[slot], Q.at[slot], LSE.at[slot], bias, O, values_here)
        o = O[...]
        osel[...] = nt(sel[0], o).astype(BF16)
        m = x + (nn(o, wo[l]) + ob[l : l + 1, :])
        M[slot] = m
        hat2, _ = normalised(m)
        a2 = (hat2 * ln2g[l : l + 1, :] + ln2b[l : l + 1, :]).astype(BF16)
        usel[...] = nt(sel[0], a2).astype(BF16)

        for j in range(FF // D):
            js = slice(j * D, (j + 1) * D)
            f = nn(a2, wu[l, :, js]) + ub[l : l + 1, js]
            f2 = f * f
            u = f * (0.7978845608028654 + 0.035677408136300125 * f2)
            t = jnp.tanh(u)
            h = 0.5 + 0.5 * t
            ga = f * h
            gp = h + ga * (1.0 - h) * (1.5957691216057308 + 0.21406444881780074 * f2)
            gb = ga.astype(BF16)
            GF[:, js] = gb
            GP[slot, :, js] = gp.astype(BF16)
            gs = nt(sel[1], gb).astype(BF16)
            n = plan.per * 2 * plan.cf
            m2 = sel.shape[1] // 2
            for cc in range(2):
                gsel[cc * plan.frows + j * n : cc * plan.frows + (j + 1) * n] = gs[cc * m2 : cc * m2 + n]

        y = m + (nn(GF[...], wd[l]) + db[l : l + 1, :])
        if l == LAYERS - 1:
            bar = jnp.where(sect < MAXP, sect, -1).astype(F32)
            y = jnp.where(passes > bar, y, X[0])
        XN[...] = y

        @pl.when(sect < MAXP)
        def _():
            for cp in stash_copies(s, slot, st_sem, False):
                cp.start()
            kv_stash(s, slot).wait()

        for cp in sel_copies_out(l, sect):
            cp.start()

    def forward_section(sect, carry):
        for l in range(LAYERS):
            forward(sect, l)
        return carry

    lax.fori_loop(0, MAXP + 1, forward_section, 0)

    block = jnp.where(z < 2, c, 3 - c)
    owner = (col * 2 + parity, block)
    mine = jnp.logical_and(parity == c, block == z)

    ret_recv_wait = pltpu.make_async_copy(ret_s, ret_r, ret_recv.at[0])
    ret_remote = pltpu.make_async_remote_copy(
        src_ref=ret_s, dst_ref=ret_r, send_sem=ret_send.at[0], recv_sem=ret_recv.at[0],
        device_id=owner, device_id_type=MESH,
    )

    @pl.when(z < 2)
    def _():
        ret_s[...] = XN[0:tok]

    @pl.when(z >= 2)
    def _():
        ret_s[...] = XN[tok:T]

    @pl.when(mine)
    def _():
        ret_recv_wait.start()

    @pl.when(jnp.logical_not(mine))
    def _():
        ret_remote.start()

    deliver_wait(cot_own, cot, cot_recv)
    deliver_sent(cot_own, cot, cot_send, cot_recv)
    U[0:tok] = cot[0]
    U[tok:T] = cot[1]
    for cp in sel_copies_out(0, 0):
        cp.wait()

    def back_copies(l, sect):
        at = pl.ds(pl.multiple_of(sect * T, T), T)
        return [
            pltpu.make_async_copy(DP, dp_h.at[l, at, :], bst_sem.at[0]),
            pltpu.make_async_copy(DY, dy_h.at[l, at, :], bst_sem.at[1]),
            pltpu.make_async_copy(GF, df_h.at[l, at, :], bst_sem.at[2]),
            pltpu.make_async_copy(DR, dr_h.at[l, at, :], bst_sem.at[3]),
        ]

    def dkv_copies(slot, half):
        at = slice(half * D, (half + 1) * D)
        return [
            pltpu.make_async_remote_copy(
                src_ref=DKV.at[pl.ds(off, tok), at], dst_ref=RDKV.at[slot, i, :, at],
                send_sem=dkv_send.at[slot, half, i], recv_sem=dkv_recv.at[slot, half, i],
                device_id=peer, device_id_type=MESH,
            )
            for i, off in enumerate((poff_lo, poff_hi))
        ]

    def backward(i, l):
        sect = MAXP - i
        s = sect * LAYERS + l
        slot = l

        def stored():
            for cp in back_copies(0, 0):
                cp.wait()

        if i >= 1 or l < LAYERS - 1:
            stored()
        if i >= 1:
            for cp in stash_copies(s, slot, ld_sem, True):
                cp.wait()
            kv_load(s, slot).wait()

        active = jnp.where(passes > (-1.0 if sect == MAXP else float(sect)), jnp.ones((1, 1), F32), jnp.zeros((1, 1), F32))
        r = U[...] * active if l == LAYERS - 1 else R[...]
        dr = r.astype(BF16)
        DR[...] = dr
        VAC[row_of(l, 7)] += column_sum(dr.astype(F32))
        for j in range(FF // D):
            js = slice(j * D, (j + 1) * D)
            dg = nt(dr, wd[l, js, :])
            df = (dg * GP[slot, :, js].astype(F32)).astype(BF16)
            GF[:, js] = df
            VAC[row_of(l, 8 + j)] += column_sum(df.astype(F32))
        da2 = nt(GF[...], wu[l])
        hat2, inv2 = normalised(M[slot])
        VAC[row_of(l, 5)] += column_sum(da2 * hat2)
        VAC[row_of(l, 6)] += column_sum(da2)
        dm = r + norm_back(da2, ln2g[l : l + 1, :], hat2, inv2)
        R[...] = dm
        dy = dm.astype(BF16)
        DY[...] = dy
        VAC[row_of(l, 4)] += column_sum(dy.astype(F32))
        O[...] = nt(dy, wo[l]).astype(BF16)

        def send_half(half):
            for cp in dkv_copies(slot, half):
                cp.start()

        attention_backward(
            KV.at[slot], Q.at[slot], LSE.at[slot], bias, O, DP, DKV,
            {HEADS // 2 - 1: lambda: send_half(0), HEADS - 1: lambda: send_half(1)},
        )
        x = X[slot]
        hat, inv = normalised(x)

        if i == 0:
            for cp in stash_copies(s - 2, slot, ld_sem, True):
                cp.start()
            kv_load(s - 2, slot).start()

        dqb = DP[:, 0:D]
        VAC[row_of(l, 2)] += column_sum(dqb.astype(F32))
        da = nt(dqb, wq[l, :, 0:D])
        for half in range(2):
            for cp in dkv_copies(slot, half):
                cp.wait()
            merge_kv(DP, DKV, RDKV.at[slot], (off_lo, off_hi), half)
        dkv = DP[:, D : 3 * D]
        VAC[row_of(l, 3)] += column_sum(dkv[:, D:].astype(F32))
        da = da + nt(dkv, wq[l, :, D : 3 * D])
        VAC[row_of(l, 0)] += column_sum(da * hat)
        VAC[row_of(l, 1)] += column_sum(da)
        new = R[...] + norm_back(da, ln1g[l : l + 1, :], hat, inv)
        if l == 0:
            U[...] = new + (1.0 - active) * U[...]
        else:
            R[...] = new
        for cp in back_copies(l, sect):
            cp.start()

    for i in range(MAXP):
        for l in range(LAYERS - 1, -1, -1):
            backward(i, l)
    ret_recv_wait.wait()

    @pl.when(jnp.logical_not(mine))
    def _():
        ret_remote.wait_send()

    hid_o[...] = ret_r[...]
    up_o[...] = U[...]
    vec_o[...] = VAC[...]
    for cp in back_copies(0, 0):
        cp.wait()


def run_main(plan, x, cot, numbers, vecs, sel, weights):
    tok = plan.tok
    T = 2 * tok
    L = 4 * tok
    vmem = pl.BlockSpec(memory_space=pltpu.VMEM)
    hbm = pl.BlockSpec(memory_space=pl.ANY)
    smem = pl.BlockSpec(memory_space=pltpu.SMEM)
    S = jax.ShapeDtypeStruct
    K = (MAXP + 1) * T
    outs = [
        (S((tok, D), F32), vmem),
        (S((T, D), F32), vmem),
        (S((LAYERS * SMALL, D), F32), vmem),
        (S((8, 128), F32), vmem),
        (S((LAYERS, plan.nsel, K), BF16), hbm),
        (S((LAYERS, plan.nsel, K), BF16), hbm),
        (S((LAYERS, plan.nsel, K), BF16), hbm),
        (S((LAYERS, 2 * plan.frows, K), BF16), hbm),
        (S((LAYERS, K, 3 * D), BF16), hbm),
        (S((LAYERS, K, D), BF16), hbm),
        (S((LAYERS, K, FF), BF16), hbm),
        (S((LAYERS, K, D), BF16), hbm),
        (S((STEPS, T, D), F32), hbm),
        (S((STEPS, T, D), BF16), hbm),
        (S((STEPS, L, 2 * D), BF16), hbm),
        (S((STEPS, 8, 8, T), F32), hbm),
        (S((STEPS, T, D), F32), hbm),
        (S((STEPS, T, FF), BF16), hbm),
    ]
    V = pltpu.VMEM
    DMA = pltpu.SemaphoreType.DMA
    nb = max(plan.bits, 1)
    scratch = [
        V((LAYERS, D, 3 * D), BF16), V((LAYERS, D, D), BF16), V((LAYERS, D, FF), BF16), V((LAYERS, FF, D), BF16),
        V((2, sel.shape[2], D), BF16), V((2, tok, D), BF16), V((2, tok, D), F32), V((8, 128), F32), V((8, 128), F32),
        V((nb, 8, 128), F32), V((nb, 8, 128), F32),
        V((L, T), F32),
        V((2, T, D), F32), V((2, T, D), BF16), V((2, L, 2 * D), BF16), V((2, 8, 8, T), F32), V((2, T, D), F32),
        V((2, T, FF), BF16), V((T, D), BF16), V((T, FF), BF16), V((T, D), F32),
        V((plan.nsel, T), BF16), V((plan.nsel, T), BF16), V((plan.nsel, T), BF16), V((2 * plan.frows, T), BF16),
        V((T, D), F32), V((T, D), F32), V((L, 2 * D), BF16), V((2, 2, tok, 2 * D), BF16), V((T, 3 * D), BF16),
        V((T, D), BF16), V((T, D), BF16), V((LAYERS * SMALL, D), F32), V((tok, D), F32), V((tok, D), F32),
        DMA((LAYERS, 4)), DMA((3, 2)), DMA((2,)), DMA((2,)), DMA((2,)), DMA((2,)), DMA((2,)), DMA((2, nb)),
        DMA((2, 2, 2)), DMA((2, 2, 2)), DMA((2, 6)), DMA((2, 6)), DMA((4,)), DMA((2, 2, 2)), DMA((2, 2, 2)), DMA((4,)),
        DMA((1,)), DMA((1,)),
    ]
    call = pl.pallas_call(
        functools.partial(main_kernel, plan),
        out_shape=[o[0] for o in outs],
        out_specs=[o[1] for o in outs],
        in_specs=[vmem] * 2 + [smem] * 3 + [vmem] * 9 + [hbm] * 5,
        scratch_shapes=scratch,
        compiler_params=pltpu.CompilerParams(
            collective_id=0, has_side_effects=True, vmem_limit_bytes=VMEM_LIMIT
        ),
        name="layers",
    )
    return call(x, cot, *numbers, *vecs, sel, *weights)


def fold(x):
    n = x.shape[1] // 2
    return jnp.concatenate([x[:, :n], x[:, n:]], axis=0)


def unfold(x):
    n = x.shape[0] // 2
    return jnp.concatenate([x[:n], x[n:]], axis=1)


class Item:
    def __init__(self, name, rows, cols, chunk):
        self.name, self.rows, self.cols, self.chunk = name, rows, cols, chunk

    def part(self, k):
        return slice(k * self.cols // 3, (k + 1) * self.cols // 3)

    def half_part(self, k):
        return slice(k * self.cols // 6, (k + 1) * self.cols // 6)


def items_of(plan):
    return [
        Item("down", plan.frows, D, plan.cf),
        Item("up", plan.rows, FF, plan.chp),
        Item("out", plan.rows, D, plan.chp),
        Item("qkv", plan.rows, 3 * D, plan.chp),
    ]


def last_kernel(
    plan,
    up_h, vec_ref, tot_ref, ln1g, ln2g, asel_h, osel_h, usel_h, gsel_h, dp_h, dy_h, df_h, dr_h,
    sx_h, sq_h, skv_h, slse_h, sm_h, sgp_h, wq_h, wo_h, wu_h, wd_h,
    *refs,
):
    items = items_of(plan)
    n = len(items)
    outs, gin_o, vec_o, refs = refs[:n], refs[n], refs[n + 1], refs[n + 2 :]
    lhs, rhs, refs = refs[:n], refs[n : 2 * n], refs[2 * n :]
    OW, CR, refs = refs[:n], refs[n : 2 * n], refs[2 * n :]
    stages = plan.bits + 1
    RB = []
    for k in range(stages - 1):
        RB.append(refs[:n])
        refs = refs[n:]
    FS, FR, refs = refs[:n], refs[n : 2 * n], refs[2 * n :]
    (
        ST, wq, wo, wu, wd, Q, KV, LSE, XM, GP, bias, R, DKV, RDKV, ret_r, vs, vr,
        l_sem, w_sem, s_sem, chip_sem, stage_sem, vec_sem, dkv_sem, ret_sem, up_sem,
    ) = refs
    tok = plan.tok
    T = 2 * tok
    g, z, c, col, outer, parity = where_am_i()
    peer = (col * 2 + 1 - c, z)
    off = [pl.multiple_of(c * tok, tok), pl.multiple_of((3 - c) * tok, tok)]
    poff = [pl.multiple_of((1 - c) * tok, tok), pl.multiple_of((2 + c) * tok, tok)]
    DOWN, UP, OUT, QKV = range(n)
    sources = ((gsel_h, dr_h), (usel_h, df_h), (osel_h, dy_h), (asel_h, dp_h))
    DR, GF, DY, DP = [r.at[0:T] for r in rhs]
    DO = DY
    blocks = FF // D
    rows4 = items[DOWN].rows // blocks
    staged = [ST.at[0:rows4, :], ST, ST.at[:, 3 * D :], ST.at[:, : 3 * D]]

    def operand_loads(l, i):
        a, b = sources[i]
        later = pl.ds(T, rhs[i].shape[0] - T)
        return (
            pltpu.make_async_copy(a.at[l], lhs[i], l_sem.at[i, 0]),
            pltpu.make_async_copy(b.at[l, later, :], rhs[i].at[later, :], l_sem.at[i, 1]),
        )

    weight_refs = {"wd": (wd_h, wd, 0), "wu": (wu_h, wu, 1), "wo": (wo_h, wo, 2), "wq": (wq_h, wq, 3)}
    slot_refs = {
        "GP": (sgp_h, GP, 0), "M": (sm_h, XM, 1), "Q": (sq_h, Q, 2), "KV": (skv_h, KV, 3), "LSE": (slse_h, LSE, 4),
        "X": (sx_h, XM, 5),
    }

    def load(l, *names):
        out = []
        for name in names:
            if name in weight_refs:
                h, v, k = weight_refs[name]
                out.append(pltpu.make_async_copy(h.at[l], v, w_sem.at[k]))
            else:
                h, v, k = slot_refs[name]
                out.append(pltpu.make_async_copy(h.at[l], v, s_sem.at[k]))
        return out

    def start(copies):
        for cp in copies:
            cp.start()

    def wait(copies):
        for cp in copies:
            cp.wait()

    top_layer = LAYERS - 1
    up_load = pltpu.make_async_copy(up_h, R, up_sem.at[0])
    up_load.start()
    start(operand_loads(top_layer, DOWN))
    start(load(top_layer, "wd", "GP"))

    def partner(dim):
        if dim < 0:
            return (g, z + 1 - 2 * lax.rem(z, 2))
        return ((col ^ (1 << dim)) * 2 + c, z)

    def bit_of(dim):
        if dim < 0:
            return lax.rem(z, 2)
        return lax.rem(lax.div(col, 1 << dim), 2)

    dims = [-1] + list(range(plan.bits))
    block = jnp.where(z < 2, c, 3 - c)
    owner = (col * 2 + parity, block)
    mine = jnp.logical_and(parity == c, block == z)
    barrier = pltpu.get_barrier_semaphore()
    count = 0
    for dc in range(2):
        for dz in range(plan.nrow):
            if dc == 0 and dz == 0:
                continue
            target = (col * 2 + lax.rem(c + dc, 2), lax.rem(z + dz, plan.nrow))
            pl.semaphore_signal(barrier, inc=1, device_id=target, device_id_type=MESH)
            count += 1
    for dim in dims[1:]:
        pl.semaphore_signal(barrier, inc=1, device_id=partner(dim), device_id_type=MESH)
        count += 1
    pl.semaphore_wait(barrier, count)

    factor = tot_ref[0:1, 0:1]
    active = jnp.where(tot_ref[1:2, 0:1] > 0.0, jnp.ones((1, 1), F32), jnp.zeros((1, 1), F32))
    fill_bias(bias, [tot_ref[2 + k : 3 + k, 0:1] for k in range(4)], c, tok)

    def chip_copy(l, i):
        return pltpu.make_async_remote_copy(
            src_ref=staged[i], dst_ref=CR[i], send_sem=chip_sem.at[0, i], recv_sem=chip_sem.at[1, i],
            device_id=peer, device_id_type=MESH,
        )

    def base_of(i, order, k):
        base, rows = 0, items[i].rows
        for j in range(k):
            rows //= 2
            base = base + bit_of(order[j]) * rows
        return base, rows

    def stage_copy(l, i, k, part):
        item, order = items[i], plan.orders[part]
        if k == stages - 1:
            at = item.half_part(part)
            src, dst = FS[i].at[:, at], FR[i].at[l, :, at]
        else:
            base, rows = base_of(i, order, k)
            rows //= 2
            first = base + (1 - bit_of(order[k])) * rows
            at = item.part(part)
            src, dst = OW[i].at[l, pl.ds(pl.multiple_of(first, 16), rows), at], RB[k][i].at[l, :, at]
        return pltpu.make_async_remote_copy(
            src_ref=src, dst_ref=dst, send_sem=stage_sem.at[0, l, i, k, part],
            recv_sem=stage_sem.at[1, l, i, k, part], device_id=partner(order[k]), device_id_type=MESH,
        )

    def product(l, i):
        wait(operand_loads(l, i))
        item = items[i]
        e = item.chunk
        for part in range(3):
            cols = item.part(part)
            place = plan.moved(part)
            r = nn(lhs[i][...], rhs[i][:, cols]) * factor
            for core in range(2):
                pieces = [r[core * item.rows + k * e : core * item.rows + (k + 1) * e] for k in place]
                r_core = jnp.concatenate(pieces, axis=0).astype(BF16)
                if core == 0:
                    OW[i][l, :, cols] = r_core
                elif i == DOWN:
                    for b in range(blocks):
                        at = slice(b * D + cols.start, b * D + cols.stop)
                        staged[i][:, at] = r_core[b * rows4 : (b + 1) * rows4]
                else:
                    staged[i][:, cols] = r_core
        if l > 0:
            start(operand_loads(l - 1, i))
        chip_copy(l, i).start()

    def after_chip(l, i):
        chip_copy(l, i).wait()
        if i == DOWN:
            for b in range(blocks):
                at = slice(b * rows4, (b + 1) * rows4)
                add = CR[i][:, b * D : (b + 1) * D].astype(F32)
                OW[i][l, at, :] = (OW[i][l, at, :].astype(F32) + add).astype(BF16)
        else:
            OW[i][l] = (OW[i][l].astype(F32) + CR[i][...].astype(F32)).astype(BF16)
        for part in range(3):
            stage_copy(l, i, 0, part).start()

    def after_stage(l, i, k):
        item = items[i]
        own = outs[i].shape[1]
        for part in range(3):
            order, cols = plan.orders[part], item.part(part)
            stage_copy(l, i, k, part).wait()
            if k == stages - 1:
                outs[i][l, :, cols] += unfold(FR[i][l, :, item.half_part(part)].astype(F32))[:own]
                continue
            base, rows = base_of(i, order, k + 1)
            at = pl.ds(pl.multiple_of(base, 16), rows)
            both = OW[i][l, at, cols].astype(F32) + RB[k][i][l, :, cols].astype(F32)
            if k + 1 == stages - 1:
                rows //= 2
                first = bit_of(order[k + 1]) == 0
                outs[i][l, :, cols] = jnp.where(first, both[:rows], both[rows:])[:own]
                FS[i][:, item.half_part(part)] = fold(jnp.where(first, both[rows:], both[:rows])).astype(BF16)
            else:
                OW[i][l, at, cols] = both.astype(BF16)
            stage_copy(l, i, k + 1, part).start()

    def dkv_copies(part):
        at = slice(part * D, (part + 1) * D)
        return [
            pltpu.make_async_remote_copy(
                src_ref=DKV.at[pl.ds(poff[j], tok), at], dst_ref=RDKV.at[j, :, at],
                send_sem=dkv_sem.at[0, part, j], recv_sem=dkv_sem.at[1, part, j],
                device_id=peer, device_id_type=MESH,
            )
            for j in range(2)
        ]

    vec_o[...] = vec_ref[...]

    def backward(l, marks):
        def mark(name):
            for f in marks.get(name, ()):
                f()

        def reload(*names):
            if l > 0:
                start(load(l - 1, *names))

        r = R[...]
        dr = r.astype(BF16)
        DR[...] = dr
        vec_o[row_of(l, 7)] += column_sum(dr.astype(F32))
        product(l, DOWN)
        if l == top_layer:
            start(operand_loads(l, UP))
            start(load(l, "wu", "M"))
        mark("down")
        wait(load(l, "wd", "GP"))
        for j in range(FF // D):
            js = slice(j * D, (j + 1) * D)
            dg = nt(dr, wd[js, :])
            df = (dg * GP[:, js].astype(F32)).astype(BF16)
            GF[:, js] = df
            vec_o[row_of(l, 8 + j)] += column_sum(df.astype(F32))
        reload("wd", "GP")
        if l == top_layer:
            start(operand_loads(l, OUT))
            start(load(l, "wo", "Q", "KV", "LSE"))
        mark("df")
        product(l, UP)
        if l == top_layer:
            start(load(l, "wq"))
            start(operand_loads(l, QKV))
        mark("up")
        wait(load(l, "wu", "M"))
        da2 = nt(GF[...], wu[...])
        hat2, inv2 = normalised(XM[...])
        vec_o[row_of(l, 5)] += column_sum(da2 * hat2)
        vec_o[row_of(l, 6)] += column_sum(da2)
        dm = r + norm_back(da2, ln2g[l : l + 1, :], hat2, inv2)
        R[...] = dm
        dy = dm.astype(BF16)
        DY[...] = dy
        vec_o[row_of(l, 4)] += column_sum(dy.astype(F32))
        start(load(l, "X"))
        reload("wu")
        mark("dy")
        product(l, OUT)
        wait(load(l, "wo", "Q", "KV", "LSE"))
        DO[...] = nt(dy, wo[...]).astype(BF16)
        reload("wo")
        def first_half():
            start(dkv_copies(0))
            mark("half")

        attention_backward(
            KV, Q, LSE, bias, DO, DP, DKV,
            {HEADS // 2 - 1: first_half, HEADS - 1: lambda: start(dkv_copies(1))},
        )
        reload("Q", "KV", "LSE")
        mark("attention")
        wait(load(l, "X", "wq"))
        hat, inv = normalised(XM[...])
        if l == 0:
            up_again.start()
        else:
            reload("M")
        dqb = DP[:, 0:D]
        vec_o[row_of(l, 2)] += column_sum(dqb.astype(F32))
        da = nt(dqb, wq[:, 0:D])
        for part in range(2):
            for cp in dkv_copies(part):
                cp.wait()
            merge_kv(DP, DKV, RDKV, off, part)
        product(l, QKV)
        mark("qkv")
        dkv = DP[:, D : 3 * D]
        vec_o[row_of(l, 3)] += column_sum(dkv[:, D:].astype(F32))
        da = da + nt(dkv, wq[:, D : 3 * D])
        reload("wq")
        vec_o[row_of(l, 0)] += column_sum(da * hat)
        vec_o[row_of(l, 1)] += column_sum(da)
        new = R[...] + norm_back(da, ln1g[l : l + 1, :], hat, inv)
        if l == 0:
            up_again.wait()
            new = (new + (1.0 - active) * XM[...]) * factor
        R[...] = new
        mark("end")

    up_again = pltpu.make_async_copy(up_h, XM, up_sem.at[0])

    done = set()

    def chip(l, i):
        return lambda: after_chip(l, i)

    def stage(l, i, k):
        done.add((l, i, k))
        return lambda: after_stage(l, i, k)

    up_load.wait()
    R[...] = R[...] * active
    backward(1, {
        "df": [chip(1, DOWN)],
        "dy": [chip(1, UP)],
        "half": [chip(1, OUT), stage(1, DOWN, 0)],
        "end": [chip(1, QKV), stage(1, UP, 0)],
    })
    backward(0, {
        "down": [stage(1, DOWN, 1), stage(1, OUT, 0)],
        "df": [chip(0, DOWN)],
        "up": [stage(1, UP, 1), stage(1, OUT, 1)],
        "dy": [chip(0, UP), stage(1, QKV, 0)],
        "half": [chip(0, OUT), stage(1, DOWN, 2), stage(0, DOWN, 0)],
        "attention": [stage(1, UP, 2), stage(1, QKV, 1), stage(1, OUT, 2)],
        "qkv": [stage(0, UP, 0), stage(0, DOWN, 1)],
    })

    home = R.at[pl.ds(pl.multiple_of(jnp.where(z < 2, 0, tok), tok), tok), :]
    ret_local = pltpu.make_async_copy(home, ret_r, ret_sem.at[1])
    ret_remote = pltpu.make_async_remote_copy(
        src_ref=home, dst_ref=ret_r, send_sem=ret_sem.at[0], recv_sem=ret_sem.at[1],
        device_id=owner, device_id_type=MESH,
    )

    @pl.when(mine)
    def _():
        ret_local.start()

    @pl.when(jnp.logical_not(mine))
    def _():
        ret_remote.start()

    vec_targets = [peer] + [partner(dim) for dim in dims]

    def vec_copy(k):
        return pltpu.make_async_remote_copy(
            src_ref=vs, dst_ref=vr.at[k], send_sem=vec_sem.at[0, k], recv_sem=vec_sem.at[1, k],
            device_id=vec_targets[k], device_id_type=MESH,
        )

    def vec_step(k):
        vec_copy(k).wait()
        if k + 1 < len(vec_targets):
            vs[...] = vs[...] + vr[k]
            vec_copy(k + 1).start()
        else:
            vec_o[...] = vs[...] + vr[k]

    vs[...] = vec_o[...] * factor
    vec_copy(0).start()
    after_chip(0, QKV)
    vec_at = 0
    ends = [
        (0, OUT, 0), (1, QKV, 2), (0, UP, 1), (0, 0, -1), (0, DOWN, 2), (0, OUT, 1), (0, QKV, 0), (0, 0, -1),
        (0, UP, 2), (0, OUT, 2), (0, QKV, 1), (0, 0, -1), (0, QKV, 2),
    ]
    order_of_items = [(1, DOWN), (1, UP), (1, OUT), (1, QKV), (0, OUT), (0, DOWN), (0, UP), (0, QKV)]
    left = [(l, i, k) for k in range(stages) for l, i in order_of_items if (l, i, k) not in done]
    if stages == 3:
        assert sorted(left) == sorted(e for e in ends if e[2] >= 0)
    else:
        ends = left
    for l, i, k in ends:
        if k >= 0:
            after_stage(l, i, k)
        else:
            vec_step(vec_at)
            vec_at += 1
    for k in range(vec_at, len(vec_targets)):
        vec_step(k)
    ret_local.wait()

    @pl.when(jnp.logical_not(mine))
    def _():
        ret_remote.wait_send()

    gin_o[...] = ret_r[...]


def run_last(plan, upstream, vec, tot, gains, stashes, weights):
    tok = plan.tok
    T = 2 * tok
    vmem = pl.BlockSpec(memory_space=pltpu.VMEM)
    hbm = pl.BlockSpec(memory_space=pl.ANY)
    S = jax.ShapeDtypeStruct
    V = pltpu.VMEM
    DMA = pltpu.SemaphoreType.DMA
    items = items_of(plan)
    n = len(items)
    stages = plan.bits + 1
    own = {"down": plan.cf, "up": plan.ch, "out": plan.ch, "qkv": plan.ch}
    outs = [S((LAYERS, own[i.name], i.cols), F32) for i in items] + [S((tok, D), F32), S(vec.shape, F32)]
    K = stashes[0].shape[2]
    scratch = [V((2 * i.rows, K), BF16) for i in items]
    scratch += [V((K, i.cols), BF16) for i in items]
    scratch += [V((LAYERS, i.rows, i.cols), BF16) for i in items]
    scratch += [
        V((i.rows * i.cols // FF, FF) if i.name == "down" else (i.rows, i.cols), BF16) for i in items
    ]
    for k in range(stages - 1):
        scratch += [V((LAYERS, i.rows >> (k + 1), i.cols), BF16) for i in items]
    last = [i.rows >> stages for i in items]
    scratch += [V((2 * r, i.cols // 2), BF16) for r, i in zip(last, items)]
    scratch += [V((LAYERS, 2 * r, i.cols // 2), BF16) for r, i in zip(last, items)]
    nv = 2 + plan.bits
    scratch += [
        V((plan.rows, FF), BF16),
        V((D, 3 * D), BF16), V((D, D), BF16), V((D, FF), BF16), V((FF, D), BF16),
        V((T, D), BF16), V((2 * T, 2 * D), BF16), V((8, 8, T), F32), V((T, D), F32), V((T, FF), BF16),
        V((2 * T, T), F32), V((T, D), F32), V((2 * T, 2 * D), BF16), V((2, tok, 2 * D), BF16),
        V((tok, D), F32), V(vec.shape, F32), V((nv,) + vec.shape, F32),
        DMA((n, 2)), DMA((4,)), DMA((6,)), DMA((2, n)), DMA((2, LAYERS, n, stages, 3)), DMA((2, nv)), DMA((2, 2, 2)),
        DMA((2,)), DMA((1,)),
    ]
    call = pl.pallas_call(
        functools.partial(last_kernel, plan),
        out_shape=outs,
        out_specs=[vmem] * len(outs),
        in_specs=[hbm] + [vmem] * 4 + [hbm] * (len(stashes) + 4),
        scratch_shapes=scratch,
        compiler_params=pltpu.CompilerParams(
            collective_id=1, has_side_effects=True, vmem_limit_bytes=VMEM_LIMIT
        ),
        name="last",
    )
    return call(upstream, vec, tot, *gains, *stashes, *weights)


def finish_kernel(plan, vec_ref, *refs):
    big = refs[:6]
    big_o, small_o = refs[6:12], refs[12:21]
    for a, b in zip(big, big_o):
        b[...] = a[...]
    me = lax.axis_index("grp") * plan.nrow + lax.axis_index("row")
    feature = lax.broadcasted_iota(jnp.int32, (D, 128), 0)
    place = lax.broadcasted_iota(jnp.int32, (D, 128), 1)

    def picked(rows, first, n):
        one_hot = jnp.where((feature == first + place) & (place < n), 1.0, 0.0)
        return jnp.dot(rows, one_hot, preferred_element_type=F32, precision=lax.Precision.HIGHEST)

    per = D // plan.cf
    rows = picked(vec_ref[...], me * plan.ch, plan.ch)
    wide = picked(vec_ref[...], lax.rem(me, per) * plan.cf, plan.cf)
    row = lax.broadcasted_iota(jnp.int32, (LAYERS * SMALL, 128), 0)
    for l in range(LAYERS):
        for i in range(8):
            small_o[i][l : l + 1, :] = rows[row_of(l, i), : plan.ch]
        line = jnp.sum(jnp.where(row == l * SMALL + 8 + lax.div(me, per), wide, 0.0), axis=0, keepdims=True)
        small_o[8][l : l + 1, :] = line[:, : plan.cf]


def run_finish(plan, vec, big):
    vmem = pl.BlockSpec(memory_space=pltpu.VMEM)
    S = jax.ShapeDtypeStruct
    outs = [S(a.shape, a.dtype) for a in big]
    outs += [S((LAYERS, plan.ch), F32)] * 8 + [S((LAYERS, plan.cf), F32)]
    return pl.pallas_call(
        functools.partial(finish_kernel, plan),
        out_shape=outs,
        in_specs=[vmem] * 7,
        out_specs=[vmem] * 15,
        name="finish",
    )(vec, *big)


def body(
    plan,
    inputs, cotangent, pass_counts, doc_starts, token_counts,
    ln1_gain, ln1_bias, qkv_weight, query_bias, value_bias, out_weight, out_bias,
    ln2_gain, ln2_bias, up_weight, up_bias, down_weight, down_bias,
):
    tables = [plan.selector(), plan.selector_ff()]
    sel = jnp.asarray(np.stack(tables).astype(jnp.bfloat16))
    vecs = (ln1_gain, ln1_bias, query_bias, value_bias, out_bias, ln2_gain, ln2_bias, up_bias, down_bias)
    weights = (qkv_weight, out_weight, up_weight, down_weight)
    hidden, upstream, vec, tot, *rest = run_main(
        plan, inputs, cotangent, (pass_counts, doc_starts, token_counts), vecs, sel, weights
    )
    g_down, g_up, g_out, g_qkv, grad_in, vec = run_last(
        plan, upstream, vec, tot, (ln1_gain, ln2_gain), rest, weights
    )
    big = (hidden, grad_in, g_qkv, g_out, g_up, g_down)
    hidden, grad_in, g_qkv, g_out, g_up, g_down, *v = run_finish(plan, vec, big)
    return (
        hidden, grad_in, v[0], v[1], g_qkv, v[2], v[3], g_out, v[4], v[5], v[6], g_up, v[8], g_down, v[7],
    )


def solution(mesh):
    ngrp, nrow = mesh.shape["grp"], mesh.shape["row"]
    whole = P(("grp", "row"), None)
    vector = P(None, ("grp", "row"))
    matrix = P(None, ("grp", "row"), None)

    def run(*args):
        return body(Plan(ngrp, nrow, args[0].shape[0]), *args)

    return jax.shard_map(
        run,
        mesh=mesh,
        in_specs=(whole, whole, P("grp"), P("grp", None), P("grp")) + (P(),) * 13,
        out_specs=(
            whole, whole, vector, vector, matrix, vector, vector, matrix, vector, vector, vector,
            matrix, vector, matrix, vector,
        ),
        check_vma=False,
    )
```

```python
import functools

import jax
import jax.numpy as jnp
from jax import lax
from jax.experimental import pallas as pl
from jax.experimental.pallas import tpu as pltpu
from jax.sharding import PartitionSpec as P

HEADS = 12
HEAD = 64
D = 768
FF = 3072
LAYERS = 2
MAXP = 2
STEPS = LAYERS * (MAXP + 1)
SMALL = 12

EPS = 1e-05
NEG = -1000000000.0
LOG2E = 1.4426950408889634
MESH = pl.DeviceIdType.MESH
VMEM_LIMIT = 63 * 2**20
F32 = jnp.float32
BF16 = jnp.bfloat16


def nn(a, b):
    return jnp.dot(a, b, preferred_element_type=F32)


def nt(a, b):
    return lax.dot_general(a, b, (((1,), (1,)), ((), ())), preferred_element_type=F32)


def tn(a, b):
    return lax.dot_general(a, b, (((0,), (0,)), ((), ())), preferred_element_type=F32)


def normalised(x):
    mean = jnp.mean(x, axis=-1, keepdims=True)
    centred = x - mean
    spread = jnp.mean(centred * centred, axis=-1, keepdims=True)
    inv = lax.rsqrt(spread + EPS)
    return centred * inv, inv


def norm_back(grad, gain, hat, inv):
    g = grad * gain
    mean_g = jnp.mean(g, axis=-1, keepdims=True)
    mean_gh = jnp.mean(g * hat, axis=-1, keepdims=True)
    return inv * (g - mean_g - hat * mean_gh)


def column_sum(x):
    return jnp.sum(x, axis=0, keepdims=True)


def of_head(h):
    p = h // 2
    at, atv = slice(p * 128, (p + 1) * 128), slice(D + p * 128, D + (p + 1) * 128)
    low = lax.broadcasted_iota(jnp.int32, (1, 128), 1) < HEAD
    return at, atv, low if h % 2 == 0 else jnp.logical_not(low)


def attention_forward(KV, Q, LSE, bias, O, before_values):
    def scores(h):
        at, _, keep = of_head(h)
        qp = Q[:, at]
        return nt(KV[:, at], jnp.where(keep, qp, jnp.zeros_like(qp)))

    def mixed(h, raw):
        _, atv, _ = of_head(h)
        logits = raw * LOG2E + bias[...]
        top = jnp.max(logits, axis=0, keepdims=True)
        expo = jnp.exp2(logits - top)
        denom = jnp.sum(expo, axis=0, keepdims=True)
        LSE[h // 2, h % 2 : h % 2 + 1, :] = top + jnp.log2(denom)
        return tn((expo * (1.0 / denom)).astype(BF16), KV[:, atv])

    ahead = scores(0)
    before_values()
    even = None
    for h in range(HEADS):
        raw = ahead
        if h + 1 < HEADS:
            ahead = scores(h + 1)
        out = mixed(h, raw)
        if h % 2 == 0:
            even = out
        else:
            at, _, high = of_head(h)
            O[:, at] = jnp.where(high, out, even).astype(BF16)


def attention_backward(KV, Q, LSE, bias, DO, DP, DKV, between):
    low_row = lax.broadcasted_iota(jnp.int32, (128, 1), 0) < HEAD

    def parts(h):
        at, atv, keep = of_head(h)
        qp, dop = Q[:, at], DO[:, at]
        zero = jnp.zeros_like(qp)
        return KV[:, at], KV[:, atv], jnp.where(keep, qp, zero), jnp.where(keep, dop, zero)

    def products(h):
        kp, vp, qe, doe = parts(h)
        return nt(kp, qe), nt(vp, doe)

    def grads(h, raw, dpr):
        lse = LSE[h // 2, h % 2 : h % 2 + 1, :]
        pr = jnp.exp2(raw * LOG2E + bias[...] - lse)
        inner = jnp.sum(pr * dpr, axis=0, keepdims=True)
        return pr.astype(BF16), (pr * (dpr - inner)).astype(BF16)

    def finish(h0, one, two):
        at, atv, _ = of_head(h0)
        kp, _, q0, do0 = parts(h0)
        _, _, q1, do1 = parts(h0 + 1)
        dqt = jnp.where(low_row, tn(kp, one[1]), tn(kp, two[1])) * 0.125
        DP[:, at] = dqt.T.astype(BF16)
        p = h0 // 2
        DKV[:, (2 * p + 1) * 128 : (2 * p + 2) * 128] = nn(
            jnp.concatenate([one[0], two[0]], axis=1), jnp.concatenate([do0, do1], axis=0)
        ).astype(BF16)
        DKV[:, 2 * p * 128 : (2 * p + 1) * 128] = nn(
            jnp.concatenate([one[1], two[1]], axis=1), jnp.concatenate([q0, q1], axis=0)
        ).astype(BF16)

    ahead = products(0)
    even = None
    for h in range(HEADS):
        now = ahead
        if h + 1 < HEADS:
            ahead = products(h + 1)
        pair = grads(h, *now)
        if h % 2 == 0:
            even = pair
        else:
            finish(h - 1, even, pair)
        if h in between:
            between[h]()


def merge_kv(DP, DKV, RDKV, off, half):
    tok = RDKV.shape[1]
    for j in range(2):
        for p in range(half * HEADS // 4, (half + 1) * HEADS // 4):
            at = slice(2 * p * 128, (2 * p + 2) * 128)
            both = (DKV[pl.ds(off[j], tok), at].astype(F32) + RDKV[j, :, at].astype(F32)).astype(BF16)
            DP[j * tok : (j + 1) * tok, D + p * 128 : D + (p + 1) * 128] = both[:, :128]
            DP[j * tok : (j + 1) * tok, 2 * D + p * 128 : 2 * D + (p + 1) * 128] = both[:, 128:]


def row_of(layer, k):
    return slice(layer * SMALL + k, layer * SMALL + k + 1)


class Plan:
    def __init__(self, ngrp, nrow, tok):
        self.ngrp, self.nrow, self.tok = ngrp, nrow, tok
        self.ncol = ngrp // 2
        self.bits = max(self.ncol.bit_length() - 1, 0)
        self.ndev = ngrp * nrow
        self.ch = D // self.ndev
        self.chp = -(-self.ch // 8) * 8
        self.cf = FF // self.ndev
        self.rows = self.ncol * 2 * self.chp
        self.nsel = 2 * self.rows
        self.wide = FF // ngrp
        self.per = D // (2 * self.wide)
        self.frows = self.ncol * 2 * self.cf
        dims = list(range(self.bits))[::-1] + [-1]
        turns = [k * len(dims) // 3 for k in range(3)]
        self.orders = [dims[t:] + dims[:t] for t in turns]

    def piece(self, order, index):
        col, pair = 0, 0
        for place, dim in enumerate(order):
            bit = (index >> (len(order) - 1 - place)) & 1
            if dim < 0:
                pair = bit
            else:
                col |= bit << dim
        return col, pair

    def moved(self, turn):
        first = {self.piece(self.orders[0], k): k for k in range(2 * self.ncol)}
        return [first[self.piece(self.orders[turn], k)] for k in range(2 * self.ncol)]

    def fill_selectors(self, sel, c, half):
        def ones(first, rows, used):
            feature = lax.broadcasted_iota(jnp.int32, (rows, D), 1)
            place = lax.broadcasted_iota(jnp.int32, (rows, D), 0)
            return jnp.where((feature == first + place) & (place < used), 1.0, 0.0)

        for side, core in enumerate((c, 1 - c)):
            for index in range(0, 2 * self.ncol, 2):
                two = []
                for k in (index, index + 1):
                    col, pair = self.piece(self.orders[0], k)
                    two.append(ones(((col * 2 + core) * 4 + 2 * half + pair) * self.ch, self.chp, self.ch))
                row = side * self.rows + index * self.chp
                sel[0, row : row + 2 * self.chp, :] = jnp.concatenate(two, axis=0).astype(BF16)
            for j in range(self.per):
                row = side * (D // 4) + j * 2 * self.cf
                first = (j * 2 + core) * self.wide + half * 2 * self.cf
                sel[1, row : row + 2 * self.cf, :] = ones(first, 2 * self.cf, 2 * self.cf).astype(BF16)


def where_am_i():
    g = lax.axis_index("grp")
    z = lax.axis_index("row")
    c = lax.rem(g, 2)
    col = lax.div(g, 2)
    outer = jnp.logical_or(z == 0, z == 3)
    parity = jnp.where(outer, 0, 1)
    return g, z, c, col, outer, parity


def fill_bias(bias, starts, c, tok):
    T = 2 * tok
    lane = lax.broadcasted_iota(jnp.int32, (1, T), 1)
    qpos = jnp.where(lane < tok, c * tok + lane, (3 - c) * tok + lane - tok).astype(F32)
    begin = jnp.zeros((1, T), F32)
    for start in starts:
        begin = jnp.maximum(begin, jnp.where(qpos >= start, start, 0.0))
    kpos = lax.broadcasted_iota(jnp.int32, (2 * T, T), 0).astype(F32)
    bias[...] = jnp.where((kpos <= qpos) & (kpos >= begin), 0.0, NEG)


def main_kernel(
    plan,
    x_own, cot_own, pass_ref, doc_ref, tok_ref, ln1g, ln1b, qb, vb, ob, ln2g, ln2b, ub, db,
    wq_h, wo_h, wu_h, wd_h,
    hid_o, up_o, vec_o, tot_o, asel_h, osel_h, usel_h, gsel_h, dp_h, dy_h, df_h, dr_h,
    sx_h, sq_h, skv_h, slse_h, sm_h, sgp_h,
    wq, wo, wu, wd, sel, xin, cot, par_ref, par_in, tsend, trecv,
    bias, X, Q, KV, LSE, M, GP, O, GF, XN, asel, osel, usel, gsel,
    R, U, DKV, RDKV, DP, DR, DY, VAC, ret_s, ret_r,
    w_sem, in_send, in_recv, cot_send, cot_recv, par_sem, t_sem, kv_send, kv_recv,
    st_sem, ld_sem, sel_out, dkv_send, dkv_recv, bst_sem, ret_send, ret_recv,
):
    tok = plan.tok
    T = 2 * tok
    g, z, c, col, outer, parity = where_am_i()
    half = lax.div(z, 2)
    peer = (col * 2 + 1 - c, z)
    off_lo = pl.multiple_of(c * tok, tok)
    off_hi = pl.multiple_of((3 - c) * tok, tok)
    poff_lo = pl.multiple_of((1 - c) * tok, tok)
    poff_hi = pl.multiple_of((2 + c) * tok, tok)

    weight_copies = []
    for l in range(LAYERS):
        for i, (src, dst) in enumerate(((wq_h, wq), (wo_h, wo), (wu_h, wu), (wd_h, wd))):
            weight_copies.append(pltpu.make_async_copy(src.at[l], dst.at[l], w_sem.at[l, i]))
    weight_copies[0].start()
    numbers = [pass_ref[0], tok_ref[0]] + [doc_ref[0, k] for k in range(4)] + [0, 0]
    for k, number in enumerate(numbers):
        par_ref[k : k + 1, :] = jnp.full((1, 128), number, jnp.int32).astype(F32)

    barrier = pltpu.get_barrier_semaphore()
    count = 0
    for dc in range(2):
        for dz in range(plan.nrow):
            if dc == 0 and dz == 0:
                continue
            target = (col * 2 + lax.rem(c + dc, 2), lax.rem(z + dz, plan.nrow))
            pl.semaphore_signal(barrier, inc=1, device_id=target, device_id_type=MESH)
            count += 1
    others = [(col ^ (1 << b)) * 2 + c for b in range(plan.bits)]
    for other in others:
        pl.semaphore_signal(barrier, inc=1, device_id=(other, z), device_id_type=MESH)
        count += 1
    pl.semaphore_wait(barrier, count)

    block_core = jnp.where(outer, 0, 1)
    slot_in = lax.div(z, 2)
    send_list = []
    for i in range(2):
        zt = jnp.where(c == 0, 3 * i, 1 + i)
        is_self = jnp.logical_and(c == block_core, zt == z)
        send_list.append((i, zt, is_self))

    def deliver(src, dst, send, recv):
        for i, zt, is_self in send_list:

            @pl.when(is_self)
            def _():
                pltpu.make_async_copy(src, dst.at[slot_in], recv.at[slot_in]).start()

            @pl.when(jnp.logical_not(is_self))
            def _():
                pltpu.make_async_remote_copy(
                    src_ref=src, dst_ref=dst.at[slot_in], send_sem=send.at[i], recv_sem=recv.at[slot_in],
                    device_id=(col * 2 + block_core, zt), device_id_type=MESH,
                ).start()

    def deliver_sent(src, dst, send, recv):
        for i, zt, is_self in send_list:

            @pl.when(jnp.logical_not(is_self))
            def _():
                pltpu.make_async_remote_copy(
                    src_ref=src, dst_ref=dst.at[slot_in], send_sem=send.at[i], recv_sem=recv.at[slot_in],
                    device_id=(col * 2 + block_core, zt), device_id_type=MESH,
                ).wait_send()

    def deliver_wait(src, dst, recv):
        for i in range(2):
            pltpu.make_async_copy(src, dst.at[i], recv.at[i]).wait()

    deliver(x_own, xin, in_send, in_recv)

    par_copy = pltpu.make_async_remote_copy(
        src_ref=par_ref, dst_ref=par_in, send_sem=par_sem.at[0], recv_sem=par_sem.at[1],
        device_id=peer, device_id_type=MESH,
    )
    par_copy.start()
    for cp in weight_copies[1:]:
        cp.start()
    par_copy.wait()
    served = jnp.where(parity == c, par_ref[...], par_in[...])
    tcount = par_ref[1:2, :] + par_in[1:2, :]
    total = jnp.broadcast_to(tcount, (8, 128))
    for b in range(plan.bits):
        tsend[b] = total
        cp = pltpu.make_async_remote_copy(
            src_ref=tsend.at[b], dst_ref=trecv.at[b], send_sem=t_sem.at[0, b], recv_sem=t_sem.at[1, b],
            device_id=(others[b], z), device_id_type=MESH,
        )
        cp.start()
        cp.wait()
        total = total + trecv[b]
    factor = served[1:2, :] / total[0:1, :]
    tot_o[0:1, :] = factor
    tot_o[1:8, :] = jnp.concatenate([served[0:1, :], served[2:8, :]], axis=0)
    passes = served[0:1, 0:1]

    fill_bias(bias, [served[2 + k : 3 + k, 0:1] for k in range(4)], c, tok)
    VAC[...] = jnp.zeros_like(VAC)
    for cp in weight_copies:
        cp.wait()
    plan.fill_selectors(sel, c, half)

    deliver_wait(x_own, xin, in_recv)
    deliver_sent(x_own, xin, in_send, in_recv)
    XN[0:tok] = xin[0].astype(F32)
    XN[tok:T] = xin[1].astype(F32)
    deliver(cot_own, cot, cot_send, cot_recv)

    def stash_copies(s, slot, sem, back):
        pairs = ((X, sx_h), (Q, sq_h), (LSE, slse_h), (M, sm_h), (GP, sgp_h))
        out = []
        for i, (v, h) in enumerate(pairs):
            if back:
                out.append(pltpu.make_async_copy(h.at[s], v.at[slot], sem.at[slot, i]))
            else:
                out.append(pltpu.make_async_copy(v.at[slot], h.at[s], sem.at[slot, i]))
        return out

    def kv_stash(s, slot):
        return pltpu.make_async_copy(KV.at[slot], skv_h.at[s], st_sem.at[slot, 5])

    def kv_load(s, slot):
        return pltpu.make_async_copy(skv_h.at[s], KV.at[slot], ld_sem.at[slot, 5])

    def sel_copies_out(l, sect):
        at = pl.ds(pl.multiple_of(sect * T, T), T)
        return [
            pltpu.make_async_copy(asel, asel_h.at[l, :, at], sel_out.at[0]),
            pltpu.make_async_copy(osel, osel_h.at[l, :, at], sel_out.at[1]),
            pltpu.make_async_copy(usel, usel_h.at[l, :, at], sel_out.at[2]),
            pltpu.make_async_copy(gsel, gsel_h.at[l, :, at], sel_out.at[3]),
        ]

    def kv_moves(slot, offsets):
        out = []
        for part in range(2):
            out.append([])
            for i, off in enumerate(offsets):
                ref = KV.at[slot, pl.ds(off, tok), part * D : (part + 1) * D]
                out[part].append(
                    pltpu.make_async_remote_copy(
                        src_ref=ref, dst_ref=ref, send_sem=kv_send.at[slot, part, i],
                        recv_sem=kv_recv.at[slot, part, i], device_id=peer, device_id_type=MESH,
                    )
                )
        return out

    def kv_copies(slot):
        return kv_moves(slot, (off_lo, off_hi))

    def kv_arrivals(slot):
        return kv_moves(slot, (poff_lo, poff_hi))

    def forward(sect, l):
        s = sect * LAYERS + l
        slot = l

        @pl.when(sect >= 1)
        def _():
            for cp in stash_copies(s - 2, slot, st_sem, False):
                cp.wait()

        x = XN[...]
        X[slot] = x
        hat, _ = normalised(x)
        a = (hat * ln1g[l : l + 1, :] + ln1b[l : l + 1, :]).astype(BF16)

        def own_rows(values, at):
            KV[slot, pl.ds(off_lo, tok), at] = values[:tok]
            KV[slot, pl.ds(off_hi, tok), at] = values[tok:]

        sends = kv_copies(slot)
        arrivals = kv_arrivals(slot)
        own_rows(nn(a, wq[l, :, D : 2 * D]).astype(BF16), slice(0, D))
        for cp in sends[0]:
            cp.start()
        own_rows((nn(a, wq[l, :, 2 * D : 3 * D]) + vb[l : l + 1, :]).astype(BF16), slice(D, 2 * D))
        for cp in sends[1]:
            cp.start()
        q = (nn(a, wq[l, :, 0:D]) + qb[l : l + 1, :]).astype(BF16)
        Q[slot] = q * jnp.asarray(0.125, BF16)

        def rows_of_before():
            for cp in sel_copies_out(0, 0):
                cp.wait()

        if l == 0:
            pl.when(sect >= 1)(rows_of_before)
        else:
            rows_of_before()
        asel[...] = nt(sel[0], a).astype(BF16)
        for cp in arrivals[0]:
            cp.wait_recv()

        def values_here():
            for cp in arrivals[1]:
                cp.wait_recv()
            for cp in sends[0] + sends[1]:
                cp.wait_send()

            @pl.when(sect < MAXP)
            def _():
                kv_stash(s, slot).start()

        attention_forward(KV.at[slot], Q.at[slot], LSE.at[slot], bias, O, values_here)
        o = O[...]
        osel[...] = nt(sel[0], o).astype(BF16)
        m = x + (nn(o, wo[l]) + ob[l : l + 1, :])
        M[slot] = m
        hat2, _ = normalised(m)
        a2 = (hat2 * ln2g[l : l + 1, :] + ln2b[l : l + 1, :]).astype(BF16)
        usel[...] = nt(sel[0], a2).astype(BF16)

        for j in range(FF // D):
            js = slice(j * D, (j + 1) * D)
            f = nn(a2, wu[l, :, js]) + ub[l : l + 1, js]
            f2 = f * f
            u = f * (0.7978845608028654 + 0.035677408136300125 * f2)
            t = jnp.tanh(u)
            h = 0.5 + 0.5 * t
            ga = f * h
            gp = h + ga * (1.0 - h) * (1.5957691216057308 + 0.21406444881780074 * f2)
            gb = ga.astype(BF16)
            GF[:, js] = gb
            GP[slot, :, js] = gp.astype(BF16)
            n = D // 4
            gs = nt(sel[1, : 2 * n], gb).astype(BF16)
            for cc in range(2):
                gsel[cc * plan.frows + j * n : cc * plan.frows + (j + 1) * n] = gs[cc * n : (cc + 1) * n]

        y = m + (nn(GF[...], wd[l]) + db[l : l + 1, :])
        if l == LAYERS - 1:
            bar = jnp.where(sect < MAXP, sect, -1).astype(F32)
            y = jnp.where(passes > bar, y, X[0])
        XN[...] = y

        @pl.when(sect < MAXP)
        def _():
            for cp in stash_copies(s, slot, st_sem, False):
                cp.start()
            kv_stash(s, slot).wait()

        for cp in sel_copies_out(l, sect):
            cp.start()

    def forward_section(sect, carry):
        for l in range(LAYERS):
            forward(sect, l)
        return carry

    lax.fori_loop(0, MAXP + 1, forward_section, 0)

    block = jnp.where(z < 2, c, 3 - c)
    owner = (col * 2 + parity, block)
    mine = jnp.logical_and(parity == c, block == z)

    ret_recv_wait = pltpu.make_async_copy(ret_s, ret_r, ret_recv.at[0])
    ret_remote = pltpu.make_async_remote_copy(
        src_ref=ret_s, dst_ref=ret_r, send_sem=ret_send.at[0], recv_sem=ret_recv.at[0],
        device_id=owner, device_id_type=MESH,
    )

    @pl.when(z < 2)
    def _():
        ret_s[...] = XN[0:tok]

    @pl.when(z >= 2)
    def _():
        ret_s[...] = XN[tok:T]

    @pl.when(mine)
    def _():
        ret_recv_wait.start()

    @pl.when(jnp.logical_not(mine))
    def _():
        ret_remote.start()

    deliver_wait(cot_own, cot, cot_recv)
    deliver_sent(cot_own, cot, cot_send, cot_recv)
    U[0:tok] = cot[0]
    U[tok:T] = cot[1]
    for cp in sel_copies_out(0, 0):
        cp.wait()

    def back_copies(l, sect):
        at = pl.ds(pl.multiple_of(sect * T, T), T)
        return [
            pltpu.make_async_copy(DP, dp_h.at[l, at, :], bst_sem.at[0]),
            pltpu.make_async_copy(DY, dy_h.at[l, at, :], bst_sem.at[1]),
            pltpu.make_async_copy(GF, df_h.at[l, at, :], bst_sem.at[2]),
            pltpu.make_async_copy(DR, dr_h.at[l, at, :], bst_sem.at[3]),
        ]

    def dkv_copies(slot, half):
        at = slice(half * D, (half + 1) * D)
        return [
            pltpu.make_async_remote_copy(
                src_ref=DKV.at[pl.ds(off, tok), at], dst_ref=RDKV.at[slot, i, :, at],
                send_sem=dkv_send.at[slot, half, i], recv_sem=dkv_recv.at[slot, half, i],
                device_id=peer, device_id_type=MESH,
            )
            for i, off in enumerate((poff_lo, poff_hi))
        ]

    def backward(i, l):
        sect = MAXP - i
        s = sect * LAYERS + l
        slot = l

        def stored():
            for cp in back_copies(0, 0):
                cp.wait()

        if i >= 1 or l < LAYERS - 1:
            stored()
        if i >= 1:
            for cp in stash_copies(s, slot, ld_sem, True):
                cp.wait()
            kv_load(s, slot).wait()

        active = jnp.where(passes > (-1.0 if sect == MAXP else float(sect)), jnp.ones((1, 1), F32), jnp.zeros((1, 1), F32))
        r = U[...] * active if l == LAYERS - 1 else R[...]
        dr = r.astype(BF16)
        DR[...] = dr
        VAC[row_of(l, 7)] += column_sum(dr.astype(F32))
        for j in range(FF // D):
            js = slice(j * D, (j + 1) * D)
            dg = nt(dr, wd[l, js, :])
            df = (dg * GP[slot, :, js].astype(F32)).astype(BF16)
            GF[:, js] = df
            VAC[row_of(l, 8 + j)] += column_sum(df.astype(F32))
        da2 = nt(GF[...], wu[l])
        hat2, inv2 = normalised(M[slot])
        VAC[row_of(l, 5)] += column_sum(da2 * hat2)
        VAC[row_of(l, 6)] += column_sum(da2)
        dm = r + norm_back(da2, ln2g[l : l + 1, :], hat2, inv2)
        R[...] = dm
        dy = dm.astype(BF16)
        DY[...] = dy
        VAC[row_of(l, 4)] += column_sum(dy.astype(F32))
        O[...] = nt(dy, wo[l]).astype(BF16)

        def send_half(half):
            for cp in dkv_copies(slot, half):
                cp.start()

        attention_backward(
            KV.at[slot], Q.at[slot], LSE.at[slot], bias, O, DP, DKV,
            {HEADS // 2 - 1: lambda: send_half(0), HEADS - 1: lambda: send_half(1)},
        )
        x = X[slot]
        hat, inv = normalised(x)

        if i == 0:
            for cp in stash_copies(s - 2, slot, ld_sem, True):
                cp.start()
            kv_load(s - 2, slot).start()

        dqb = DP[:, 0:D]
        VAC[row_of(l, 2)] += column_sum(dqb.astype(F32))
        da = nt(dqb, wq[l, :, 0:D])
        for half in range(2):
            for cp in dkv_copies(slot, half):
                cp.wait()
            merge_kv(DP, DKV, RDKV.at[slot], (off_lo, off_hi), half)
        dkv = DP[:, D : 3 * D]
        VAC[row_of(l, 3)] += column_sum(dkv[:, D:].astype(F32))
        da = da + nt(dkv, wq[l, :, D : 3 * D])
        VAC[row_of(l, 0)] += column_sum(da * hat)
        VAC[row_of(l, 1)] += column_sum(da)
        new = R[...] + norm_back(da, ln1g[l : l + 1, :], hat, inv)
        if l == 0:
            U[...] = new + (1.0 - active) * U[...]
        else:
            R[...] = new
        for cp in back_copies(l, sect):
            cp.start()

    for i in range(MAXP):
        for l in range(LAYERS - 1, -1, -1):
            backward(i, l)
    ret_recv_wait.wait()

    @pl.when(jnp.logical_not(mine))
    def _():
        ret_remote.wait_send()

    hid_o[...] = ret_r[...]
    up_o[...] = U[...]
    vec_o[...] = VAC[...]
    for cp in back_copies(0, 0):
        cp.wait()


def run_main(plan, x, cot, numbers, vecs, weights):
    tok = plan.tok
    T = 2 * tok
    L = 4 * tok
    vmem = pl.BlockSpec(memory_space=pltpu.VMEM)
    hbm = pl.BlockSpec(memory_space=pl.ANY)
    smem = pl.BlockSpec(memory_space=pltpu.SMEM)
    S = jax.ShapeDtypeStruct
    K = (MAXP + 1) * T
    outs = [
        (S((tok, D), F32), vmem),
        (S((T, D), F32), vmem),
        (S((LAYERS * SMALL, D), F32), vmem),
        (S((8, 128), F32), vmem),
        (S((LAYERS, plan.nsel, K), BF16), hbm),
        (S((LAYERS, plan.nsel, K), BF16), hbm),
        (S((LAYERS, plan.nsel, K), BF16), hbm),
        (S((LAYERS, 2 * plan.frows, K), BF16), hbm),
        (S((LAYERS, K, 3 * D), BF16), hbm),
        (S((LAYERS, K, D), BF16), hbm),
        (S((LAYERS, K, FF), BF16), hbm),
        (S((LAYERS, K, D), BF16), hbm),
        (S((STEPS, T, D), F32), hbm),
        (S((STEPS, T, D), BF16), hbm),
        (S((STEPS, L, 2 * D), BF16), hbm),
        (S((STEPS, 8, 8, T), F32), hbm),
        (S((STEPS, T, D), F32), hbm),
        (S((STEPS, T, FF), BF16), hbm),
    ]
    V = pltpu.VMEM
    DMA = pltpu.SemaphoreType.DMA
    nb = max(plan.bits, 1)
    scratch = [
        V((LAYERS, D, 3 * D), BF16), V((LAYERS, D, D), BF16), V((LAYERS, D, FF), BF16), V((LAYERS, FF, D), BF16),
        V((2, plan.nsel, D), BF16), V((2, tok, D), BF16), V((2, tok, D), F32), V((8, 128), F32), V((8, 128), F32),
        V((nb, 8, 128), F32), V((nb, 8, 128), F32),
        V((L, T), F32),
        V((2, T, D), F32), V((2, T, D), BF16), V((2, L, 2 * D), BF16), V((2, 8, 8, T), F32), V((2, T, D), F32),
        V((2, T, FF), BF16), V((T, D), BF16), V((T, FF), BF16), V((T, D), F32),
        V((plan.nsel, T), BF16), V((plan.nsel, T), BF16), V((plan.nsel, T), BF16), V((2 * plan.frows, T), BF16),
        V((T, D), F32), V((T, D), F32), V((L, 2 * D), BF16), V((2, 2, tok, 2 * D), BF16), V((T, 3 * D), BF16),
        V((T, D), BF16), V((T, D), BF16), V((LAYERS * SMALL, D), F32), V((tok, D), F32), V((tok, D), F32),
        DMA((LAYERS, 4)), DMA((2,)), DMA((2,)), DMA((2,)), DMA((2,)), DMA((2,)), DMA((2, nb)),
        DMA((2, 2, 2)), DMA((2, 2, 2)), DMA((2, 6)), DMA((2, 6)), DMA((4,)), DMA((2, 2, 2)), DMA((2, 2, 2)), DMA((4,)),
        DMA((1,)), DMA((1,)),
    ]
    call = pl.pallas_call(
        functools.partial(main_kernel, plan),
        out_shape=[o[0] for o in outs],
        out_specs=[o[1] for o in outs],
        in_specs=[vmem] * 2 + [smem] * 3 + [vmem] * 9 + [hbm] * 4,
        scratch_shapes=scratch,
        compiler_params=pltpu.CompilerParams(
            collective_id=0, has_side_effects=True, vmem_limit_bytes=VMEM_LIMIT
        ),
        name="layers",
    )
    return call(x, cot, *numbers, *vecs, *weights)


def fold(x):
    n = x.shape[1] // 2
    return jnp.concatenate([x[:, :n], x[:, n:]], axis=0)


def unfold(x):
    n = x.shape[0] // 2
    return jnp.concatenate([x[:n], x[n:]], axis=1)


class Item:
    def __init__(self, name, rows, cols, chunk):
        self.name, self.rows, self.cols, self.chunk = name, rows, cols, chunk

    def part(self, k):
        return slice(k * self.cols // 3, (k + 1) * self.cols // 3)

    def half_part(self, k):
        return slice(k * self.cols // 6, (k + 1) * self.cols // 6)


def items_of(plan):
    return [
        Item("down", plan.frows, D, plan.cf),
        Item("up", plan.rows, FF, plan.chp),
        Item("out", plan.rows, D, plan.chp),
        Item("qkv", plan.rows, 3 * D, plan.chp),
    ]


def last_kernel(
    plan,
    up_h, vec_ref, tot_ref, ln1g, ln2g, asel_h, osel_h, usel_h, gsel_h, dp_h, dy_h, df_h, dr_h,
    sx_h, sq_h, skv_h, slse_h, sm_h, sgp_h, wq_h, wo_h, wu_h, wd_h,
    *refs,
):
    items = items_of(plan)
    n = len(items)
    outs, gin_o, vec_o, refs = refs[:n], refs[n], refs[n + 1], refs[n + 2 :]
    lhs, rhs, refs = refs[:n], refs[n : 2 * n], refs[2 * n :]
    OW, CR, refs = refs[:n], refs[n : 2 * n], refs[2 * n :]
    stages = plan.bits + 1
    RB = []
    for k in range(stages - 1):
        RB.append(refs[:n])
        refs = refs[n:]
    FS, FR, refs = refs[:n], refs[n : 2 * n], refs[2 * n :]
    (
        ST, wq, wo, wu, wd, Q, KV, LSE, XM, GP, bias, R, DKV, RDKV, ret_r, vs, vr,
        l_sem, w_sem, s_sem, chip_sem, stage_sem, vec_sem, dkv_sem, ret_sem, up_sem,
    ) = refs
    tok = plan.tok
    T = 2 * tok
    g, z, c, col, outer, parity = where_am_i()
    peer = (col * 2 + 1 - c, z)
    off = [pl.multiple_of(c * tok, tok), pl.multiple_of((3 - c) * tok, tok)]
    poff = [pl.multiple_of((1 - c) * tok, tok), pl.multiple_of((2 + c) * tok, tok)]
    DOWN, UP, OUT, QKV = range(n)
    sources = ((gsel_h, dr_h), (usel_h, df_h), (osel_h, dy_h), (asel_h, dp_h))
    DR, GF, DY, DP = [r.at[0:T] for r in rhs]
    DO = DY
    blocks = FF // D
    rows4 = items[DOWN].rows // blocks
    staged = [ST.at[0:rows4, :], ST, ST.at[:, 3 * D :], ST.at[:, : 3 * D]]

    def operand_loads(l, i):
        a, b = sources[i]
        later = pl.ds(T, rhs[i].shape[0] - T)
        return (
            pltpu.make_async_copy(a.at[l], lhs[i], l_sem.at[i, 0]),
            pltpu.make_async_copy(b.at[l, later, :], rhs[i].at[later, :], l_sem.at[i, 1]),
        )

    weight_refs = {"wd": (wd_h, wd, 0), "wu": (wu_h, wu, 1), "wo": (wo_h, wo, 2), "wq": (wq_h, wq, 3)}
    slot_refs = {
        "GP": (sgp_h, GP, 0), "M": (sm_h, XM, 1), "Q": (sq_h, Q, 2), "KV": (skv_h, KV, 3), "LSE": (slse_h, LSE, 4),
        "X": (sx_h, XM, 5),
    }

    def load(l, *names):
        out = []
        for name in names:
            if name in weight_refs:
                h, v, k = weight_refs[name]
                out.append(pltpu.make_async_copy(h.at[l], v, w_sem.at[k]))
            else:
                h, v, k = slot_refs[name]
                out.append(pltpu.make_async_copy(h.at[l], v, s_sem.at[k]))
        return out

    def start(copies):
        for cp in copies:
            cp.start()

    def wait(copies):
        for cp in copies:
            cp.wait()

    top_layer = LAYERS - 1
    up_load = pltpu.make_async_copy(up_h, R, up_sem.at[0])
    up_load.start()
    start(operand_loads(top_layer, DOWN))
    start(load(top_layer, "wd", "GP"))

    def partner(dim):
        if dim < 0:
            return (g, z + 1 - 2 * lax.rem(z, 2))
        return ((col ^ (1 << dim)) * 2 + c, z)

    def bit_of(dim):
        if dim < 0:
            return lax.rem(z, 2)
        return lax.rem(lax.div(col, 1 << dim), 2)

    dims = [-1] + list(range(plan.bits))
    block = jnp.where(z < 2, c, 3 - c)
    owner = (col * 2 + parity, block)
    mine = jnp.logical_and(parity == c, block == z)
    barrier = pltpu.get_barrier_semaphore()
    count = 0
    for dc in range(2):
        for dz in range(plan.nrow):
            if dc == 0 and dz == 0:
                continue
            target = (col * 2 + lax.rem(c + dc, 2), lax.rem(z + dz, plan.nrow))
            pl.semaphore_signal(barrier, inc=1, device_id=target, device_id_type=MESH)
            count += 1
    for dim in dims[1:]:
        pl.semaphore_signal(barrier, inc=1, device_id=partner(dim), device_id_type=MESH)
        count += 1
    pl.semaphore_wait(barrier, count)

    factor = tot_ref[0:1, 0:1]
    active = jnp.where(tot_ref[1:2, 0:1] > 0.0, jnp.ones((1, 1), F32), jnp.zeros((1, 1), F32))
    fill_bias(bias, [tot_ref[2 + k : 3 + k, 0:1] for k in range(4)], c, tok)

    def chip_copy(l, i):
        return pltpu.make_async_remote_copy(
            src_ref=staged[i], dst_ref=CR[i], send_sem=chip_sem.at[0, i], recv_sem=chip_sem.at[1, i],
            device_id=peer, device_id_type=MESH,
        )

    def base_of(i, order, k):
        base, rows = 0, items[i].rows
        for j in range(k):
            rows //= 2
            base = base + bit_of(order[j]) * rows
        return base, rows

    def stage_copy(l, i, k, part):
        item, order = items[i], plan.orders[part]
        if k == stages - 1:
            at = item.half_part(part)
            src, dst = FS[i].at[:, at], FR[i].at[l, :, at]
        else:
            base, rows = base_of(i, order, k)
            rows //= 2
            first = base + (1 - bit_of(order[k])) * rows
            at = item.part(part)
            src, dst = OW[i].at[l, pl.ds(pl.multiple_of(first, 16), rows), at], RB[k][i].at[l, :, at]
        return pltpu.make_async_remote_copy(
            src_ref=src, dst_ref=dst, send_sem=stage_sem.at[0, l, i, k, part],
            recv_sem=stage_sem.at[1, l, i, k, part], device_id=partner(order[k]), device_id_type=MESH,
        )

    def add_rows(total, base, more, rows):
        step = 32 if rows % 32 == 0 else 16

        def add(b, carry):
            at = pl.ds(pl.multiple_of(base + b * step, 16), step)
            other = more[pl.ds(pl.multiple_of(b * step, 16), step), :]
            total[at, :] = (total[at, :].astype(F32) + other.astype(F32)).astype(BF16)
            return carry

        lax.fori_loop(0, rows // step, add, 0)

    def product(l, i):
        wait(operand_loads(l, i))
        item = items[i]
        e = item.chunk
        for part in range(3):
            cols = item.part(part)
            place = plan.moved(part)
            r = nn(lhs[i][...], rhs[i][:, cols]) * factor
            for core in range(2):
                pieces = [r[core * item.rows + k * e : core * item.rows + (k + 1) * e] for k in place]
                r_core = jnp.concatenate(pieces, axis=0).astype(BF16)
                if core == 0:
                    OW[i][l, :, cols] = r_core
                elif i == DOWN:
                    for b in range(blocks):
                        at = slice(b * D + cols.start, b * D + cols.stop)
                        staged[i][:, at] = r_core[b * rows4 : (b + 1) * rows4]
                else:
                    staged[i][:, cols] = r_core
        if l > 0:
            start(operand_loads(l - 1, i))
        chip_copy(l, i).start()

    def after_chip(l, i):
        chip_copy(l, i).wait()
        if i == DOWN:
            for b in range(blocks):
                add_rows(OW[i].at[l], b * rows4, CR[i].at[:, b * D : (b + 1) * D], rows4)
        else:
            add_rows(OW[i].at[l], 0, CR[i], items[i].rows)
        for part in range(3):
            stage_copy(l, i, 0, part).start()

    def after_stage(l, i, k):
        item = items[i]
        own = outs[i].shape[1]
        for part in range(3):
            order, cols = plan.orders[part], item.part(part)
            stage_copy(l, i, k, part).wait()
            if k == stages - 1:
                outs[i][l, :, cols] += unfold(FR[i][l, :, item.half_part(part)].astype(F32))[:own]
                continue
            base, rows = base_of(i, order, k + 1)
            if k + 1 == stages - 1:
                at = pl.ds(pl.multiple_of(base, 16), rows)
                both = OW[i][l, at, cols].astype(F32) + RB[k][i][l, :, cols].astype(F32)
                rows //= 2
                first = bit_of(order[k + 1]) == 0
                outs[i][l, :, cols] = jnp.where(first, both[:rows], both[rows:])[:own]
                FS[i][:, item.half_part(part)] = fold(jnp.where(first, both[rows:], both[:rows])).astype(BF16)
            else:
                add_rows(OW[i].at[l, :, cols], base, RB[k][i].at[l, :, cols], rows)
            stage_copy(l, i, k + 1, part).start()

    def dkv_copies(part):
        at = slice(part * D, (part + 1) * D)
        return [
            pltpu.make_async_remote_copy(
                src_ref=DKV.at[pl.ds(poff[j], tok), at], dst_ref=RDKV.at[j, :, at],
                send_sem=dkv_sem.at[0, part, j], recv_sem=dkv_sem.at[1, part, j],
                device_id=peer, device_id_type=MESH,
            )
            for j in range(2)
        ]

    vec_o[...] = vec_ref[...]

    def backward(l, marks):
        def mark(name):
            for f in marks.get(name, ()):
                f()

        def reload(*names):
            if l > 0:
                start(load(l - 1, *names))

        r = R[...]
        dr = r.astype(BF16)
        DR[...] = dr
        vec_o[row_of(l, 7)] += column_sum(dr.astype(F32))
        product(l, DOWN)
        if l == top_layer:
            start(operand_loads(l, UP))
            start(load(l, "wu", "M"))
        mark("down")
        wait(load(l, "wd", "GP"))
        for j in range(FF // D):
            js = slice(j * D, (j + 1) * D)
            dg = nt(dr, wd[js, :])
            df = (dg * GP[:, js].astype(F32)).astype(BF16)
            GF[:, js] = df
            vec_o[row_of(l, 8 + j)] += column_sum(df.astype(F32))
        reload("wd", "GP")
        if l == top_layer:
            start(operand_loads(l, OUT))
            start(load(l, "wo", "Q", "KV", "LSE"))
        mark("df")
        product(l, UP)
        if l == top_layer:
            start(load(l, "wq"))
            start(operand_loads(l, QKV))
        mark("up")
        wait(load(l, "wu", "M"))
        da2 = nt(GF[...], wu[...])
        hat2, inv2 = normalised(XM[...])
        vec_o[row_of(l, 5)] += column_sum(da2 * hat2)
        vec_o[row_of(l, 6)] += column_sum(da2)
        dm = r + norm_back(da2, ln2g[l : l + 1, :], hat2, inv2)
        R[...] = dm
        dy = dm.astype(BF16)
        DY[...] = dy
        vec_o[row_of(l, 4)] += column_sum(dy.astype(F32))
        start(load(l, "X"))
        reload("wu")
        mark("dy")
        product(l, OUT)
        wait(load(l, "wo", "Q", "KV", "LSE"))
        DO[...] = nt(dy, wo[...]).astype(BF16)
        reload("wo")
        def first_half():
            start(dkv_copies(0))
            mark("half")

        attention_backward(
            KV, Q, LSE, bias, DO, DP, DKV,
            {HEADS // 2 - 1: first_half, HEADS - 1: lambda: start(dkv_copies(1))},
        )
        reload("Q", "KV", "LSE")
        mark("attention")
        wait(load(l, "X", "wq"))
        hat, inv = normalised(XM[...])
        if l == 0:
            up_again.start()
        else:
            reload("M")
        dqb = DP[:, 0:D]
        vec_o[row_of(l, 2)] += column_sum(dqb.astype(F32))
        da = nt(dqb, wq[:, 0:D])
        for part in range(2):
            for cp in dkv_copies(part):
                cp.wait()
            merge_kv(DP, DKV, RDKV, off, part)
        product(l, QKV)
        mark("qkv")
        dkv = DP[:, D : 3 * D]
        vec_o[row_of(l, 3)] += column_sum(dkv[:, D:].astype(F32))
        da = da + nt(dkv, wq[:, D : 3 * D])
        reload("wq")
        vec_o[row_of(l, 0)] += column_sum(da * hat)
        vec_o[row_of(l, 1)] += column_sum(da)
        new = R[...] + norm_back(da, ln1g[l : l + 1, :], hat, inv)
        if l == 0:
            up_again.wait()
            new = (new + (1.0 - active) * XM[...]) * factor
        R[...] = new
        mark("end")

    up_again = pltpu.make_async_copy(up_h, XM, up_sem.at[0])

    done = set()

    def chip(l, i):
        return lambda: after_chip(l, i)

    def stage(l, i, k):
        done.add((l, i, k))
        return lambda: after_stage(l, i, k)

    up_load.wait()
    R[...] = R[...] * active
    backward(1, {
        "df": [chip(1, DOWN)],
        "dy": [chip(1, UP)],
        "half": [chip(1, OUT), stage(1, DOWN, 0)],
        "end": [chip(1, QKV), stage(1, UP, 0)],
    })
    backward(0, {
        "down": [stage(1, DOWN, 1), stage(1, OUT, 0)],
        "df": [chip(0, DOWN)],
        "up": [stage(1, UP, 1), stage(1, OUT, 1)],
        "dy": [chip(0, UP), stage(1, QKV, 0)],
        "half": [chip(0, OUT), stage(1, DOWN, 2), stage(0, DOWN, 0)],
        "attention": [stage(1, UP, 2), stage(1, QKV, 1), stage(1, OUT, 2)],
        "qkv": [stage(0, UP, 0), stage(0, DOWN, 1)],
    })

    home = R.at[pl.ds(pl.multiple_of(jnp.where(z < 2, 0, tok), tok), tok), :]
    ret_local = pltpu.make_async_copy(home, ret_r, ret_sem.at[1])
    ret_remote = pltpu.make_async_remote_copy(
        src_ref=home, dst_ref=ret_r, send_sem=ret_sem.at[0], recv_sem=ret_sem.at[1],
        device_id=owner, device_id_type=MESH,
    )

    @pl.when(mine)
    def _():
        ret_local.start()

    @pl.when(jnp.logical_not(mine))
    def _():
        ret_remote.start()

    vec_targets = [peer] + [partner(dim) for dim in dims]

    def vec_copy(k):
        return pltpu.make_async_remote_copy(
            src_ref=vs, dst_ref=vr.at[k], send_sem=vec_sem.at[0, k], recv_sem=vec_sem.at[1, k],
            device_id=vec_targets[k], device_id_type=MESH,
        )

    def vec_step(k):
        vec_copy(k).wait()
        if k + 1 < len(vec_targets):
            vs[...] = vs[...] + vr[k]
            vec_copy(k + 1).start()
        else:
            vec_o[...] = vs[...] + vr[k]

    vs[...] = vec_o[...] * factor
    vec_copy(0).start()
    after_chip(0, QKV)
    vec_at = 0
    ends = [
        (0, OUT, 0), (1, QKV, 2), (0, UP, 1), (0, 0, -1), (0, DOWN, 2), (0, OUT, 1), (0, QKV, 0), (0, 0, -1),
        (0, UP, 2), (0, OUT, 2), (0, QKV, 1), (0, 0, -1), (0, QKV, 2),
    ]
    order_of_items = [(1, DOWN), (1, UP), (1, OUT), (1, QKV), (0, OUT), (0, DOWN), (0, UP), (0, QKV)]
    left = [(l, i, k) for k in range(stages) for l, i in order_of_items if (l, i, k) not in done]
    if stages == 3:
        assert sorted(left) == sorted(e for e in ends if e[2] >= 0)
    else:
        ends = left
    for l, i, k in ends:
        if k >= 0:
            after_stage(l, i, k)
        else:
            vec_step(vec_at)
            vec_at += 1
    for k in range(vec_at, len(vec_targets)):
        vec_step(k)
    ret_local.wait()

    @pl.when(jnp.logical_not(mine))
    def _():
        ret_remote.wait_send()

    gin_o[...] = ret_r[...]


def run_last(plan, upstream, vec, tot, gains, stashes, weights):
    tok = plan.tok
    T = 2 * tok
    vmem = pl.BlockSpec(memory_space=pltpu.VMEM)
    hbm = pl.BlockSpec(memory_space=pl.ANY)
    S = jax.ShapeDtypeStruct
    V = pltpu.VMEM
    DMA = pltpu.SemaphoreType.DMA
    items = items_of(plan)
    n = len(items)
    stages = plan.bits + 1
    own = {"down": plan.cf, "up": plan.ch, "out": plan.ch, "qkv": plan.ch}
    outs = [S((LAYERS, own[i.name], i.cols), F32) for i in items] + [S((tok, D), F32), S(vec.shape, F32)]
    K = stashes[0].shape[2]
    scratch = [V((2 * i.rows, K), BF16) for i in items]
    scratch += [V((K, i.cols), BF16) for i in items]
    scratch += [V((LAYERS, i.rows, i.cols), BF16) for i in items]
    scratch += [
        V((i.rows * i.cols // FF, FF) if i.name == "down" else (i.rows, i.cols), BF16) for i in items
    ]
    for k in range(stages - 1):
        scratch += [V((LAYERS, i.rows >> (k + 1), i.cols), BF16) for i in items]
    last = [i.rows >> stages for i in items]
    scratch += [V((2 * r, i.cols // 2), BF16) for r, i in zip(last, items)]
    scratch += [V((LAYERS, 2 * r, i.cols // 2), BF16) for r, i in zip(last, items)]
    nv = 2 + plan.bits
    scratch += [
        V((plan.rows, FF), BF16),
        V((D, 3 * D), BF16), V((D, D), BF16), V((D, FF), BF16), V((FF, D), BF16),
        V((T, D), BF16), V((2 * T, 2 * D), BF16), V((8, 8, T), F32), V((T, D), F32), V((T, FF), BF16),
        V((2 * T, T), F32), V((T, D), F32), V((2 * T, 2 * D), BF16), V((2, tok, 2 * D), BF16),
        V((tok, D), F32), V(vec.shape, F32), V((nv,) + vec.shape, F32),
        DMA((n, 2)), DMA((4,)), DMA((6,)), DMA((2, n)), DMA((2, LAYERS, n, stages, 3)), DMA((2, nv)), DMA((2, 2, 2)),
        DMA((2,)), DMA((1,)),
    ]
    call = pl.pallas_call(
        functools.partial(last_kernel, plan),
        out_shape=outs,
        out_specs=[vmem] * len(outs),
        in_specs=[hbm] + [vmem] * 4 + [hbm] * (len(stashes) + 4),
        scratch_shapes=scratch,
        compiler_params=pltpu.CompilerParams(
            collective_id=1, has_side_effects=True, vmem_limit_bytes=VMEM_LIMIT
        ),
        name="last",
    )
    return call(upstream, vec, tot, *gains, *stashes, *weights)


def finish_kernel(plan, vec_ref, *refs):
    big = refs[:6]
    big_o, small_o = refs[6:12], refs[12:21]
    for a, b in zip(big, big_o):
        b[...] = a[...]
    me = lax.axis_index("grp") * plan.nrow + lax.axis_index("row")
    feature = lax.broadcasted_iota(jnp.int32, (D, 128), 0)
    place = lax.broadcasted_iota(jnp.int32, (D, 128), 1)

    def picked(rows, first, n):
        one_hot = jnp.where((feature == first + place) & (place < n), 1.0, 0.0)
        return jnp.dot(rows, one_hot, preferred_element_type=F32, precision=lax.Precision.HIGHEST)

    per = D // plan.cf
    rows = picked(vec_ref[...], me * plan.ch, plan.ch)
    wide = picked(vec_ref[...], lax.rem(me, per) * plan.cf, plan.cf)
    row = lax.broadcasted_iota(jnp.int32, (LAYERS * SMALL, 128), 0)
    for l in range(LAYERS):
        for i in range(8):
            small_o[i][l : l + 1, :] = rows[row_of(l, i), : plan.ch]
        line = jnp.sum(jnp.where(row == l * SMALL + 8 + lax.div(me, per), wide, 0.0), axis=0, keepdims=True)
        small_o[8][l : l + 1, :] = line[:, : plan.cf]


def run_finish(plan, vec, big):
    vmem = pl.BlockSpec(memory_space=pltpu.VMEM)
    S = jax.ShapeDtypeStruct
    outs = [S(a.shape, a.dtype) for a in big]
    outs += [S((LAYERS, plan.ch), F32)] * 8 + [S((LAYERS, plan.cf), F32)]
    return pl.pallas_call(
        functools.partial(finish_kernel, plan),
        out_shape=outs,
        in_specs=[vmem] * 7,
        out_specs=[vmem] * 15,
        name="finish",
    )(vec, *big)


def body(
    plan,
    inputs, cotangent, pass_counts, doc_starts, token_counts,
    ln1_gain, ln1_bias, qkv_weight, query_bias, value_bias, out_weight, out_bias,
    ln2_gain, ln2_bias, up_weight, up_bias, down_weight, down_bias,
):
    vecs = (ln1_gain, ln1_bias, query_bias, value_bias, out_bias, ln2_gain, ln2_bias, up_bias, down_bias)
    weights = (qkv_weight, out_weight, up_weight, down_weight)
    hidden, upstream, vec, tot, *rest = run_main(
        plan, inputs, cotangent, (pass_counts, doc_starts, token_counts), vecs, weights
    )
    g_down, g_up, g_out, g_qkv, grad_in, vec = run_last(
        plan, upstream, vec, tot, (ln1_gain, ln2_gain), rest, weights
    )
    big = (hidden, grad_in, g_qkv, g_out, g_up, g_down)
    hidden, grad_in, g_qkv, g_out, g_up, g_down, *v = run_finish(plan, vec, big)
    return (
        hidden, grad_in, v[0], v[1], g_qkv, v[2], v[3], g_out, v[4], v[5], v[6], g_up, v[8], g_down, v[7],
    )


def solution(mesh):
    ngrp, nrow = mesh.shape["grp"], mesh.shape["row"]
    whole = P(("grp", "row"), None)
    vector = P(None, ("grp", "row"))
    matrix = P(None, ("grp", "row"), None)

    def run(*args):
        return body(Plan(ngrp, nrow, args[0].shape[0]), *args)

    return jax.shard_map(
        run,
        mesh=mesh,
        in_specs=(whole, whole, P("grp"), P("grp", None), P("grp")) + (P(),) * 13,
        out_specs=(
            whole, whole, vector, vector, matrix, vector, vector, matrix, vector, vector, vector,
            matrix, vector, matrix, vector,
        ),
        check_vma=False,
    )
```

```python
import functools

import jax
import jax.numpy as jnp
from jax import lax
from jax.experimental import pallas as pl
from jax.experimental.pallas import tpu as pltpu
from jax.sharding import PartitionSpec as P

HEADS = 12
HEAD = 64
D = 768
FF = 3072
LAYERS = 2
MAXP = 2
STEPS = LAYERS * (MAXP + 1)
SMALL = 12

EPS = 1e-05
NEG = -1000000000.0
LOG2E = 1.4426950408889634
MESH = pl.DeviceIdType.MESH
VMEM_LIMIT = 63 * 2**20
F32 = jnp.float32
BF16 = jnp.bfloat16


def nn(a, b):
    return jnp.dot(a, b, preferred_element_type=F32)


def nt(a, b):
    return lax.dot_general(a, b, (((1,), (1,)), ((), ())), preferred_element_type=F32)


def tn(a, b):
    return lax.dot_general(a, b, (((0,), (0,)), ((), ())), preferred_element_type=F32)


def normalised(x):
    mean = jnp.mean(x, axis=-1, keepdims=True)
    centred = x - mean
    spread = jnp.mean(centred * centred, axis=-1, keepdims=True)
    inv = lax.rsqrt(spread + EPS)
    return centred * inv, inv


def norm_back(grad, gain, hat, inv):
    g = grad * gain
    mean_g = jnp.mean(g, axis=-1, keepdims=True)
    mean_gh = jnp.mean(g * hat, axis=-1, keepdims=True)
    return inv * (g - mean_g - hat * mean_gh)


def column_sum(x):
    return jnp.sum(x, axis=0, keepdims=True)


def of_head(h):
    p = h // 2
    at, atv = slice(p * 128, (p + 1) * 128), slice(D + p * 128, D + (p + 1) * 128)
    low = lax.broadcasted_iota(jnp.int32, (1, 128), 1) < HEAD
    return at, atv, low if h % 2 == 0 else jnp.logical_not(low)


def attention_forward(KV, Q, LSE, bias, O, before_values):
    def scores(h):
        at, _, keep = of_head(h)
        qp = Q[:, at]
        return nt(KV[:, at], jnp.where(keep, qp, jnp.zeros_like(qp)))

    def mixed(h, raw):
        _, atv, _ = of_head(h)
        logits = raw * LOG2E + bias[...]
        top = jnp.max(logits, axis=0, keepdims=True)
        expo = jnp.exp2(logits - top)
        denom = jnp.sum(expo, axis=0, keepdims=True)
        LSE[h // 2, h % 2 : h % 2 + 1, :] = top + jnp.log2(denom)
        return tn((expo * (1.0 / denom)).astype(BF16), KV[:, atv])

    ahead = scores(0)
    before_values()
    even = None
    for h in range(HEADS):
        raw = ahead
        if h + 1 < HEADS:
            ahead = scores(h + 1)
        out = mixed(h, raw)
        if h % 2 == 0:
            even = out
        else:
            at, _, high = of_head(h)
            O[:, at] = jnp.where(high, out, even).astype(BF16)


def attention_backward(KV, Q, LSE, bias, DO, DP, DKV, between):
    low_row = lax.broadcasted_iota(jnp.int32, (128, 1), 0) < HEAD

    def parts(h):
        at, atv, keep = of_head(h)
        qp, dop = Q[:, at], DO[:, at]
        zero = jnp.zeros_like(qp)
        return KV[:, at], KV[:, atv], jnp.where(keep, qp, zero), jnp.where(keep, dop, zero)

    def products(h):
        kp, vp, qe, doe = parts(h)
        return nt(kp, qe), nt(vp, doe)

    def grads(h, raw, dpr):
        lse = LSE[h // 2, h % 2 : h % 2 + 1, :]
        pr = jnp.exp2(raw * LOG2E + bias[...] - lse)
        inner = jnp.sum(pr * dpr, axis=0, keepdims=True)
        return pr.astype(BF16), (pr * (dpr - inner)).astype(BF16)

    def finish(h0, one, two):
        at, atv, _ = of_head(h0)
        kp, _, q0, do0 = parts(h0)
        _, _, q1, do1 = parts(h0 + 1)
        dqt = jnp.where(low_row, tn(kp, one[1]), tn(kp, two[1])) * 0.125
        DP[:, at] = dqt.T.astype(BF16)
        p = h0 // 2
        DKV[:, (2 * p + 1) * 128 : (2 * p + 2) * 128] = nn(
            jnp.concatenate([one[0], two[0]], axis=1), jnp.concatenate([do0, do1], axis=0)
        ).astype(BF16)
        DKV[:, 2 * p * 128 : (2 * p + 1) * 128] = nn(
            jnp.concatenate([one[1], two[1]], axis=1), jnp.concatenate([q0, q1], axis=0)
        ).astype(BF16)

    ahead = products(0)
    even = None
    for h in range(HEADS):
        now = ahead
        if h + 1 < HEADS:
            ahead = products(h + 1)
        pair = grads(h, *now)
        if h % 2 == 0:
            even = pair
        else:
            finish(h - 1, even, pair)
        if h in between:
            between[h]()


def merge_kv(DP, DKV, RDKV, off, half):
    tok = RDKV.shape[1]
    for j in range(2):
        for p in range(half * HEADS // 4, (half + 1) * HEADS // 4):
            at = slice(2 * p * 128, (2 * p + 2) * 128)
            both = (DKV[pl.ds(off[j], tok), at].astype(F32) + RDKV[j, :, at].astype(F32)).astype(BF16)
            DP[j * tok : (j + 1) * tok, D + p * 128 : D + (p + 1) * 128] = both[:, :128]
            DP[j * tok : (j + 1) * tok, 2 * D + p * 128 : 2 * D + (p + 1) * 128] = both[:, 128:]


def row_of(layer, k):
    return slice(layer * SMALL + k, layer * SMALL + k + 1)


class Plan:
    def __init__(self, ngrp, nrow, tok):
        self.ngrp, self.nrow, self.tok = ngrp, nrow, tok
        self.ncol = ngrp // 2
        self.bits = max(self.ncol.bit_length() - 1, 0)
        self.ndev = ngrp * nrow
        self.ch = D // self.ndev
        self.chp = -(-self.ch // 8) * 8
        self.cf = FF // self.ndev
        self.rows = self.ncol * 2 * self.chp
        self.nsel = 2 * self.rows
        self.wide = FF // ngrp
        self.per = D // (2 * self.wide)
        self.frows = self.ncol * 2 * self.cf
        dims = list(range(self.bits))[::-1] + [-1]
        turns = [k * len(dims) // 3 for k in range(3)]
        self.orders = [dims[t:] + dims[:t] for t in turns]

    def piece(self, order, index):
        col, pair = 0, 0
        for place, dim in enumerate(order):
            bit = (index >> (len(order) - 1 - place)) & 1
            if dim < 0:
                pair = bit
            else:
                col |= bit << dim
        return col, pair

    def moved(self, turn):
        first = {self.piece(self.orders[0], k): k for k in range(2 * self.ncol)}
        return [first[self.piece(self.orders[turn], k)] for k in range(2 * self.ncol)]

    def fill_selectors(self, sel, c, half):
        def ones(first, rows, used):
            feature = lax.broadcasted_iota(jnp.int32, (rows, D), 1)
            place = lax.broadcasted_iota(jnp.int32, (rows, D), 0)
            return jnp.where((feature == first + place) & (place < used), 1.0, 0.0)

        for side, core in enumerate((c, 1 - c)):
            for index in range(0, 2 * self.ncol, 2):
                two = []
                for k in (index, index + 1):
                    col, pair = self.piece(self.orders[0], k)
                    two.append(ones(((col * 2 + core) * 4 + 2 * half + pair) * self.ch, self.chp, self.ch))
                row = side * self.rows + index * self.chp
                sel[0, row : row + 2 * self.chp, :] = jnp.concatenate(two, axis=0).astype(BF16)
            for j in range(self.per):
                row = side * (D // 4) + j * 2 * self.cf
                first = (j * 2 + core) * self.wide + half * 2 * self.cf
                sel[1, row : row + 2 * self.cf, :] = ones(first, 2 * self.cf, 2 * self.cf).astype(BF16)


def where_am_i():
    g = lax.axis_index("grp")
    z = lax.axis_index("row")
    c = lax.rem(g, 2)
    col = lax.div(g, 2)
    outer = jnp.logical_or(z == 0, z == 3)
    parity = jnp.where(outer, 0, 1)
    return g, z, c, col, outer, parity


def fill_bias(bias, starts, c, tok):
    T = 2 * tok
    lane = lax.broadcasted_iota(jnp.int32, (1, T), 1)
    qpos = jnp.where(lane < tok, c * tok + lane, (3 - c) * tok + lane - tok).astype(F32)
    begin = jnp.zeros((1, T), F32)
    for start in starts:
        begin = jnp.maximum(begin, jnp.where(qpos >= start, start, 0.0))
    kpos = lax.broadcasted_iota(jnp.int32, (2 * T, T), 0).astype(F32)
    bias[...] = jnp.where((kpos <= qpos) & (kpos >= begin), 0.0, NEG)


def main_kernel(
    plan,
    x_own, cot_own, pass_ref, doc_ref, tok_ref, ln1g, ln1b, qb, vb, ob, ln2g, ln2b, ub, db,
    wq_h, wo_h, wu_h, wd_h,
    hid_o, up_o, vec_o, tot_o, asel_h, osel_h, usel_h, gsel_h, dp_h, dy_h, df_h, dr_h,
    sx_h, sq_h, skv_h, slse_h, sm_h, sgp_h,
    wq, wo, wu, wd, sel, xin, cot, par_ref, par_in, tsend, trecv,
    bias, X, Q, KV, LSE, M, GP, O, GF, XN, asel, osel, usel, gsel,
    R, U, DKV, RDKV, DP, DR, DY, VAC, ret_s, ret_r,
    w_sem, in_send, in_recv, cot_send, cot_recv, par_sem, t_sem, kv_send, kv_recv,
    st_sem, ld_sem, sel_out, dkv_send, dkv_recv, bst_sem, ret_send, ret_recv,
):
    tok = plan.tok
    T = 2 * tok
    g, z, c, col, outer, parity = where_am_i()
    half = lax.div(z, 2)
    peer = (col * 2 + 1 - c, z)
    off_lo = pl.multiple_of(c * tok, tok)
    off_hi = pl.multiple_of((3 - c) * tok, tok)
    poff_lo = pl.multiple_of((1 - c) * tok, tok)
    poff_hi = pl.multiple_of((2 + c) * tok, tok)

    weight_copies = []
    for l in range(LAYERS):
        for i, (src, dst) in enumerate(((wq_h, wq), (wo_h, wo), (wu_h, wu), (wd_h, wd))):
            weight_copies.append(pltpu.make_async_copy(src.at[l], dst.at[l], w_sem.at[l, i]))
    weight_copies[0].start()
    numbers = [pass_ref[0], tok_ref[0]] + [doc_ref[0, k] for k in range(4)] + [0, 0]
    for k, number in enumerate(numbers):
        par_ref[k : k + 1, :] = jnp.full((1, 128), number, jnp.int32).astype(F32)

    barrier = pltpu.get_barrier_semaphore()
    count = 0
    for dc in range(2):
        for dz in range(plan.nrow):
            if dc == 0 and dz == 0:
                continue
            target = (col * 2 + lax.rem(c + dc, 2), lax.rem(z + dz, plan.nrow))
            pl.semaphore_signal(barrier, inc=1, device_id=target, device_id_type=MESH)
            count += 1
    others = [(col ^ (1 << b)) * 2 + c for b in range(plan.bits)]
    for other in others:
        pl.semaphore_signal(barrier, inc=1, device_id=(other, z), device_id_type=MESH)
        count += 1
    pl.semaphore_wait(barrier, count)

    block_core = jnp.where(outer, 0, 1)
    slot_in = lax.div(z, 2)
    send_list = []
    for i in range(2):
        zt = jnp.where(c == 0, 3 * i, 1 + i)
        is_self = jnp.logical_and(c == block_core, zt == z)
        send_list.append((i, zt, is_self))

    def deliver(src, dst, send, recv):
        for i, zt, is_self in send_list:

            @pl.when(is_self)
            def _():
                pltpu.make_async_copy(src, dst.at[slot_in], recv.at[slot_in]).start()

            @pl.when(jnp.logical_not(is_self))
            def _():
                pltpu.make_async_remote_copy(
                    src_ref=src, dst_ref=dst.at[slot_in], send_sem=send.at[i], recv_sem=recv.at[slot_in],
                    device_id=(col * 2 + block_core, zt), device_id_type=MESH,
                ).start()

    def deliver_sent(src, dst, send, recv):
        for i, zt, is_self in send_list:

            @pl.when(jnp.logical_not(is_self))
            def _():
                pltpu.make_async_remote_copy(
                    src_ref=src, dst_ref=dst.at[slot_in], send_sem=send.at[i], recv_sem=recv.at[slot_in],
                    device_id=(col * 2 + block_core, zt), device_id_type=MESH,
                ).wait_send()

    def deliver_wait(src, dst, recv):
        for i in range(2):
            pltpu.make_async_copy(src, dst.at[i], recv.at[i]).wait()

    deliver(x_own, xin, in_send, in_recv)

    par_copy = pltpu.make_async_remote_copy(
        src_ref=par_ref, dst_ref=par_in, send_sem=par_sem.at[0], recv_sem=par_sem.at[1],
        device_id=peer, device_id_type=MESH,
    )
    par_copy.start()
    for cp in weight_copies[1:]:
        cp.start()
    par_copy.wait()
    served = jnp.where(parity == c, par_ref[...], par_in[...])
    tcount = par_ref[1:2, :] + par_in[1:2, :]
    total = jnp.broadcast_to(tcount, (8, 128))
    for b in range(plan.bits):
        tsend[b] = total
        cp = pltpu.make_async_remote_copy(
            src_ref=tsend.at[b], dst_ref=trecv.at[b], send_sem=t_sem.at[0, b], recv_sem=t_sem.at[1, b],
            device_id=(others[b], z), device_id_type=MESH,
        )
        cp.start()
        cp.wait()
        total = total + trecv[b]
    factor = served[1:2, :] / total[0:1, :]
    tot_o[0:1, :] = factor
    tot_o[1:8, :] = jnp.concatenate([served[0:1, :], served[2:8, :]], axis=0)
    passes = served[0:1, 0:1]

    fill_bias(bias, [served[2 + k : 3 + k, 0:1] for k in range(4)], c, tok)
    VAC[...] = jnp.zeros_like(VAC)
    for cp in weight_copies:
        cp.wait()
    plan.fill_selectors(sel, c, half)

    deliver_wait(x_own, xin, in_recv)
    deliver_sent(x_own, xin, in_send, in_recv)
    XN[0:tok] = xin[0].astype(F32)
    XN[tok:T] = xin[1].astype(F32)
    deliver(cot_own, cot, cot_send, cot_recv)

    def stash_copies(s, slot, sem, back):
        pairs = ((X, sx_h), (Q, sq_h), (LSE, slse_h), (M, sm_h), (GP, sgp_h))
        out = []
        for i, (v, h) in enumerate(pairs):
            if back:
                out.append(pltpu.make_async_copy(h.at[s], v.at[slot], sem.at[slot, i]))
            else:
                out.append(pltpu.make_async_copy(v.at[slot], h.at[s], sem.at[slot, i]))
        return out

    def kv_stash(s, slot):
        return pltpu.make_async_copy(KV.at[slot], skv_h.at[s], st_sem.at[slot, 5])

    def kv_load(s, slot):
        return pltpu.make_async_copy(skv_h.at[s], KV.at[slot], ld_sem.at[slot, 5])

    def sel_copies_out(l, sect):
        at = pl.ds(pl.multiple_of(sect * T, T), T)
        return [
            pltpu.make_async_copy(asel, asel_h.at[l, :, at], sel_out.at[0]),
            pltpu.make_async_copy(osel, osel_h.at[l, :, at], sel_out.at[1]),
            pltpu.make_async_copy(usel, usel_h.at[l, :, at], sel_out.at[2]),
            pltpu.make_async_copy(gsel, gsel_h.at[l, :, at], sel_out.at[3]),
        ]

    def kv_moves(slot, offsets):
        out = []
        for part in range(2):
            out.append([])
            for i, off in enumerate(offsets):
                ref = KV.at[slot, pl.ds(off, tok), part * D : (part + 1) * D]
                out[part].append(
                    pltpu.make_async_remote_copy(
                        src_ref=ref, dst_ref=ref, send_sem=kv_send.at[slot, part, i],
                        recv_sem=kv_recv.at[slot, part, i], device_id=peer, device_id_type=MESH,
                    )
                )
        return out

    def kv_copies(slot):
        return kv_moves(slot, (off_lo, off_hi))

    def kv_arrivals(slot):
        return kv_moves(slot, (poff_lo, poff_hi))

    def forward(sect, l):
        s = sect * LAYERS + l
        slot = l

        @pl.when(sect >= 1)
        def _():
            for cp in stash_copies(s - 2, slot, st_sem, False):
                cp.wait()

        x = XN[...]
        X[slot] = x
        stash = stash_copies(s, slot, st_sem, False)
        rows_out = sel_copies_out(l, sect)
        stash[0].start()
        hat, _ = normalised(x)
        a = (hat * ln1g[l : l + 1, :] + ln1b[l : l + 1, :]).astype(BF16)

        def own_rows(values, at):
            KV[slot, pl.ds(off_lo, tok), at] = values[:tok]
            KV[slot, pl.ds(off_hi, tok), at] = values[tok:]

        sends = kv_copies(slot)
        arrivals = kv_arrivals(slot)
        own_rows(nn(a, wq[l, :, D : 2 * D]).astype(BF16), slice(0, D))
        for cp in sends[0]:
            cp.start()
        own_rows((nn(a, wq[l, :, 2 * D : 3 * D]) + vb[l : l + 1, :]).astype(BF16), slice(D, 2 * D))
        for cp in sends[1]:
            cp.start()
        q = (nn(a, wq[l, :, 0:D]) + qb[l : l + 1, :]).astype(BF16)
        Q[slot] = q * jnp.asarray(0.125, BF16)
        stash[1].start()

        def rows_of_before():
            for cp in sel_copies_out(0, 0):
                cp.wait()

        if l == 0:
            pl.when(sect >= 1)(rows_of_before)
        else:
            rows_of_before()
        asel[...] = nt(sel[0], a).astype(BF16)
        rows_out[0].start()
        for cp in arrivals[0]:
            cp.wait_recv()

        def values_here():
            for cp in arrivals[1]:
                cp.wait_recv()
            for cp in sends[0] + sends[1]:
                cp.wait_send()
            kv_stash(s, slot).start()

        attention_forward(KV.at[slot], Q.at[slot], LSE.at[slot], bias, O, values_here)
        o = O[...]
        osel[...] = nt(sel[0], o).astype(BF16)
        stash[2].start()
        rows_out[1].start()
        m = x + (nn(o, wo[l]) + ob[l : l + 1, :])
        M[slot] = m
        stash[3].start()
        hat2, _ = normalised(m)
        a2 = (hat2 * ln2g[l : l + 1, :] + ln2b[l : l + 1, :]).astype(BF16)
        usel[...] = nt(sel[0], a2).astype(BF16)
        rows_out[2].start()

        for j in range(FF // D):
            js = slice(j * D, (j + 1) * D)
            f = nn(a2, wu[l, :, js]) + ub[l : l + 1, js]
            f2 = f * f
            u = f * (0.7978845608028654 + 0.035677408136300125 * f2)
            t = jnp.tanh(u)
            h = 0.5 + 0.5 * t
            ga = f * h
            gp = h + ga * (1.0 - h) * (1.5957691216057308 + 0.21406444881780074 * f2)
            gb = ga.astype(BF16)
            GF[:, js] = gb
            GP[slot, :, js] = gp.astype(BF16)
            n = D // 4
            gs = nt(sel[1, : 2 * n], gb).astype(BF16)
            for cc in range(2):
                gsel[cc * plan.frows + j * n : cc * plan.frows + (j + 1) * n] = gs[cc * n : (cc + 1) * n]

        stash[4].start()
        rows_out[3].start()
        y = m + (nn(GF[...], wd[l]) + db[l : l + 1, :])
        if l == LAYERS - 1:
            bar = jnp.where(sect < MAXP, sect, -1).astype(F32)
            y = jnp.where(passes > bar, y, X[0])
        XN[...] = y
        kv_stash(s, slot).wait()

    def forward_section(sect, carry):
        for l in range(LAYERS):
            forward(sect, l)
        return carry

    lax.fori_loop(0, MAXP + 1, forward_section, 0)

    block = jnp.where(z < 2, c, 3 - c)
    owner = (col * 2 + parity, block)
    mine = jnp.logical_and(parity == c, block == z)

    ret_recv_wait = pltpu.make_async_copy(ret_s, ret_r, ret_recv.at[0])
    ret_remote = pltpu.make_async_remote_copy(
        src_ref=ret_s, dst_ref=ret_r, send_sem=ret_send.at[0], recv_sem=ret_recv.at[0],
        device_id=owner, device_id_type=MESH,
    )

    @pl.when(z < 2)
    def _():
        ret_s[...] = XN[0:tok]

    @pl.when(z >= 2)
    def _():
        ret_s[...] = XN[tok:T]

    @pl.when(mine)
    def _():
        ret_recv_wait.start()

    @pl.when(jnp.logical_not(mine))
    def _():
        ret_remote.start()

    deliver_wait(cot_own, cot, cot_recv)
    deliver_sent(cot_own, cot, cot_send, cot_recv)
    U[0:tok] = cot[0]
    U[tok:T] = cot[1]
    for cp in sel_copies_out(0, 0):
        cp.wait()
    for l in range(LAYERS):
        for cp in stash_copies(MAXP * LAYERS + l, l, st_sem, False):
            cp.wait()

    def back_copies(l, sect):
        at = pl.ds(pl.multiple_of(sect * T, T), T)
        return [
            pltpu.make_async_copy(DP, dp_h.at[l, at, :], bst_sem.at[0]),
            pltpu.make_async_copy(DY, dy_h.at[l, at, :], bst_sem.at[1]),
            pltpu.make_async_copy(GF, df_h.at[l, at, :], bst_sem.at[2]),
            pltpu.make_async_copy(DR, dr_h.at[l, at, :], bst_sem.at[3]),
        ]

    def dkv_copies(slot, half):
        at = slice(half * D, (half + 1) * D)
        return [
            pltpu.make_async_remote_copy(
                src_ref=DKV.at[pl.ds(off, tok), at], dst_ref=RDKV.at[slot, i, :, at],
                send_sem=dkv_send.at[slot, half, i], recv_sem=dkv_recv.at[slot, half, i],
                device_id=peer, device_id_type=MESH,
            )
            for i, off in enumerate((poff_lo, poff_hi))
        ]

    def backward(i, l):
        sect = MAXP - i
        s = sect * LAYERS + l
        slot = l

        stores = back_copies(l, sect)

        def stored(k):
            if i >= 1 or l < LAYERS - 1:
                stores[k].wait()

        if i >= 1:
            for cp in stash_copies(s, slot, ld_sem, True):
                cp.wait()
            kv_load(s, slot).wait()

        active = jnp.where(passes > (-1.0 if sect == MAXP else float(sect)), jnp.ones((1, 1), F32), jnp.zeros((1, 1), F32))
        r = U[...] * active if l == LAYERS - 1 else R[...]
        dr = r.astype(BF16)
        stored(3)
        DR[...] = dr
        stores[3].start()
        stored(2)
        VAC[row_of(l, 7)] += column_sum(dr.astype(F32))
        for j in range(FF // D):
            js = slice(j * D, (j + 1) * D)
            dg = nt(dr, wd[l, js, :])
            df = (dg * GP[slot, :, js].astype(F32)).astype(BF16)
            GF[:, js] = df
            VAC[row_of(l, 8 + j)] += column_sum(df.astype(F32))
        stores[2].start()
        da2 = nt(GF[...], wu[l])
        hat2, inv2 = normalised(M[slot])
        VAC[row_of(l, 5)] += column_sum(da2 * hat2)
        VAC[row_of(l, 6)] += column_sum(da2)
        dm = r + norm_back(da2, ln2g[l : l + 1, :], hat2, inv2)
        R[...] = dm
        dy = dm.astype(BF16)
        stored(1)
        DY[...] = dy
        stores[1].start()
        VAC[row_of(l, 4)] += column_sum(dy.astype(F32))
        O[...] = nt(dy, wo[l]).astype(BF16)

        stored(0)

        def send_half(half):
            for cp in dkv_copies(slot, half):
                cp.start()

        attention_backward(
            KV.at[slot], Q.at[slot], LSE.at[slot], bias, O, DP, DKV,
            {HEADS // 2 - 1: lambda: send_half(0), HEADS - 1: lambda: send_half(1)},
        )
        x = X[slot]
        hat, inv = normalised(x)

        if i == 0:
            for cp in stash_copies(s - 2, slot, ld_sem, True):
                cp.start()
            kv_load(s - 2, slot).start()

        dqb = DP[:, 0:D]
        VAC[row_of(l, 2)] += column_sum(dqb.astype(F32))
        da = nt(dqb, wq[l, :, 0:D])
        for half in range(2):
            for cp in dkv_copies(slot, half):
                cp.wait()
            merge_kv(DP, DKV, RDKV.at[slot], (off_lo, off_hi), half)
        stores[0].start()
        dkv = DP[:, D : 3 * D]
        VAC[row_of(l, 3)] += column_sum(dkv[:, D:].astype(F32))
        da = da + nt(dkv, wq[l, :, D : 3 * D])
        VAC[row_of(l, 0)] += column_sum(da * hat)
        VAC[row_of(l, 1)] += column_sum(da)
        new = R[...] + norm_back(da, ln1g[l : l + 1, :], hat, inv)
        if l == 0:
            U[...] = new + (1.0 - active) * U[...]
        else:
            R[...] = new

    for i in range(MAXP):
        for l in range(LAYERS - 1, -1, -1):
            backward(i, l)
    ret_recv_wait.wait()

    @pl.when(jnp.logical_not(mine))
    def _():
        ret_remote.wait_send()

    hid_o[...] = ret_r[...]
    up_o[...] = U[...]
    vec_o[...] = VAC[...]
    for cp in back_copies(0, 0):
        cp.wait()


def run_main(plan, x, cot, numbers, vecs, weights):
    tok = plan.tok
    T = 2 * tok
    L = 4 * tok
    vmem = pl.BlockSpec(memory_space=pltpu.VMEM)
    hbm = pl.BlockSpec(memory_space=pl.ANY)
    smem = pl.BlockSpec(memory_space=pltpu.SMEM)
    S = jax.ShapeDtypeStruct
    K = (MAXP + 1) * T
    outs = [
        (S((tok, D), F32), vmem),
        (S((T, D), F32), vmem),
        (S((LAYERS * SMALL, D), F32), vmem),
        (S((8, 128), F32), vmem),
        (S((LAYERS, plan.nsel, K), BF16), hbm),
        (S((LAYERS, plan.nsel, K), BF16), hbm),
        (S((LAYERS, plan.nsel, K), BF16), hbm),
        (S((LAYERS, 2 * plan.frows, K), BF16), hbm),
        (S((LAYERS, K, 3 * D), BF16), hbm),
        (S((LAYERS, K, D), BF16), hbm),
        (S((LAYERS, K, FF), BF16), hbm),
        (S((LAYERS, K, D), BF16), hbm),
        (S((STEPS, T, D), F32), hbm),
        (S((STEPS, T, D), BF16), hbm),
        (S((STEPS, L, 2 * D), BF16), hbm),
        (S((STEPS, 8, 8, T), F32), hbm),
        (S((STEPS, T, D), F32), hbm),
        (S((STEPS, T, FF), BF16), hbm),
    ]
    V = pltpu.VMEM
    DMA = pltpu.SemaphoreType.DMA
    nb = max(plan.bits, 1)
    scratch = [
        V((LAYERS, D, 3 * D), BF16), V((LAYERS, D, D), BF16), V((LAYERS, D, FF), BF16), V((LAYERS, FF, D), BF16),
        V((2, plan.nsel, D), BF16), V((2, tok, D), BF16), V((2, tok, D), F32), V((8, 128), F32), V((8, 128), F32),
        V((nb, 8, 128), F32), V((nb, 8, 128), F32),
        V((L, T), F32),
        V((2, T, D), F32), V((2, T, D), BF16), V((2, L, 2 * D), BF16), V((2, 8, 8, T), F32), V((2, T, D), F32),
        V((2, T, FF), BF16), V((T, D), BF16), V((T, FF), BF16), V((T, D), F32),
        V((plan.nsel, T), BF16), V((plan.nsel, T), BF16), V((plan.nsel, T), BF16), V((2 * plan.frows, T), BF16),
        V((T, D), F32), V((T, D), F32), V((L, 2 * D), BF16), V((2, 2, tok, 2 * D), BF16), V((T, 3 * D), BF16),
        V((T, D), BF16), V((T, D), BF16), V((LAYERS * SMALL, D), F32), V((tok, D), F32), V((tok, D), F32),
        DMA((LAYERS, 4)), DMA((2,)), DMA((2,)), DMA((2,)), DMA((2,)), DMA((2,)), DMA((2, nb)),
        DMA((2, 2, 2)), DMA((2, 2, 2)), DMA((2, 6)), DMA((2, 6)), DMA((4,)), DMA((2, 2, 2)), DMA((2, 2, 2)), DMA((4,)),
        DMA((1,)), DMA((1,)),
    ]
    call = pl.pallas_call(
        functools.partial(main_kernel, plan),
        out_shape=[o[0] for o in outs],
        out_specs=[o[1] for o in outs],
        in_specs=[vmem] * 2 + [smem] * 3 + [vmem] * 9 + [hbm] * 4,
        scratch_shapes=scratch,
        compiler_params=pltpu.CompilerParams(
            collective_id=0, has_side_effects=True, vmem_limit_bytes=VMEM_LIMIT
        ),
        name="layers",
    )
    return call(x, cot, *numbers, *vecs, *weights)


def fold(x):
    n = x.shape[1] // 2
    return jnp.concatenate([x[:, :n], x[:, n:]], axis=0)


def unfold(x):
    n = x.shape[0] // 2
    return jnp.concatenate([x[:n], x[n:]], axis=1)


class Item:
    def __init__(self, name, rows, cols, chunk):
        self.name, self.rows, self.cols, self.chunk = name, rows, cols, chunk

    def part(self, k):
        return slice(k * self.cols // 3, (k + 1) * self.cols // 3)

    def half_part(self, k):
        return slice(k * self.cols // 6, (k + 1) * self.cols // 6)


def items_of(plan):
    return [
        Item("down", plan.frows, D, plan.cf),
        Item("up", plan.rows, FF, plan.chp),
        Item("out", plan.rows, D, plan.chp),
        Item("qkv", plan.rows, 3 * D, plan.chp),
    ]


def last_kernel(
    plan,
    up_h, vec_ref, tot_ref, ln1g, ln2g, asel_h, osel_h, usel_h, gsel_h, dp_h, dy_h, df_h, dr_h,
    sx_h, sq_h, skv_h, slse_h, sm_h, sgp_h, wq_h, wo_h, wu_h, wd_h,
    *refs,
):
    items = items_of(plan)
    n = len(items)
    outs, gin_o, vec_o, refs = refs[:n], refs[n], refs[n + 1], refs[n + 2 :]
    lhs, rhs, refs = refs[:n], refs[n : 2 * n], refs[2 * n :]
    OW, CR, refs = refs[:n], refs[n : 2 * n], refs[2 * n :]
    stages = plan.bits + 1
    RB = []
    for k in range(stages - 1):
        RB.append(refs[:n])
        refs = refs[n:]
    FS, FR, refs = refs[:n], refs[n : 2 * n], refs[2 * n :]
    (
        ST, wq, wo, wu, wd, Q, KV, LSE, XM, GP, bias, R, DKV, RDKV, ret_r, vs, vr,
        l_sem, w_sem, s_sem, chip_sem, stage_sem, vec_sem, dkv_sem, ret_sem, up_sem,
    ) = refs
    tok = plan.tok
    T = 2 * tok
    g, z, c, col, outer, parity = where_am_i()
    peer = (col * 2 + 1 - c, z)
    off = [pl.multiple_of(c * tok, tok), pl.multiple_of((3 - c) * tok, tok)]
    poff = [pl.multiple_of((1 - c) * tok, tok), pl.multiple_of((2 + c) * tok, tok)]
    DOWN, UP, OUT, QKV = range(n)
    sources = ((gsel_h, dr_h), (usel_h, df_h), (osel_h, dy_h), (asel_h, dp_h))
    DR, GF, DY, DP = [r.at[0:T] for r in rhs]
    DO = DY
    blocks = FF // D
    rows4 = items[DOWN].rows // blocks
    staged = [ST.at[0:rows4, :], ST, ST.at[:, 3 * D :], ST.at[:, : 3 * D]]

    def operand_loads(l, i):
        a, b = sources[i]
        later = pl.ds(T, rhs[i].shape[0] - T)
        return (
            pltpu.make_async_copy(a.at[l], lhs[i], l_sem.at[i, 0]),
            pltpu.make_async_copy(b.at[l, later, :], rhs[i].at[later, :], l_sem.at[i, 1]),
        )

    weight_refs = {"wd": (wd_h, wd, 0), "wu": (wu_h, wu, 1), "wo": (wo_h, wo, 2), "wq": (wq_h, wq, 3)}
    slot_refs = {
        "GP": (sgp_h, GP, 0), "M": (sm_h, XM, 1), "Q": (sq_h, Q, 2), "KV": (skv_h, KV, 3), "LSE": (slse_h, LSE, 4),
        "X": (sx_h, XM, 5),
    }

    def load(l, *names):
        out = []
        for name in names:
            if name in weight_refs:
                h, v, k = weight_refs[name]
                out.append(pltpu.make_async_copy(h.at[l], v, w_sem.at[k]))
            else:
                h, v, k = slot_refs[name]
                out.append(pltpu.make_async_copy(h.at[l], v, s_sem.at[k]))
        return out

    def start(copies):
        for cp in copies:
            cp.start()

    def wait(copies):
        for cp in copies:
            cp.wait()

    top_layer = LAYERS - 1
    up_load = pltpu.make_async_copy(up_h, R, up_sem.at[0])
    up_load.start()
    start(operand_loads(top_layer, DOWN))
    start(load(top_layer, "wd", "GP"))

    def partner(dim):
        if dim < 0:
            return (g, z + 1 - 2 * lax.rem(z, 2))
        return ((col ^ (1 << dim)) * 2 + c, z)

    def bit_of(dim):
        if dim < 0:
            return lax.rem(z, 2)
        return lax.rem(lax.div(col, 1 << dim), 2)

    dims = [-1] + list(range(plan.bits))
    block = jnp.where(z < 2, c, 3 - c)
    owner = (col * 2 + parity, block)
    mine = jnp.logical_and(parity == c, block == z)
    barrier = pltpu.get_barrier_semaphore()
    count = 0
    for dc in range(2):
        for dz in range(plan.nrow):
            if dc == 0 and dz == 0:
                continue
            target = (col * 2 + lax.rem(c + dc, 2), lax.rem(z + dz, plan.nrow))
            pl.semaphore_signal(barrier, inc=1, device_id=target, device_id_type=MESH)
            count += 1
    for dim in dims[1:]:
        pl.semaphore_signal(barrier, inc=1, device_id=partner(dim), device_id_type=MESH)
        count += 1
    pl.semaphore_wait(barrier, count)

    factor = tot_ref[0:1, 0:1]
    active = jnp.where(tot_ref[1:2, 0:1] > 0.0, jnp.ones((1, 1), F32), jnp.zeros((1, 1), F32))
    fill_bias(bias, [tot_ref[2 + k : 3 + k, 0:1] for k in range(4)], c, tok)

    def chip_copy(l, i):
        return pltpu.make_async_remote_copy(
            src_ref=staged[i], dst_ref=CR[i], send_sem=chip_sem.at[0, i], recv_sem=chip_sem.at[1, i],
            device_id=peer, device_id_type=MESH,
        )

    def base_of(i, order, k):
        base, rows = 0, items[i].rows
        for j in range(k):
            rows //= 2
            base = base + bit_of(order[j]) * rows
        return base, rows

    def stage_copy(l, i, k, part):
        item, order = items[i], plan.orders[part]
        if k == stages - 1:
            at = item.half_part(part)
            src, dst = FS[i].at[:, at], FR[i].at[l, :, at]
        else:
            base, rows = base_of(i, order, k)
            rows //= 2
            first = base + (1 - bit_of(order[k])) * rows
            at = item.part(part)
            src, dst = OW[i].at[l, pl.ds(pl.multiple_of(first, 16), rows), at], RB[k][i].at[l, :, at]
        return pltpu.make_async_remote_copy(
            src_ref=src, dst_ref=dst, send_sem=stage_sem.at[0, l, i, k, part],
            recv_sem=stage_sem.at[1, l, i, k, part], device_id=partner(order[k]), device_id_type=MESH,
        )

    def add_rows(total, base, more, rows):
        step = 32 if rows % 32 == 0 else 16

        def add(b, carry):
            at = pl.ds(pl.multiple_of(base + b * step, 16), step)
            other = more[pl.ds(pl.multiple_of(b * step, 16), step), :]
            total[at, :] = (total[at, :].astype(F32) + other.astype(F32)).astype(BF16)
            return carry

        lax.fori_loop(0, rows // step, add, 0)

    def product(l, i):
        wait(operand_loads(l, i))
        item = items[i]
        e = item.chunk
        for part in range(3):
            cols = item.part(part)
            place = plan.moved(part)
            r = nn(lhs[i][...], rhs[i][:, cols]) * factor
            for core in range(2):
                pieces = [r[core * item.rows + k * e : core * item.rows + (k + 1) * e] for k in place]
                r_core = jnp.concatenate(pieces, axis=0).astype(BF16)
                if core == 0:
                    OW[i][l, :, cols] = r_core
                elif i == DOWN:
                    for b in range(blocks):
                        at = slice(b * D + cols.start, b * D + cols.stop)
                        staged[i][:, at] = r_core[b * rows4 : (b + 1) * rows4]
                else:
                    staged[i][:, cols] = r_core
        if l > 0:
            start(operand_loads(l - 1, i))
        chip_copy(l, i).start()

    def after_chip(l, i):
        chip_copy(l, i).wait()
        if i == DOWN:
            for b in range(blocks):
                add_rows(OW[i].at[l], b * rows4, CR[i].at[:, b * D : (b + 1) * D], rows4)
        else:
            add_rows(OW[i].at[l], 0, CR[i], items[i].rows)
        for part in range(3):
            stage_copy(l, i, 0, part).start()

    def after_stage(l, i, k):
        item = items[i]
        own = outs[i].shape[1]
        for part in range(3):
            order, cols = plan.orders[part], item.part(part)
            stage_copy(l, i, k, part).wait()
            if k == stages - 1:
                outs[i][l, :, cols] += unfold(FR[i][l, :, item.half_part(part)].astype(F32))[:own]
                continue
            base, rows = base_of(i, order, k + 1)
            if k + 1 == stages - 1:
                at = pl.ds(pl.multiple_of(base, 16), rows)
                both = OW[i][l, at, cols].astype(F32) + RB[k][i][l, :, cols].astype(F32)
                rows //= 2
                first = bit_of(order[k + 1]) == 0
                outs[i][l, :, cols] = jnp.where(first, both[:rows], both[rows:])[:own]
                FS[i][:, item.half_part(part)] = fold(jnp.where(first, both[rows:], both[:rows])).astype(BF16)
            else:
                add_rows(OW[i].at[l, :, cols], base, RB[k][i].at[l, :, cols], rows)
            stage_copy(l, i, k + 1, part).start()

    def dkv_copies(part):
        at = slice(part * D, (part + 1) * D)
        return [
            pltpu.make_async_remote_copy(
                src_ref=DKV.at[pl.ds(poff[j], tok), at], dst_ref=RDKV.at[j, :, at],
                send_sem=dkv_sem.at[0, part, j], recv_sem=dkv_sem.at[1, part, j],
                device_id=peer, device_id_type=MESH,
            )
            for j in range(2)
        ]

    vec_o[...] = vec_ref[...]

    def backward(l, marks):
        def mark(name):
            for f in marks.get(name, ()):
                f()

        def reload(*names):
            if l > 0:
                start(load(l - 1, *names))

        r = R[...]
        dr = r.astype(BF16)
        DR[...] = dr
        vec_o[row_of(l, 7)] += column_sum(dr.astype(F32))
        product(l, DOWN)
        if l == top_layer:
            start(operand_loads(l, UP))
            start(load(l, "wu", "M"))
        mark("down")
        wait(load(l, "wd", "GP"))
        for j in range(FF // D):
            js = slice(j * D, (j + 1) * D)
            dg = nt(dr, wd[js, :])
            df = (dg * GP[:, js].astype(F32)).astype(BF16)
            GF[:, js] = df
            vec_o[row_of(l, 8 + j)] += column_sum(df.astype(F32))
        reload("wd", "GP")
        if l == top_layer:
            start(operand_loads(l, OUT))
            start(load(l, "wo", "Q", "KV", "LSE"))
        mark("df")
        product(l, UP)
        if l == top_layer:
            start(load(l, "wq"))
            start(operand_loads(l, QKV))
        mark("up")
        wait(load(l, "wu", "M"))
        da2 = nt(GF[...], wu[...])
        hat2, inv2 = normalised(XM[...])
        vec_o[row_of(l, 5)] += column_sum(da2 * hat2)
        vec_o[row_of(l, 6)] += column_sum(da2)
        dm = r + norm_back(da2, ln2g[l : l + 1, :], hat2, inv2)
        R[...] = dm
        dy = dm.astype(BF16)
        DY[...] = dy
        vec_o[row_of(l, 4)] += column_sum(dy.astype(F32))
        start(load(l, "X"))
        reload("wu")
        mark("dy")
        product(l, OUT)
        wait(load(l, "wo", "Q", "KV", "LSE"))
        DO[...] = nt(dy, wo[...]).astype(BF16)
        reload("wo")
        def first_half():
            start(dkv_copies(0))
            mark("half")

        attention_backward(
            KV, Q, LSE, bias, DO, DP, DKV,
            {HEADS // 2 - 1: first_half, HEADS - 1: lambda: start(dkv_copies(1))},
        )
        reload("Q", "KV", "LSE")
        mark("attention")
        wait(load(l, "X", "wq"))
        hat, inv = normalised(XM[...])
        if l == 0:
            up_again.start()
        else:
            reload("M")
        dqb = DP[:, 0:D]
        vec_o[row_of(l, 2)] += column_sum(dqb.astype(F32))
        da = nt(dqb, wq[:, 0:D])
        for part in range(2):
            for cp in dkv_copies(part):
                cp.wait()
            merge_kv(DP, DKV, RDKV, off, part)
        product(l, QKV)
        mark("qkv")
        dkv = DP[:, D : 3 * D]
        vec_o[row_of(l, 3)] += column_sum(dkv[:, D:].astype(F32))
        da = da + nt(dkv, wq[:, D : 3 * D])
        reload("wq")
        vec_o[row_of(l, 0)] += column_sum(da * hat)
        vec_o[row_of(l, 1)] += column_sum(da)
        new = R[...] + norm_back(da, ln1g[l : l + 1, :], hat, inv)
        if l == 0:
            up_again.wait()
            new = (new + (1.0 - active) * XM[...]) * factor
        R[...] = new
        mark("end")

    up_again = pltpu.make_async_copy(up_h, XM, up_sem.at[0])

    done = set()

    def chip(l, i):
        return lambda: after_chip(l, i)

    def stage(l, i, k):
        done.add((l, i, k))
        return lambda: after_stage(l, i, k)

    up_load.wait()
    R[...] = R[...] * active
    backward(1, {
        "df": [chip(1, DOWN)],
        "dy": [chip(1, UP)],
        "half": [chip(1, OUT), stage(1, DOWN, 0)],
        "end": [chip(1, QKV), stage(1, UP, 0)],
    })
    backward(0, {
        "down": [stage(1, DOWN, 1), stage(1, OUT, 0)],
        "df": [chip(0, DOWN)],
        "up": [stage(1, UP, 1), stage(1, OUT, 1)],
        "dy": [chip(0, UP), stage(1, QKV, 0)],
        "half": [chip(0, OUT), stage(1, DOWN, 2), stage(0, DOWN, 0)],
        "attention": [stage(1, UP, 2), stage(1, QKV, 1), stage(1, OUT, 2)],
        "qkv": [stage(0, UP, 0), stage(0, DOWN, 1)],
    })

    home = R.at[pl.ds(pl.multiple_of(jnp.where(z < 2, 0, tok), tok), tok), :]
    ret_local = pltpu.make_async_copy(home, ret_r, ret_sem.at[1])
    ret_remote = pltpu.make_async_remote_copy(
        src_ref=home, dst_ref=ret_r, send_sem=ret_sem.at[0], recv_sem=ret_sem.at[1],
        device_id=owner, device_id_type=MESH,
    )

    @pl.when(mine)
    def _():
        ret_local.start()

    @pl.when(jnp.logical_not(mine))
    def _():
        ret_remote.start()

    vec_targets = [peer] + [partner(dim) for dim in dims]

    def vec_copy(k):
        return pltpu.make_async_remote_copy(
            src_ref=vs, dst_ref=vr.at[k], send_sem=vec_sem.at[0, k], recv_sem=vec_sem.at[1, k],
            device_id=vec_targets[k], device_id_type=MESH,
        )

    def vec_step(k):
        vec_copy(k).wait()
        if k + 1 < len(vec_targets):
            vs[...] = vs[...] + vr[k]
            vec_copy(k + 1).start()
        else:
            vec_o[...] = vs[...] + vr[k]

    vs[...] = vec_o[...] * factor
    vec_copy(0).start()
    after_chip(0, QKV)
    vec_at = 0
    ends = [
        (0, OUT, 0), (1, QKV, 2), (0, UP, 1), (0, 0, -1), (0, DOWN, 2), (0, OUT, 1), (0, QKV, 0), (0, 0, -1),
        (0, UP, 2), (0, OUT, 2), (0, QKV, 1), (0, 0, -1), (0, QKV, 2),
    ]
    order_of_items = [(1, DOWN), (1, UP), (1, OUT), (1, QKV), (0, OUT), (0, DOWN), (0, UP), (0, QKV)]
    left = [(l, i, k) for k in range(stages) for l, i in order_of_items if (l, i, k) not in done]
    if stages == 3:
        assert sorted(left) == sorted(e for e in ends if e[2] >= 0)
    else:
        ends = left
    for l, i, k in ends:
        if k >= 0:
            after_stage(l, i, k)
        else:
            vec_step(vec_at)
            vec_at += 1
    for k in range(vec_at, len(vec_targets)):
        vec_step(k)
    ret_local.wait()

    @pl.when(jnp.logical_not(mine))
    def _():
        ret_remote.wait_send()

    gin_o[...] = ret_r[...]


def run_last(plan, upstream, vec, tot, gains, stashes, weights):
    tok = plan.tok
    T = 2 * tok
    vmem = pl.BlockSpec(memory_space=pltpu.VMEM)
    hbm = pl.BlockSpec(memory_space=pl.ANY)
    S = jax.ShapeDtypeStruct
    V = pltpu.VMEM
    DMA = pltpu.SemaphoreType.DMA
    items = items_of(plan)
    n = len(items)
    stages = plan.bits + 1
    own = {"down": plan.cf, "up": plan.ch, "out": plan.ch, "qkv": plan.ch}
    outs = [S((LAYERS, own[i.name], i.cols), F32) for i in items] + [S((tok, D), F32), S(vec.shape, F32)]
    K = stashes[0].shape[2]
    scratch = [V((2 * i.rows, K), BF16) for i in items]
    scratch += [V((K, i.cols), BF16) for i in items]
    scratch += [V((LAYERS, i.rows, i.cols), BF16) for i in items]
    scratch += [
        V((i.rows * i.cols // FF, FF) if i.name == "down" else (i.rows, i.cols), BF16) for i in items
    ]
    for k in range(stages - 1):
        scratch += [V((LAYERS, i.rows >> (k + 1), i.cols), BF16) for i in items]
    last = [i.rows >> stages for i in items]
    scratch += [V((2 * r, i.cols // 2), BF16) for r, i in zip(last, items)]
    scratch += [V((LAYERS, 2 * r, i.cols // 2), BF16) for r, i in zip(last, items)]
    nv = 2 + plan.bits
    scratch += [
        V((plan.rows, FF), BF16),
        V((D, 3 * D), BF16), V((D, D), BF16), V((D, FF), BF16), V((FF, D), BF16),
        V((T, D), BF16), V((2 * T, 2 * D), BF16), V((8, 8, T), F32), V((T, D), F32), V((T, FF), BF16),
        V((2 * T, T), F32), V((T, D), F32), V((2 * T, 2 * D), BF16), V((2, tok, 2 * D), BF16),
        V((tok, D), F32), V(vec.shape, F32), V((nv,) + vec.shape, F32),
        DMA((n, 2)), DMA((4,)), DMA((6,)), DMA((2, n)), DMA((2, LAYERS, n, stages, 3)), DMA((2, nv)), DMA((2, 2, 2)),
        DMA((2,)), DMA((1,)),
    ]
    call = pl.pallas_call(
        functools.partial(last_kernel, plan),
        out_shape=outs,
        out_specs=[vmem] * len(outs),
        in_specs=[hbm] + [vmem] * 4 + [hbm] * (len(stashes) + 4),
        scratch_shapes=scratch,
        compiler_params=pltpu.CompilerParams(
            collective_id=1, has_side_effects=True, vmem_limit_bytes=VMEM_LIMIT
        ),
        name="last",
    )
    return call(upstream, vec, tot, *gains, *stashes, *weights)


def finish_kernel(plan, vec_ref, *refs):
    big = refs[:6]
    big_o, small_o = refs[6:12], refs[12:21]
    for a, b in zip(big, big_o):
        b[...] = a[...]
    me = lax.axis_index("grp") * plan.nrow + lax.axis_index("row")
    feature = lax.broadcasted_iota(jnp.int32, (D, 128), 0)
    place = lax.broadcasted_iota(jnp.int32, (D, 128), 1)

    def picked(rows, first, n):
        one_hot = jnp.where((feature == first + place) & (place < n), 1.0, 0.0)
        return jnp.dot(rows, one_hot, preferred_element_type=F32, precision=lax.Precision.HIGHEST)

    per = D // plan.cf
    rows = picked(vec_ref[...], me * plan.ch, plan.ch)
    wide = picked(vec_ref[...], lax.rem(me, per) * plan.cf, plan.cf)
    row = lax.broadcasted_iota(jnp.int32, (LAYERS * SMALL, 128), 0)
    for l in range(LAYERS):
        for i in range(8):
            small_o[i][l : l + 1, :] = rows[row_of(l, i), : plan.ch]
        line = jnp.sum(jnp.where(row == l * SMALL + 8 + lax.div(me, per), wide, 0.0), axis=0, keepdims=True)
        small_o[8][l : l + 1, :] = line[:, : plan.cf]


def run_finish(plan, vec, big):
    vmem = pl.BlockSpec(memory_space=pltpu.VMEM)
    S = jax.ShapeDtypeStruct
    outs = [S(a.shape, a.dtype) for a in big]
    outs += [S((LAYERS, plan.ch), F32)] * 8 + [S((LAYERS, plan.cf), F32)]
    return pl.pallas_call(
        functools.partial(finish_kernel, plan),
        out_shape=outs,
        in_specs=[vmem] * 7,
        out_specs=[vmem] * 15,
        name="finish",
    )(vec, *big)


def body(
    plan,
    inputs, cotangent, pass_counts, doc_starts, token_counts,
    ln1_gain, ln1_bias, qkv_weight, query_bias, value_bias, out_weight, out_bias,
    ln2_gain, ln2_bias, up_weight, up_bias, down_weight, down_bias,
):
    vecs = (ln1_gain, ln1_bias, query_bias, value_bias, out_bias, ln2_gain, ln2_bias, up_bias, down_bias)
    weights = (qkv_weight, out_weight, up_weight, down_weight)
    hidden, upstream, vec, tot, *rest = run_main(
        plan, inputs, cotangent, (pass_counts, doc_starts, token_counts), vecs, weights
    )
    g_down, g_up, g_out, g_qkv, grad_in, vec = run_last(
        plan, upstream, vec, tot, (ln1_gain, ln2_gain), rest, weights
    )
    big = (hidden, grad_in, g_qkv, g_out, g_up, g_down)
    hidden, grad_in, g_qkv, g_out, g_up, g_down, *v = run_finish(plan, vec, big)
    return (
        hidden, grad_in, v[0], v[1], g_qkv, v[2], v[3], g_out, v[4], v[5], v[6], g_up, v[8], g_down, v[7],
    )


def solution(mesh):
    ngrp, nrow = mesh.shape["grp"], mesh.shape["row"]
    whole = P(("grp", "row"), None)
    vector = P(None, ("grp", "row"))
    matrix = P(None, ("grp", "row"), None)

    def run(*args):
        return body(Plan(ngrp, nrow, args[0].shape[0]), *args)

    return jax.shard_map(
        run,
        mesh=mesh,
        in_specs=(whole, whole, P("grp"), P("grp", None), P("grp")) + (P(),) * 13,
        out_specs=(
            whole, whole, vector, vector, matrix, vector, vector, matrix, vector, vector, vector,
            matrix, vector, matrix, vector,
        ),
        check_vma=False,
    )
```

```python
import functools

import jax
import jax.numpy as jnp
from jax import lax
from jax.experimental import pallas as pl
from jax.experimental.pallas import tpu as pltpu
from jax.sharding import PartitionSpec as P

HEADS = 12
HEAD = 64
D = 768
FF = 3072
LAYERS = 2
MAXP = 2
STEPS = LAYERS * (MAXP + 1)
SMALL = 12

EPS = 1e-05
NEG = -1000000000.0
LOG2E = 1.4426950408889634
MESH = pl.DeviceIdType.MESH
VMEM_LIMIT = 63 * 2**20
F32 = jnp.float32
BF16 = jnp.bfloat16


def nn(a, b):
    return jnp.dot(a, b, preferred_element_type=F32)


def nt(a, b):
    return lax.dot_general(a, b, (((1,), (1,)), ((), ())), preferred_element_type=F32)


def tn(a, b):
    return lax.dot_general(a, b, (((0,), (0,)), ((), ())), preferred_element_type=F32)


def normalised(x):
    mean = jnp.mean(x, axis=-1, keepdims=True)
    centred = x - mean
    spread = jnp.mean(centred * centred, axis=-1, keepdims=True)
    inv = lax.rsqrt(spread + EPS)
    return centred * inv, inv


def norm_back(grad, gain, hat, inv):
    g = grad * gain
    mean_g = jnp.mean(g, axis=-1, keepdims=True)
    mean_gh = jnp.mean(g * hat, axis=-1, keepdims=True)
    return inv * (g - mean_g - hat * mean_gh)


def column_sum(x):
    return jnp.sum(x, axis=0, keepdims=True)


def of_head(h):
    p = h // 2
    at, atv = slice(p * 128, (p + 1) * 128), slice(D + p * 128, D + (p + 1) * 128)
    low = lax.broadcasted_iota(jnp.int32, (1, 128), 1) < HEAD
    return at, atv, low if h % 2 == 0 else jnp.logical_not(low)


def attention_forward(KV, Q, LSE, bias, O, before_values):
    def scores(h):
        at, _, keep = of_head(h)
        qp = Q[:, at]
        return nt(KV[:, at], jnp.where(keep, qp, jnp.zeros_like(qp)))

    def mixed(h, raw):
        _, atv, _ = of_head(h)
        logits = raw * LOG2E + bias[...]
        top = jnp.max(logits, axis=0, keepdims=True)
        expo = jnp.exp2(logits - top)
        denom = jnp.sum(expo, axis=0, keepdims=True)
        LSE[h // 2, h % 2 : h % 2 + 1, :] = top + jnp.log2(denom)
        return tn((expo * (1.0 / denom)).astype(BF16), KV[:, atv])

    ahead = scores(0)
    before_values()
    even = None
    for h in range(HEADS):
        raw = ahead
        if h + 1 < HEADS:
            ahead = scores(h + 1)
        out = mixed(h, raw)
        if h % 2 == 0:
            even = out
        else:
            at, _, high = of_head(h)
            O[:, at] = jnp.where(high, out, even).astype(BF16)


def attention_backward(KV, Q, LSE, bias, DO, DP, DKV, between):
    low_row = lax.broadcasted_iota(jnp.int32, (128, 1), 0) < HEAD

    def parts(h):
        at, atv, keep = of_head(h)
        qp, dop = Q[:, at], DO[:, at]
        zero = jnp.zeros_like(qp)
        return KV[:, at], KV[:, atv], jnp.where(keep, qp, zero), jnp.where(keep, dop, zero)

    def products(h):
        kp, vp, qe, doe = parts(h)
        return nt(kp, qe), nt(vp, doe)

    def grads(h, raw, dpr):
        lse = LSE[h // 2, h % 2 : h % 2 + 1, :]
        pr = jnp.exp2(raw * LOG2E + bias[...] - lse)
        inner = jnp.sum(pr * dpr, axis=0, keepdims=True)
        return pr.astype(BF16), (pr * (dpr - inner)).astype(BF16)

    def finish(h0, one, two):
        at, atv, _ = of_head(h0)
        kp, _, q0, do0 = parts(h0)
        _, _, q1, do1 = parts(h0 + 1)
        dqt = jnp.where(low_row, tn(kp, one[1]), tn(kp, two[1])) * 0.125
        DP[:, at] = dqt.T.astype(BF16)
        p = h0 // 2
        DKV[:, (2 * p + 1) * 128 : (2 * p + 2) * 128] = nn(
            jnp.concatenate([one[0], two[0]], axis=1), jnp.concatenate([do0, do1], axis=0)
        ).astype(BF16)
        DKV[:, 2 * p * 128 : (2 * p + 1) * 128] = nn(
            jnp.concatenate([one[1], two[1]], axis=1), jnp.concatenate([q0, q1], axis=0)
        ).astype(BF16)

    ahead = products(0)
    even = None
    for h in range(HEADS):
        now = ahead
        if h + 1 < HEADS:
            ahead = products(h + 1)
        pair = grads(h, *now)
        if h % 2 == 0:
            even = pair
        else:
            finish(h - 1, even, pair)
        if h in between:
            between[h]()


def merge_kv(DP, DKV, RDKV, off, half):
    tok = RDKV.shape[1]
    for j in range(2):
        for p in range(half * HEADS // 4, (half + 1) * HEADS // 4):
            at = slice(2 * p * 128, (2 * p + 2) * 128)
            both = (DKV[pl.ds(off[j], tok), at].astype(F32) + RDKV[j, :, at].astype(F32)).astype(BF16)
            DP[j * tok : (j + 1) * tok, D + p * 128 : D + (p + 1) * 128] = both[:, :128]
            DP[j * tok : (j + 1) * tok, 2 * D + p * 128 : 2 * D + (p + 1) * 128] = both[:, 128:]


def row_of(layer, k):
    return slice(layer * SMALL + k, layer * SMALL + k + 1)


class Plan:
    def __init__(self, ngrp, nrow, tok):
        self.ngrp, self.nrow, self.tok = ngrp, nrow, tok
        self.ncol = ngrp // 2
        self.bits = max(self.ncol.bit_length() - 1, 0)
        self.ndev = ngrp * nrow
        self.ch = D // self.ndev
        self.chp = -(-self.ch // 8) * 8
        self.cf = FF // self.ndev
        self.rows = self.ncol * 2 * self.chp
        self.nsel = 2 * self.rows
        self.wide = FF // ngrp
        self.per = D // (2 * self.wide)
        self.frows = self.ncol * 2 * self.cf
        dims = list(range(self.bits))[::-1] + [-1]
        turns = [k * len(dims) // 3 for k in range(3)]
        self.orders = [dims[t:] + dims[:t] for t in turns]

    def piece(self, order, index):
        col, pair = 0, 0
        for place, dim in enumerate(order):
            bit = (index >> (len(order) - 1 - place)) & 1
            if dim < 0:
                pair = bit
            else:
                col |= bit << dim
        return col, pair

    def moved(self, turn):
        first = {self.piece(self.orders[0], k): k for k in range(2 * self.ncol)}
        return [first[self.piece(self.orders[turn], k)] for k in range(2 * self.ncol)]

    def fill_selectors(self, sel, c, half):
        def ones(first, rows, used):
            feature = lax.broadcasted_iota(jnp.int32, (rows, D), 1)
            place = lax.broadcasted_iota(jnp.int32, (rows, D), 0)
            return jnp.where((feature == first + place) & (place < used), 1.0, 0.0)

        for side, core in enumerate((c, 1 - c)):
            for index in range(0, 2 * self.ncol, 2):
                two = []
                for k in (index, index + 1):
                    col, pair = self.piece(self.orders[0], k)
                    two.append(ones(((col * 2 + core) * 4 + 2 * half + pair) * self.ch, self.chp, self.ch))
                row = side * self.rows + index * self.chp
                sel[0, row : row + 2 * self.chp, :] = jnp.concatenate(two, axis=0).astype(BF16)
            for j in range(self.per):
                row = side * (D // 4) + j * 2 * self.cf
                first = (j * 2 + core) * self.wide + half * 2 * self.cf
                sel[1, row : row + 2 * self.cf, :] = ones(first, 2 * self.cf, 2 * self.cf).astype(BF16)


def where_am_i():
    g = lax.axis_index("grp")
    z = lax.axis_index("row")
    c = lax.rem(g, 2)
    col = lax.div(g, 2)
    outer = jnp.logical_or(z == 0, z == 3)
    parity = jnp.where(outer, 0, 1)
    return g, z, c, col, outer, parity


def fill_bias(bias, starts, c, tok):
    T = 2 * tok
    lane = lax.broadcasted_iota(jnp.int32, (1, T), 1)
    qpos = jnp.where(lane < tok, c * tok + lane, (3 - c) * tok + lane - tok).astype(F32)
    begin = jnp.zeros((1, T), F32)
    for start in starts:
        begin = jnp.maximum(begin, jnp.where(qpos >= start, start, 0.0))
    kpos = lax.broadcasted_iota(jnp.int32, (2 * T, T), 0).astype(F32)
    bias[...] = jnp.where((kpos <= qpos) & (kpos >= begin), 0.0, NEG)


def main_kernel(
    plan,
    x_own, cot_own, pass_ref, doc_ref, tok_ref, ln1g, ln1b, qb, vb, ob, ln2g, ln2b, ub, db,
    wq_h, wo_h, wu_h, wd_h,
    hid_o, up_o, vec_o, tot_o, asel_h, osel_h, usel_h, gsel_h, dp_h, dy_h, df_h, dr_h,
    sx_h, sq_h, skv_h, slse_h, sm_h, sgp_h,
    wq, wo, wu, wd, sel, xin, cot, par_ref, par_in, tsend, trecv,
    bias, X, Q, KV, LSE, M, GP, O, GF, XN, asel, osel, usel, gsel,
    R, U, DKV, RDKV, DP, DR, DY, VAC, ret_s, ret_r,
    w_sem, in_send, in_recv, cot_send, cot_recv, par_sem, t_sem, kv_send, kv_recv,
    st_sem, ld_sem, sel_out, dkv_send, dkv_recv, bst_sem, ret_send, ret_recv,
):
    tok = plan.tok
    T = 2 * tok
    g, z, c, col, outer, parity = where_am_i()
    half = lax.div(z, 2)
    peer = (col * 2 + 1 - c, z)
    off_lo = pl.multiple_of(c * tok, tok)
    off_hi = pl.multiple_of((3 - c) * tok, tok)
    poff_lo = pl.multiple_of((1 - c) * tok, tok)
    poff_hi = pl.multiple_of((2 + c) * tok, tok)

    weight_copies = []
    for l in range(LAYERS):
        for i, (src, dst) in enumerate(((wq_h, wq), (wo_h, wo), (wu_h, wu), (wd_h, wd))):
            weight_copies.append(pltpu.make_async_copy(src.at[l], dst.at[l], w_sem.at[l, i]))
    weight_copies[0].start()
    numbers = [pass_ref[0], tok_ref[0]] + [doc_ref[0, k] for k in range(4)] + [0, 0]
    for k, number in enumerate(numbers):
        par_ref[k : k + 1, :] = jnp.full((1, 128), number, jnp.int32).astype(F32)

    barrier = pltpu.get_barrier_semaphore()
    count = 0
    for dc in range(2):
        for dz in range(plan.nrow):
            if dc == 0 and dz == 0:
                continue
            target = (col * 2 + lax.rem(c + dc, 2), lax.rem(z + dz, plan.nrow))
            pl.semaphore_signal(barrier, inc=1, device_id=target, device_id_type=MESH)
            count += 1
    others = [(col ^ (1 << b)) * 2 + c for b in range(plan.bits)]
    for other in others:
        pl.semaphore_signal(barrier, inc=1, device_id=(other, z), device_id_type=MESH)
        count += 1
    pl.semaphore_wait(barrier, count)

    block_core = jnp.where(outer, 0, 1)
    slot_in = lax.div(z, 2)
    send_list = []
    for i in range(2):
        zt = jnp.where(c == 0, 3 * i, 1 + i)
        is_self = jnp.logical_and(c == block_core, zt == z)
        send_list.append((i, zt, is_self))

    def deliver(src, dst, send, recv):
        for i, zt, is_self in send_list:

            @pl.when(is_self)
            def _():
                pltpu.make_async_copy(src, dst.at[slot_in], recv.at[slot_in]).start()

            @pl.when(jnp.logical_not(is_self))
            def _():
                pltpu.make_async_remote_copy(
                    src_ref=src, dst_ref=dst.at[slot_in], send_sem=send.at[i], recv_sem=recv.at[slot_in],
                    device_id=(col * 2 + block_core, zt), device_id_type=MESH,
                ).start()

    def deliver_sent(src, dst, send, recv):
        for i, zt, is_self in send_list:

            @pl.when(jnp.logical_not(is_self))
            def _():
                pltpu.make_async_remote_copy(
                    src_ref=src, dst_ref=dst.at[slot_in], send_sem=send.at[i], recv_sem=recv.at[slot_in],
                    device_id=(col * 2 + block_core, zt), device_id_type=MESH,
                ).wait_send()

    def deliver_wait(src, dst, recv):
        for i in range(2):
            pltpu.make_async_copy(src, dst.at[i], recv.at[i]).wait()

    deliver(x_own, xin, in_send, in_recv)

    par_copy = pltpu.make_async_remote_copy(
        src_ref=par_ref, dst_ref=par_in, send_sem=par_sem.at[0], recv_sem=par_sem.at[1],
        device_id=peer, device_id_type=MESH,
    )
    par_copy.start()
    for cp in weight_copies[1:]:
        cp.start()
    par_copy.wait()
    served = jnp.where(parity == c, par_ref[...], par_in[...])
    tcount = par_ref[1:2, :] + par_in[1:2, :]
    total = jnp.broadcast_to(tcount, (8, 128))
    for b in range(plan.bits):
        tsend[b] = total
        cp = pltpu.make_async_remote_copy(
            src_ref=tsend.at[b], dst_ref=trecv.at[b], send_sem=t_sem.at[0, b], recv_sem=t_sem.at[1, b],
            device_id=(others[b], z), device_id_type=MESH,
        )
        cp.start()
        cp.wait()
        total = total + trecv[b]
    factor = served[1:2, :] / total[0:1, :]
    tot_o[0:1, :] = factor
    tot_o[1:8, :] = jnp.concatenate([served[0:1, :], served[2:8, :]], axis=0)
    passes = served[0:1, 0:1]

    fill_bias(bias, [served[2 + k : 3 + k, 0:1] for k in range(4)], c, tok)
    VAC[...] = jnp.zeros_like(VAC)
    plan.fill_selectors(sel, c, half)

    deliver_wait(x_own, xin, in_recv)
    deliver_sent(x_own, xin, in_send, in_recv)
    XN[0:tok] = xin[0].astype(F32)
    XN[tok:T] = xin[1].astype(F32)
    deliver(cot_own, cot, cot_send, cot_recv)

    def stash_copies(s, slot, sem, back):
        pairs = ((X, sx_h), (Q, sq_h), (LSE, slse_h), (M, sm_h), (GP, sgp_h))
        out = []
        for i, (v, h) in enumerate(pairs):
            if back:
                out.append(pltpu.make_async_copy(h.at[s], v.at[slot], sem.at[slot, i]))
            else:
                out.append(pltpu.make_async_copy(v.at[slot], h.at[s], sem.at[slot, i]))
        return out

    def kv_stash(s, slot):
        return pltpu.make_async_copy(KV.at[slot], skv_h.at[s], st_sem.at[slot, 5])

    def kv_load(s, slot):
        return pltpu.make_async_copy(skv_h.at[s], KV.at[slot], ld_sem.at[slot, 5])

    def sel_copies_out(l, sect):
        at = pl.ds(pl.multiple_of(sect * T, T), T)
        return [
            pltpu.make_async_copy(asel, asel_h.at[l, :, at], sel_out.at[0]),
            pltpu.make_async_copy(osel, osel_h.at[l, :, at], sel_out.at[1]),
            pltpu.make_async_copy(usel, usel_h.at[l, :, at], sel_out.at[2]),
            pltpu.make_async_copy(gsel, gsel_h.at[l, :, at], sel_out.at[3]),
        ]

    def kv_moves(slot, offsets):
        out = []
        for part in range(2):
            out.append([])
            for i, off in enumerate(offsets):
                ref = KV.at[slot, pl.ds(off, tok), part * D : (part + 1) * D]
                out[part].append(
                    pltpu.make_async_remote_copy(
                        src_ref=ref, dst_ref=ref, send_sem=kv_send.at[slot, part, i],
                        recv_sem=kv_recv.at[slot, part, i], device_id=peer, device_id_type=MESH,
                    )
                )
        return out

    def kv_copies(slot):
        return kv_moves(slot, (off_lo, off_hi))

    def kv_arrivals(slot):
        return kv_moves(slot, (poff_lo, poff_hi))

    def forward(sect, l):
        s = sect * LAYERS + l
        slot = l

        @pl.when(sect >= 1)
        def _():
            for cp in stash_copies(s - 2, slot, st_sem, False):
                cp.wait()

        x = XN[...]
        X[slot] = x
        stash = stash_copies(s, slot, st_sem, False)
        rows_out = sel_copies_out(l, sect)
        stash[0].start()
        hat, _ = normalised(x)
        a = (hat * ln1g[l : l + 1, :] + ln1b[l : l + 1, :]).astype(BF16)

        def own_rows(values, at):
            KV[slot, pl.ds(off_lo, tok), at] = values[:tok]
            KV[slot, pl.ds(off_hi, tok), at] = values[tok:]

        sends = kv_copies(slot)
        arrivals = kv_arrivals(slot)
        own_rows(nn(a, wq[l, :, D : 2 * D]).astype(BF16), slice(0, D))
        for cp in sends[0]:
            cp.start()
        own_rows((nn(a, wq[l, :, 2 * D : 3 * D]) + vb[l : l + 1, :]).astype(BF16), slice(D, 2 * D))
        for cp in sends[1]:
            cp.start()
        q = (nn(a, wq[l, :, 0:D]) + qb[l : l + 1, :]).astype(BF16)
        Q[slot] = q * jnp.asarray(0.125, BF16)
        stash[1].start()

        def rows_of_before():
            for cp in sel_copies_out(0, 0):
                cp.wait()

        if l == 0:
            pl.when(sect >= 1)(rows_of_before)
        else:
            rows_of_before()
        asel[...] = nt(sel[0], a).astype(BF16)
        rows_out[0].start()
        for cp in arrivals[0]:
            cp.wait_recv()

        def values_here():
            for cp in arrivals[1]:
                cp.wait_recv()
            for cp in sends[0] + sends[1]:
                cp.wait_send()
            kv_stash(s, slot).start()

        attention_forward(KV.at[slot], Q.at[slot], LSE.at[slot], bias, O, values_here)
        o = O[...]
        osel[...] = nt(sel[0], o).astype(BF16)
        stash[2].start()
        rows_out[1].start()
        m = x + (nn(o, wo[l]) + ob[l : l + 1, :])
        M[slot] = m
        stash[3].start()
        hat2, _ = normalised(m)
        a2 = (hat2 * ln2g[l : l + 1, :] + ln2b[l : l + 1, :]).astype(BF16)
        usel[...] = nt(sel[0], a2).astype(BF16)
        rows_out[2].start()

        for j in range(FF // D):
            js = slice(j * D, (j + 1) * D)
            f = nn(a2, wu[l, :, js]) + ub[l : l + 1, js]
            f2 = f * f
            u = f * (0.7978845608028654 + 0.035677408136300125 * f2)
            t = jnp.tanh(u)
            h = 0.5 + 0.5 * t
            ga = f * h
            gp = h + ga * (1.0 - h) * (1.5957691216057308 + 0.21406444881780074 * f2)
            gb = ga.astype(BF16)
            GF[:, js] = gb
            GP[slot, :, js] = gp.astype(BF16)
            n = D // 4
            gs = nt(sel[1, : 2 * n], gb).astype(BF16)
            for cc in range(2):
                gsel[cc * plan.frows + j * n : cc * plan.frows + (j + 1) * n] = gs[cc * n : (cc + 1) * n]

        stash[4].start()
        rows_out[3].start()
        y = m + (nn(GF[...], wd[l]) + db[l : l + 1, :])
        if l == LAYERS - 1:
            bar = jnp.where(sect < MAXP, sect, -1).astype(F32)
            y = jnp.where(passes > bar, y, X[0])
        XN[...] = y
        kv_stash(s, slot).wait()

    def forward_section(sect, carry):
        for l in range(LAYERS):
            forward(sect, l)
        return carry

    for cp in weight_copies:
        cp.wait()
    lax.fori_loop(0, MAXP + 1, forward_section, 0)

    block = jnp.where(z < 2, c, 3 - c)
    owner = (col * 2 + parity, block)
    mine = jnp.logical_and(parity == c, block == z)

    ret_recv_wait = pltpu.make_async_copy(ret_s, ret_r, ret_recv.at[0])
    ret_remote = pltpu.make_async_remote_copy(
        src_ref=ret_s, dst_ref=ret_r, send_sem=ret_send.at[0], recv_sem=ret_recv.at[0],
        device_id=owner, device_id_type=MESH,
    )

    @pl.when(z < 2)
    def _():
        ret_s[...] = XN[0:tok]

    @pl.when(z >= 2)
    def _():
        ret_s[...] = XN[tok:T]

    @pl.when(mine)
    def _():
        ret_recv_wait.start()

    @pl.when(jnp.logical_not(mine))
    def _():
        ret_remote.start()

    deliver_wait(cot_own, cot, cot_recv)
    deliver_sent(cot_own, cot, cot_send, cot_recv)
    U[0:tok] = cot[0]
    U[tok:T] = cot[1]
    for cp in sel_copies_out(0, 0):
        cp.wait()
    for l in range(LAYERS):
        for cp in stash_copies(MAXP * LAYERS + l, l, st_sem, False):
            cp.wait()

    def back_copies(l, sect):
        at = pl.ds(pl.multiple_of(sect * T, T), T)
        return [
            pltpu.make_async_copy(DP, dp_h.at[l, at, :], bst_sem.at[0]),
            pltpu.make_async_copy(DY, dy_h.at[l, at, :], bst_sem.at[1]),
            pltpu.make_async_copy(GF, df_h.at[l, at, :], bst_sem.at[2]),
            pltpu.make_async_copy(DR, dr_h.at[l, at, :], bst_sem.at[3]),
        ]

    def dkv_copies(slot, half):
        at = slice(half * D, (half + 1) * D)
        return [
            pltpu.make_async_remote_copy(
                src_ref=DKV.at[pl.ds(off, tok), at], dst_ref=RDKV.at[slot, i, :, at],
                send_sem=dkv_send.at[slot, half, i], recv_sem=dkv_recv.at[slot, half, i],
                device_id=peer, device_id_type=MESH,
            )
            for i, off in enumerate((poff_lo, poff_hi))
        ]

    def backward(i, l):
        sect = MAXP - i
        s = sect * LAYERS + l
        slot = l

        stores = back_copies(l, sect)

        def stored(k):
            if i >= 1 or l < LAYERS - 1:
                stores[k].wait()

        if i >= 1:
            for cp in stash_copies(s, slot, ld_sem, True):
                cp.wait()
            kv_load(s, slot).wait()

        active = jnp.where(passes > (-1.0 if sect == MAXP else float(sect)), jnp.ones((1, 1), F32), jnp.zeros((1, 1), F32))
        r = U[...] * active if l == LAYERS - 1 else R[...]
        dr = r.astype(BF16)
        stored(3)
        DR[...] = dr
        stores[3].start()
        stored(2)
        VAC[row_of(l, 7)] += column_sum(dr.astype(F32))
        for j in range(FF // D):
            js = slice(j * D, (j + 1) * D)
            dg = nt(dr, wd[l, js, :])
            df = (dg * GP[slot, :, js].astype(F32)).astype(BF16)
            GF[:, js] = df
            VAC[row_of(l, 8 + j)] += column_sum(df.astype(F32))
        stores[2].start()
        da2 = nt(GF[...], wu[l])
        hat2, inv2 = normalised(M[slot])
        VAC[row_of(l, 5)] += column_sum(da2 * hat2)
        VAC[row_of(l, 6)] += column_sum(da2)
        dm = r + norm_back(da2, ln2g[l : l + 1, :], hat2, inv2)
        R[...] = dm
        dy = dm.astype(BF16)
        stored(1)
        DY[...] = dy
        stores[1].start()
        VAC[row_of(l, 4)] += column_sum(dy.astype(F32))
        O[...] = nt(dy, wo[l]).astype(BF16)

        stored(0)

        def send_half(half):
            for cp in dkv_copies(slot, half):
                cp.start()

        attention_backward(
            KV.at[slot], Q.at[slot], LSE.at[slot], bias, O, DP, DKV,
            {HEADS // 2 - 1: lambda: send_half(0), HEADS - 1: lambda: send_half(1)},
        )
        x = X[slot]
        hat, inv = normalised(x)

        if i == 0:
            for cp in stash_copies(s - 2, slot, ld_sem, True):
                cp.start()
            kv_load(s - 2, slot).start()

        dqb = DP[:, 0:D]
        VAC[row_of(l, 2)] += column_sum(dqb.astype(F32))
        da = nt(dqb, wq[l, :, 0:D])
        for half in range(2):
            for cp in dkv_copies(slot, half):
                cp.wait()
            merge_kv(DP, DKV, RDKV.at[slot], (off_lo, off_hi), half)
        stores[0].start()
        dkv = DP[:, D : 3 * D]
        VAC[row_of(l, 3)] += column_sum(dkv[:, D:].astype(F32))
        da = da + nt(dkv, wq[l, :, D : 3 * D])
        VAC[row_of(l, 0)] += column_sum(da * hat)
        VAC[row_of(l, 1)] += column_sum(da)
        new = R[...] + norm_back(da, ln1g[l : l + 1, :], hat, inv)
        if l == 0:
            U[...] = new + (1.0 - active) * U[...]
        else:
            R[...] = new

    for i in range(MAXP):
        for l in range(LAYERS - 1, -1, -1):
            backward(i, l)
    ret_recv_wait.wait()

    @pl.when(jnp.logical_not(mine))
    def _():
        ret_remote.wait_send()

    hid_o[...] = ret_r[...]
    up_o[...] = U[...]
    vec_o[...] = VAC[...]
    for cp in back_copies(0, 0):
        cp.wait()


def run_main(plan, x, cot, numbers, vecs, weights):
    tok = plan.tok
    T = 2 * tok
    L = 4 * tok
    vmem = pl.BlockSpec(memory_space=pltpu.VMEM)
    hbm = pl.BlockSpec(memory_space=pl.ANY)
    smem = pl.BlockSpec(memory_space=pltpu.SMEM)
    S = jax.ShapeDtypeStruct
    K = (MAXP + 1) * T
    outs = [
        (S((tok, D), F32), vmem),
        (S((T, D), F32), vmem),
        (S((LAYERS * SMALL, D), F32), vmem),
        (S((8, 128), F32), vmem),
        (S((LAYERS, plan.nsel, K), BF16), hbm),
        (S((LAYERS, plan.nsel, K), BF16), hbm),
        (S((LAYERS, plan.nsel, K), BF16), hbm),
        (S((LAYERS, 2 * plan.frows, K), BF16), hbm),
        (S((LAYERS, K, 3 * D), BF16), hbm),
        (S((LAYERS, K, D), BF16), hbm),
        (S((LAYERS, K, FF), BF16), hbm),
        (S((LAYERS, K, D), BF16), hbm),
        (S((STEPS, T, D), F32), hbm),
        (S((STEPS, T, D), BF16), hbm),
        (S((STEPS, L, 2 * D), BF16), hbm),
        (S((STEPS, 8, 8, T), F32), hbm),
        (S((STEPS, T, D), F32), hbm),
        (S((STEPS, T, FF), BF16), hbm),
    ]
    V = pltpu.VMEM
    DMA = pltpu.SemaphoreType.DMA
    nb = max(plan.bits, 1)
    scratch = [
        V((LAYERS, D, 3 * D), BF16), V((LAYERS, D, D), BF16), V((LAYERS, D, FF), BF16), V((LAYERS, FF, D), BF16),
        V((2, plan.nsel, D), BF16), V((2, tok, D), BF16), V((2, tok, D), F32), V((8, 128), F32), V((8, 128), F32),
        V((nb, 8, 128), F32), V((nb, 8, 128), F32),
        V((L, T), F32),
        V((2, T, D), F32), V((2, T, D), BF16), V((2, L, 2 * D), BF16), V((2, 8, 8, T), F32), V((2, T, D), F32),
        V((2, T, FF), BF16), V((T, D), BF16), V((T, FF), BF16), V((T, D), F32),
        V((plan.nsel, T), BF16), V((plan.nsel, T), BF16), V((plan.nsel, T), BF16), V((2 * plan.frows, T), BF16),
        V((T, D), F32), V((T, D), F32), V((L, 2 * D), BF16), V((2, 2, tok, 2 * D), BF16), V((T, 3 * D), BF16),
        V((T, D), BF16), V((T, D), BF16), V((LAYERS * SMALL, D), F32), V((tok, D), F32), V((tok, D), F32),
        DMA((LAYERS, 4)), DMA((2,)), DMA((2,)), DMA((2,)), DMA((2,)), DMA((2,)), DMA((2, nb)),
        DMA((2, 2, 2)), DMA((2, 2, 2)), DMA((2, 6)), DMA((2, 6)), DMA((4,)), DMA((2, 2, 2)), DMA((2, 2, 2)), DMA((4,)),
        DMA((1,)), DMA((1,)),
    ]
    call = pl.pallas_call(
        functools.partial(main_kernel, plan),
        out_shape=[o[0] for o in outs],
        out_specs=[o[1] for o in outs],
        in_specs=[vmem] * 2 + [smem] * 3 + [vmem] * 9 + [hbm] * 4,
        scratch_shapes=scratch,
        compiler_params=pltpu.CompilerParams(
            collective_id=0, has_side_effects=True, vmem_limit_bytes=VMEM_LIMIT
        ),
        name="layers",
    )
    return call(x, cot, *numbers, *vecs, *weights)


def fold(x):
    n = x.shape[1] // 2
    return jnp.concatenate([x[:, :n], x[:, n:]], axis=0)


def unfold(x):
    n = x.shape[0] // 2
    return jnp.concatenate([x[:n], x[n:]], axis=1)


class Item:
    def __init__(self, name, rows, cols, chunk):
        self.name, self.rows, self.cols, self.chunk = name, rows, cols, chunk

    def part(self, k):
        return slice(k * self.cols // 3, (k + 1) * self.cols // 3)

    def half_part(self, k):
        return slice(k * self.cols // 6, (k + 1) * self.cols // 6)


def items_of(plan):
    return [
        Item("down", plan.frows, D, plan.cf),
        Item("up", plan.rows, FF, plan.chp),
        Item("out", plan.rows, D, plan.chp),
        Item("qkv", plan.rows, 3 * D, plan.chp),
    ]


def last_kernel(
    plan,
    up_h, vec_ref, tot_ref, ln1g, ln2g, asel_h, osel_h, usel_h, gsel_h, dp_h, dy_h, df_h, dr_h,
    sx_h, sq_h, skv_h, slse_h, sm_h, sgp_h, wq_h, wo_h, wu_h, wd_h,
    *refs,
):
    items = items_of(plan)
    n = len(items)
    outs, gin_o, vec_o, refs = refs[:n], refs[n], refs[n + 1], refs[n + 2 :]
    lhs, rhs, refs = refs[:n], refs[n : 2 * n], refs[2 * n :]
    OW, CR, refs = refs[:n], refs[n : 2 * n], refs[2 * n :]
    stages = plan.bits + 1
    RB = []
    for k in range(stages - 1):
        RB.append(refs[:n])
        refs = refs[n:]
    FS, FR, refs = refs[:n], refs[n : 2 * n], refs[2 * n :]
    (
        ST, wq, wo, wu, wd, Q, KV, LSE, XM, GP, bias, R, DKV, RDKV, ret_r, vs, vr,
        l_sem, w_sem, s_sem, chip_sem, stage_sem, vec_sem, dkv_sem, ret_sem, up_sem,
    ) = refs
    tok = plan.tok
    T = 2 * tok
    g, z, c, col, outer, parity = where_am_i()
    peer = (col * 2 + 1 - c, z)
    off = [pl.multiple_of(c * tok, tok), pl.multiple_of((3 - c) * tok, tok)]
    poff = [pl.multiple_of((1 - c) * tok, tok), pl.multiple_of((2 + c) * tok, tok)]
    DOWN, UP, OUT, QKV = range(n)
    sources = ((gsel_h, dr_h), (usel_h, df_h), (osel_h, dy_h), (asel_h, dp_h))
    DR, GF, DY, DP = [r.at[0:T] for r in rhs]
    DO = DY
    blocks = FF // D
    rows4 = items[DOWN].rows // blocks
    staged = [ST.at[0:rows4, :], ST, ST.at[:, 3 * D :], ST.at[:, : 3 * D]]

    def operand_loads(l, i):
        a, b = sources[i]
        later = pl.ds(T, rhs[i].shape[0] - T)
        return (
            pltpu.make_async_copy(a.at[l], lhs[i], l_sem.at[i, 0]),
            pltpu.make_async_copy(b.at[l, later, :], rhs[i].at[later, :], l_sem.at[i, 1]),
        )

    weight_refs = {"wd": (wd_h, wd, 0), "wu": (wu_h, wu, 1), "wo": (wo_h, wo, 2), "wq": (wq_h, wq, 3)}
    slot_refs = {
        "GP": (sgp_h, GP, 0), "M": (sm_h, XM, 1), "Q": (sq_h, Q, 2), "KV": (skv_h, KV, 3), "LSE": (slse_h, LSE, 4),
        "X": (sx_h, XM, 5),
    }

    def load(l, *names):
        out = []
        for name in names:
            if name in weight_refs:
                h, v, k = weight_refs[name]
                out.append(pltpu.make_async_copy(h.at[l], v, w_sem.at[k]))
            else:
                h, v, k = slot_refs[name]
                out.append(pltpu.make_async_copy(h.at[l], v, s_sem.at[k]))
        return out

    def start(copies):
        for cp in copies:
            cp.start()

    def wait(copies):
        for cp in copies:
            cp.wait()

    top_layer = LAYERS - 1
    up_load = pltpu.make_async_copy(up_h, R, up_sem.at[0])
    up_load.start()
    start(operand_loads(top_layer, DOWN))
    start(load(top_layer, "wd", "GP"))

    def partner(dim):
        if dim < 0:
            return (g, z + 1 - 2 * lax.rem(z, 2))
        return ((col ^ (1 << dim)) * 2 + c, z)

    def bit_of(dim):
        if dim < 0:
            return lax.rem(z, 2)
        return lax.rem(lax.div(col, 1 << dim), 2)

    dims = [-1] + list(range(plan.bits))
    block = jnp.where(z < 2, c, 3 - c)
    owner = (col * 2 + parity, block)
    mine = jnp.logical_and(parity == c, block == z)
    barrier = pltpu.get_barrier_semaphore()
    count = 0
    for dc in range(2):
        for dz in range(plan.nrow):
            if dc == 0 and dz == 0:
                continue
            target = (col * 2 + lax.rem(c + dc, 2), lax.rem(z + dz, plan.nrow))
            pl.semaphore_signal(barrier, inc=1, device_id=target, device_id_type=MESH)
            count += 1
    for dim in dims[1:]:
        pl.semaphore_signal(barrier, inc=1, device_id=partner(dim), device_id_type=MESH)
        count += 1
    pl.semaphore_wait(barrier, count)

    factor = tot_ref[0:1, 0:1]
    active = jnp.where(tot_ref[1:2, 0:1] > 0.0, jnp.ones((1, 1), F32), jnp.zeros((1, 1), F32))
    fill_bias(bias, [tot_ref[2 + k : 3 + k, 0:1] for k in range(4)], c, tok)

    def chip_copy(l, i):
        return pltpu.make_async_remote_copy(
            src_ref=staged[i], dst_ref=CR[i], send_sem=chip_sem.at[0, i], recv_sem=chip_sem.at[1, i],
            device_id=peer, device_id_type=MESH,
        )

    def base_of(i, order, k):
        base, rows = 0, items[i].rows
        for j in range(k):
            rows //= 2
            base = base + bit_of(order[j]) * rows
        return base, rows

    def stage_copy(l, i, k, part):
        item, order = items[i], plan.orders[part]
        if k == stages - 1:
            at = item.half_part(part)
            src, dst = FS[i].at[:, at], FR[i].at[l, :, at]
        else:
            base, rows = base_of(i, order, k)
            rows //= 2
            first = base + (1 - bit_of(order[k])) * rows
            at = item.part(part)
            src, dst = OW[i].at[l, pl.ds(pl.multiple_of(first, 16), rows), at], RB[k][i].at[l, :, at]
        return pltpu.make_async_remote_copy(
            src_ref=src, dst_ref=dst, send_sem=stage_sem.at[0, l, i, k, part],
            recv_sem=stage_sem.at[1, l, i, k, part], device_id=partner(order[k]), device_id_type=MESH,
        )

    def add_rows(total, base, more, rows):
        step = 32 if rows % 32 == 0 else 16

        def add(b, carry):
            at = pl.ds(pl.multiple_of(base + b * step, 16), step)
            other = more[pl.ds(pl.multiple_of(b * step, 16), step), :]
            total[at, :] = (total[at, :].astype(F32) + other.astype(F32)).astype(BF16)
            return carry

        lax.fori_loop(0, rows // step, add, 0)

    def product(l, i):
        wait(operand_loads(l, i))
        item = items[i]
        e = item.chunk
        for part in range(3):
            cols = item.part(part)
            place = plan.moved(part)
            r = nn(lhs[i][...], rhs[i][:, cols]) * factor
            for core in range(2):
                pieces = [r[core * item.rows + k * e : core * item.rows + (k + 1) * e] for k in place]
                r_core = jnp.concatenate(pieces, axis=0).astype(BF16)
                if core == 0:
                    OW[i][l, :, cols] = r_core
                elif i == DOWN:
                    for b in range(blocks):
                        at = slice(b * D + cols.start, b * D + cols.stop)
                        staged[i][:, at] = r_core[b * rows4 : (b + 1) * rows4]
                else:
                    staged[i][:, cols] = r_core
        if l > 0:
            start(operand_loads(l - 1, i))
        chip_copy(l, i).start()

    def after_chip(l, i):
        chip_copy(l, i).wait()
        if i == DOWN:
            for b in range(blocks):
                add_rows(OW[i].at[l], b * rows4, CR[i].at[:, b * D : (b + 1) * D], rows4)
        else:
            add_rows(OW[i].at[l], 0, CR[i], items[i].rows)
        for part in range(3):
            stage_copy(l, i, 0, part).start()

    def after_stage(l, i, k):
        item = items[i]
        own = outs[i].shape[1]
        for part in range(3):
            order, cols = plan.orders[part], item.part(part)
            stage_copy(l, i, k, part).wait()
            if k == stages - 1:
                outs[i][l, :, cols] += unfold(FR[i][l, :, item.half_part(part)].astype(F32))[:own]
                continue
            base, rows = base_of(i, order, k + 1)
            if k + 1 == stages - 1:
                at = pl.ds(pl.multiple_of(base, 16), rows)
                both = OW[i][l, at, cols].astype(F32) + RB[k][i][l, :, cols].astype(F32)
                rows //= 2
                first = bit_of(order[k + 1]) == 0
                outs[i][l, :, cols] = jnp.where(first, both[:rows], both[rows:])[:own]
                FS[i][:, item.half_part(part)] = fold(jnp.where(first, both[rows:], both[:rows])).astype(BF16)
            else:
                add_rows(OW[i].at[l, :, cols], base, RB[k][i].at[l, :, cols], rows)
            stage_copy(l, i, k + 1, part).start()

    def dkv_copies(part):
        at = slice(part * D, (part + 1) * D)
        return [
            pltpu.make_async_remote_copy(
                src_ref=DKV.at[pl.ds(poff[j], tok), at], dst_ref=RDKV.at[j, :, at],
                send_sem=dkv_sem.at[0, part, j], recv_sem=dkv_sem.at[1, part, j],
                device_id=peer, device_id_type=MESH,
            )
            for j in range(2)
        ]

    vec_o[...] = vec_ref[...]

    def backward(l, marks):
        def mark(name):
            for f in marks.get(name, ()):
                f()

        def reload(*names):
            if l > 0:
                start(load(l - 1, *names))

        r = R[...]
        dr = r.astype(BF16)
        DR[...] = dr
        vec_o[row_of(l, 7)] += column_sum(dr.astype(F32))
        product(l, DOWN)
        if l == top_layer:
            start(operand_loads(l, UP))
            start(load(l, "wu", "M"))
        mark("down")
        wait(load(l, "wd", "GP"))
        for j in range(FF // D):
            js = slice(j * D, (j + 1) * D)
            dg = nt(dr, wd[js, :])
            df = (dg * GP[:, js].astype(F32)).astype(BF16)
            GF[:, js] = df
            vec_o[row_of(l, 8 + j)] += column_sum(df.astype(F32))
        reload("wd", "GP")
        if l == top_layer:
            start(operand_loads(l, OUT))
            start(load(l, "wo", "Q", "KV", "LSE"))
        mark("df")
        product(l, UP)
        if l == top_layer:
            start(load(l, "wq"))
            start(operand_loads(l, QKV))
        mark("up")
        wait(load(l, "wu", "M"))
        da2 = nt(GF[...], wu[...])
        hat2, inv2 = normalised(XM[...])
        vec_o[row_of(l, 5)] += column_sum(da2 * hat2)
        vec_o[row_of(l, 6)] += column_sum(da2)
        dm = r + norm_back(da2, ln2g[l : l + 1, :], hat2, inv2)
        R[...] = dm
        dy = dm.astype(BF16)
        DY[...] = dy
        vec_o[row_of(l, 4)] += column_sum(dy.astype(F32))
        start(load(l, "X"))
        reload("wu")
        mark("dy")
        product(l, OUT)
        wait(load(l, "wo", "Q", "KV", "LSE"))
        DO[...] = nt(dy, wo[...]).astype(BF16)
        reload("wo")
        def first_half():
            start(dkv_copies(0))
            mark("half")

        attention_backward(
            KV, Q, LSE, bias, DO, DP, DKV,
            {HEADS // 2 - 1: first_half, HEADS - 1: lambda: start(dkv_copies(1))},
        )
        reload("Q", "KV", "LSE")
        mark("attention")
        wait(load(l, "X", "wq"))
        hat, inv = normalised(XM[...])
        if l == 0:
            up_again.start()
        else:
            reload("M")
        dqb = DP[:, 0:D]
        vec_o[row_of(l, 2)] += column_sum(dqb.astype(F32))
        da = nt(dqb, wq[:, 0:D])
        for part in range(2):
            for cp in dkv_copies(part):
                cp.wait()
            merge_kv(DP, DKV, RDKV, off, part)
        product(l, QKV)
        mark("qkv")
        dkv = DP[:, D : 3 * D]
        vec_o[row_of(l, 3)] += column_sum(dkv[:, D:].astype(F32))
        da = da + nt(dkv, wq[:, D : 3 * D])
        reload("wq")
        vec_o[row_of(l, 0)] += column_sum(da * hat)
        vec_o[row_of(l, 1)] += column_sum(da)
        new = R[...] + norm_back(da, ln1g[l : l + 1, :], hat, inv)
        if l == 0:
            up_again.wait()
            new = (new + (1.0 - active) * XM[...]) * factor
        R[...] = new
        mark("end")

    up_again = pltpu.make_async_copy(up_h, XM, up_sem.at[0])

    done = set()

    def chip(l, i):
        return lambda: after_chip(l, i)

    def stage(l, i, k):
        done.add((l, i, k))
        return lambda: after_stage(l, i, k)

    up_load.wait()
    R[...] = R[...] * active
    backward(1, {
        "df": [chip(1, DOWN)],
        "dy": [chip(1, UP)],
        "half": [chip(1, OUT), stage(1, DOWN, 0)],
        "end": [chip(1, QKV), stage(1, UP, 0)],
    })
    backward(0, {
        "down": [stage(1, DOWN, 1), stage(1, OUT, 0)],
        "df": [chip(0, DOWN)],
        "up": [stage(1, UP, 1), stage(1, OUT, 1)],
        "dy": [chip(0, UP), stage(1, QKV, 0)],
        "half": [chip(0, OUT), stage(1, DOWN, 2), stage(0, DOWN, 0)],
        "attention": [stage(1, UP, 2), stage(1, QKV, 1), stage(1, OUT, 2)],
        "qkv": [stage(0, UP, 0), stage(0, DOWN, 1)],
    })

    home = R.at[pl.ds(pl.multiple_of(jnp.where(z < 2, 0, tok), tok), tok), :]
    ret_local = pltpu.make_async_copy(home, ret_r, ret_sem.at[1])
    ret_remote = pltpu.make_async_remote_copy(
        src_ref=home, dst_ref=ret_r, send_sem=ret_sem.at[0], recv_sem=ret_sem.at[1],
        device_id=owner, device_id_type=MESH,
    )

    @pl.when(mine)
    def _():
        ret_local.start()

    @pl.when(jnp.logical_not(mine))
    def _():
        ret_remote.start()

    vec_targets = [peer] + [partner(dim) for dim in dims]

    def vec_copy(k):
        return pltpu.make_async_remote_copy(
            src_ref=vs, dst_ref=vr.at[k], send_sem=vec_sem.at[0, k], recv_sem=vec_sem.at[1, k],
            device_id=vec_targets[k], device_id_type=MESH,
        )

    def vec_step(k):
        vec_copy(k).wait()
        if k + 1 < len(vec_targets):
            vs[...] = vs[...] + vr[k]
            vec_copy(k + 1).start()
        else:
            vec_o[...] = vs[...] + vr[k]

    vs[...] = vec_o[...] * factor
    vec_copy(0).start()
    after_chip(0, QKV)
    vec_at = 0
    ends = [
        (0, OUT, 0), (1, QKV, 2), (0, UP, 1), (0, 0, -1), (0, DOWN, 2), (0, OUT, 1), (0, QKV, 0), (0, 0, -1),
        (0, UP, 2), (0, OUT, 2), (0, QKV, 1), (0, 0, -1), (0, QKV, 2),
    ]
    order_of_items = [(1, DOWN), (1, UP), (1, OUT), (1, QKV), (0, OUT), (0, DOWN), (0, UP), (0, QKV)]
    left = [(l, i, k) for k in range(stages) for l, i in order_of_items if (l, i, k) not in done]
    if stages == 3:
        assert sorted(left) == sorted(e for e in ends if e[2] >= 0)
    else:
        ends = left
    for l, i, k in ends:
        if k >= 0:
            after_stage(l, i, k)
        else:
            vec_step(vec_at)
            vec_at += 1
    for k in range(vec_at, len(vec_targets)):
        vec_step(k)
    ret_local.wait()

    @pl.when(jnp.logical_not(mine))
    def _():
        ret_remote.wait_send()

    gin_o[...] = ret_r[...]


def run_last(plan, upstream, vec, tot, gains, stashes, weights):
    tok = plan.tok
    T = 2 * tok
    vmem = pl.BlockSpec(memory_space=pltpu.VMEM)
    hbm = pl.BlockSpec(memory_space=pl.ANY)
    S = jax.ShapeDtypeStruct
    V = pltpu.VMEM
    DMA = pltpu.SemaphoreType.DMA
    items = items_of(plan)
    n = len(items)
    stages = plan.bits + 1
    own = {"down": plan.cf, "up": plan.ch, "out": plan.ch, "qkv": plan.ch}
    outs = [S((LAYERS, own[i.name], i.cols), F32) for i in items] + [S((tok, D), F32), S(vec.shape, F32)]
    K = stashes[0].shape[2]
    scratch = [V((2 * i.rows, K), BF16) for i in items]
    scratch += [V((K, i.cols), BF16) for i in items]
    scratch += [V((LAYERS, i.rows, i.cols), BF16) for i in items]
    scratch += [
        V((i.rows * i.cols // FF, FF) if i.name == "down" else (i.rows, i.cols), BF16) for i in items
    ]
    for k in range(stages - 1):
        scratch += [V((LAYERS, i.rows >> (k + 1), i.cols), BF16) for i in items]
    last = [i.rows >> stages for i in items]
    scratch += [V((2 * r, i.cols // 2), BF16) for r, i in zip(last, items)]
    scratch += [V((LAYERS, 2 * r, i.cols // 2), BF16) for r, i in zip(last, items)]
    nv = 2 + plan.bits
    scratch += [
        V((plan.rows, FF), BF16),
        V((D, 3 * D), BF16), V((D, D), BF16), V((D, FF), BF16), V((FF, D), BF16),
        V((T, D), BF16), V((2 * T, 2 * D), BF16), V((8, 8, T), F32), V((T, D), F32), V((T, FF), BF16),
        V((2 * T, T), F32), V((T, D), F32), V((2 * T, 2 * D), BF16), V((2, tok, 2 * D), BF16),
        V((tok, D), F32), V(vec.shape, F32), V((nv,) + vec.shape, F32),
        DMA((n, 2)), DMA((4,)), DMA((6,)), DMA((2, n)), DMA((2, LAYERS, n, stages, 3)), DMA((2, nv)), DMA((2, 2, 2)),
        DMA((2,)), DMA((1,)),
    ]
    call = pl.pallas_call(
        functools.partial(last_kernel, plan),
        out_shape=outs,
        out_specs=[vmem] * len(outs),
        in_specs=[hbm] + [vmem] * 4 + [hbm] * (len(stashes) + 4),
        scratch_shapes=scratch,
        compiler_params=pltpu.CompilerParams(
            collective_id=1, has_side_effects=True, vmem_limit_bytes=VMEM_LIMIT
        ),
        name="last",
    )
    return call(upstream, vec, tot, *gains, *stashes, *weights)


def finish_kernel(plan, vec_ref, *refs):
    big = refs[:6]
    big_o, small_o = refs[6:12], refs[12:21]
    for a, b in zip(big, big_o):
        b[...] = a[...]
    me = lax.axis_index("grp") * plan.nrow + lax.axis_index("row")
    feature = lax.broadcasted_iota(jnp.int32, (D, 128), 0)
    place = lax.broadcasted_iota(jnp.int32, (D, 128), 1)

    def picked(rows, first, n):
        one_hot = jnp.where((feature == first + place) & (place < n), 1.0, 0.0)
        return jnp.dot(rows, one_hot, preferred_element_type=F32, precision=lax.Precision.HIGHEST)

    per = D // plan.cf
    rows = picked(vec_ref[...], me * plan.ch, plan.ch)
    wide = picked(vec_ref[...], lax.rem(me, per) * plan.cf, plan.cf)
    row = lax.broadcasted_iota(jnp.int32, (LAYERS * SMALL, 128), 0)
    for l in range(LAYERS):
        for i in range(8):
            small_o[i][l : l + 1, :] = rows[row_of(l, i), : plan.ch]
        line = jnp.sum(jnp.where(row == l * SMALL + 8 + lax.div(me, per), wide, 0.0), axis=0, keepdims=True)
        small_o[8][l : l + 1, :] = line[:, : plan.cf]


def run_finish(plan, vec, big):
    vmem = pl.BlockSpec(memory_space=pltpu.VMEM)
    S = jax.ShapeDtypeStruct
    outs = [S(a.shape, a.dtype) for a in big]
    outs += [S((LAYERS, plan.ch), F32)] * 8 + [S((LAYERS, plan.cf), F32)]
    return pl.pallas_call(
        functools.partial(finish_kernel, plan),
        out_shape=outs,
        in_specs=[vmem] * 7,
        out_specs=[vmem] * 15,
        name="finish",
    )(vec, *big)


def body(
    plan,
    inputs, cotangent, pass_counts, doc_starts, token_counts,
    ln1_gain, ln1_bias, qkv_weight, query_bias, value_bias, out_weight, out_bias,
    ln2_gain, ln2_bias, up_weight, up_bias, down_weight, down_bias,
):
    vecs = (ln1_gain, ln1_bias, query_bias, value_bias, out_bias, ln2_gain, ln2_bias, up_bias, down_bias)
    weights = (qkv_weight, out_weight, up_weight, down_weight)
    hidden, upstream, vec, tot, *rest = run_main(
        plan, inputs, cotangent, (pass_counts, doc_starts, token_counts), vecs, weights
    )
    g_down, g_up, g_out, g_qkv, grad_in, vec = run_last(
        plan, upstream, vec, tot, (ln1_gain, ln2_gain), rest, weights
    )
    big = (hidden, grad_in, g_qkv, g_out, g_up, g_down)
    hidden, grad_in, g_qkv, g_out, g_up, g_down, *v = run_finish(plan, vec, big)
    return (
        hidden, grad_in, v[0], v[1], g_qkv, v[2], v[3], g_out, v[4], v[5], v[6], g_up, v[8], g_down, v[7],
    )


def solution(mesh):
    ngrp, nrow = mesh.shape["grp"], mesh.shape["row"]
    whole = P(("grp", "row"), None)
    vector = P(None, ("grp", "row"))
    matrix = P(None, ("grp", "row"), None)

    def run(*args):
        return body(Plan(ngrp, nrow, args[0].shape[0]), *args)

    return jax.shard_map(
        run,
        mesh=mesh,
        in_specs=(whole, whole, P("grp"), P("grp", None), P("grp")) + (P(),) * 13,
        out_specs=(
            whole, whole, vector, vector, matrix, vector, vector, matrix, vector, vector, vector,
            matrix, vector, matrix, vector,
        ),
        check_vma=False,
    )
```
